32 devices in a mesh: dp: 4 (over y, core), band: 8 (over z, x).
Axes of the slice: x: 2, y: 2, z: 4, core: 2. Of those that a mesh axis runs over, the one named last changes fastest.
Arguments:
- tokens: bfloat16 [8, 1024, 1152], P('dp', 'band'), may hold values from -6 to 6
- cotangent: bfloat16 [8, 1024, 1152], P('dp', 'band'), may hold values from -6 to 6
- lengths: int32 [8, 4], P('dp'), may hold values from 0 to 1024, as said below
- cond_index: int32 [8, 4], P('dp'), may hold values from 0 to 999
- cond_table: bfloat16 [1000, 1152], replicated, may hold values from -6 to 6
- w_mod: bfloat16 [1152, 6912], P(None, 'dp'), may hold values from -0.1875 to 0.1875
- b_mod: float32 [6912], replicated, may hold values from -3 to 3
- w_qkv: bfloat16 [1152, 3456], P(None, 'dp'), may hold values from -0.1875 to 0.1875
- b_query: float32 [1152], replicated, may hold values from -2 to 2
- b_value: float32 [1152], replicated, may hold values from -2 to 2
- w_out: bfloat16 [1152, 1152], P(None, 'dp'), may hold values from -1.5 to 1.5
- b_out: float32 [1152], replicated, may hold values from -2 to 2
- w_up: bfloat16 [1152, 4608], P(None, 'dp'), may hold values from -0.1875 to 0.1875
- b_up: float32 [4608], replicated, may hold values from -2 to 2
- w_down: bfloat16 [4608, 1152], P(None, 'dp'), may hold values from -0.09375 to 0.09375
- b_down: float32 [1152], replicated, may hold values from -2 to 2
Outputs:
- output: bfloat16 [8, 1024, 1152], P('dp', 'band')
- grad_tokens: bfloat16 [8, 1024, 1152], P('dp', 'band')
- grad_cond_table: float32 [1000, 1152], replicated
- grad_w_mod: float32 [1152, 6912], P('dp', 'band')
- grad_w_qkv: float32 [1152, 3456], P('dp', 'band')
- grad_w_out: float32 [1152, 1152], P('dp', 'band')
- grad_w_up: float32 [1152, 4608], P('dp', 'band')
- grad_w_down: float32 [4608, 1152], P('band', 'dp')
- grad_b_mod: float32 [6912], replicated
- grad_b_query: float32 [1152], replicated
- grad_b_value: float32 [1152], replicated
- grad_b_out: float32 [1152], replicated
- grad_b_up: float32 [4608], replicated
- grad_b_down: float32 [1152], replicated
The draws below stay inside these ranges and needn't reach their ends.
Inputs may be any that keep to these rules, and one draw needn't show every extreme that they name: In each row the nonzero lengths come first and add up to 1024; each is 256, 1024 or 1024. In every aligned block of 2 rows one row, drawn from the seed, is a single image of 1024 patches; the other rows hold images of 256 and 1024 patches only.
All inputs are finite; a program needn't handle non-finite values.
Results may differ from the reference program's by a relative error of at most 0.023.
Values may be sent and summed in bfloat16 or wider, within the bound.
No kernel may reach another device: no remote copies, remote signals or barrier semaphores. Data moves between devices by JAX's collectives and lax.ppermute only.
A program may use at most 384 MiB of HBM per device.

```python
import math
import jax
import jax.numpy as jnp
from jax import lax

D = 1152
H = 16
HD = 72
FF = 4608
CLASSES = 1000
ROWS_DEV = 2
SMALL_IMG = 256
BIG_IMG = 1024
ROWS = 8
LEN = 1024
IMGS = 4


def draw_lengths(key, part):
    key = jax.random.fold_in(key, 11)
    coin_key, pick_key = jax.random.split(key)
    groups = LEN // BIG_IMG
    per_group = BIG_IMG // SMALL_IMG
    coin_flips = jax.random.randint(coin_key, (ROWS, groups), 0, 2)
    slot_ids = jnp.arange(IMGS)
    leading = slot_ids % per_group == 0
    big_slots = jnp.repeat(coin_flips, per_group, axis=1)
    raw_lengths = jnp.where(big_slots == 1, jnp.where(leading[None, :], BIG_IMG, 0), SMALL_IMG)
    sort_order = jnp.argsort((raw_lengths == 0).astype(jnp.int32), axis=1, stable=True)
    packed = jnp.take_along_axis(raw_lengths, sort_order, axis=1)
    chosen = jax.random.randint(pick_key, (ROWS // ROWS_DEV,), 0, ROWS_DEV)
    within = jnp.arange(ROWS) % ROWS_DEV
    full_rows = within == jnp.repeat(chosen, ROWS_DEV)
    whole_row = jnp.where(slot_ids == 0, LEN, 0)
    return jnp.where(full_rows[:, None], whole_row[None, :], packed).astype(jnp.int32)


def plant(values, own_key, low, high):
    longest = values.shape.index(max(values.shape))
    spots = []
    for shift in (0, 1):
        where = [jax.random.randint(jax.random.fold_in(own_key, axis), (), 0, length) for axis, length in enumerate(values.shape)]
        where[longest] = (where[longest] + shift) % values.shape[longest]
        spots.append(tuple(where))
    return values.at[spots[0]].set(low).at[spots[1]].set(high)


def shard_levels(stream_key, dims, pieces, smallest, high):
    gain, own = 1.0, jax.random.fold_in(stream_key, 6)
    for axis_at, blocks in pieces:
        steps = jnp.exp(jax.random.uniform(jax.random.fold_in(own, axis_at), (blocks,), jnp.float32, smallest / len(pieces), high / len(pieces)))
        gain = gain * jnp.repeat(steps, dims[axis_at] // blocks).reshape([-1 if axis == axis_at else 1 for axis in range(len(dims))])
    return gain


def bell_draw(rng, dims, width, most, cuts=(), kind=jnp.bfloat16):
    array = width * jax.random.normal(rng, dims, jnp.float32)
    if cuts:
        array = array * shard_levels(rng, dims, cuts, -0.22, 0.18)
    return jnp.clip(array, -most, most).astype(kind)


def setup_inputs(seed: int = 0) -> dict:
    key_list = jax.random.split(jax.random.key(seed), 17)
    tokens = bell_draw(key_list[0], (ROWS, LEN, D), 1.0, 6.0, ((0, 4), (1, 8)))
    cotangent = bell_draw(key_list[1], (ROWS, LEN, D), 1.0, 6.0, ((0, 4), (1, 8)))
    lengths = draw_lengths(jax.random.fold_in(key_list[16], 71), 0)
    cond_index = plant(jax.random.randint(key_list[3], (ROWS, IMGS), 0, CLASSES), jax.random.fold_in(key_list[3], 1), 0, CLASSES - 1).astype(jnp.int32)
    cond_table = bell_draw(key_list[4], (CLASSES, D), 1.0, 6.0)
    w_mod = bell_draw(key_list[5], (D, 6 * D), D ** -0.5, 0.1875, ((1, 4),))
    b_mod = bell_draw(key_list[6], (6 * D,), 0.5, 3.0, (), jnp.float32)
    w_qkv = bell_draw(key_list[7], (D, 3 * D), D ** -0.5, 0.1875, ((1, 4),))
    b_query = bell_draw(key_list[8], (D,), 0.3, 2.0, (), jnp.float32)
    b_value = bell_draw(key_list[9], (D,), 0.3, 2.0, (), jnp.float32)
    w_out = bell_draw(key_list[10], (D, D), (max(1, D // 64)) ** -0.5, 1.5, ((1, 4),))
    b_out = bell_draw(key_list[11], (D,), 0.3, 2.0, (), jnp.float32)
    w_up = bell_draw(key_list[12], (D, FF), D ** -0.5, 0.1875, ((1, 4),))
    b_up = bell_draw(key_list[13], (FF,), 0.3, 2.0, (), jnp.float32)
    w_down = bell_draw(key_list[14], (FF, D), FF ** -0.5, 0.09375, ((1, 4),))
    b_down = bell_draw(key_list[15], (D,), 0.3, 2.0, (), jnp.float32)
    return {"tokens": tokens, "cotangent": cotangent, "lengths": lengths, "cond_index": cond_index, "cond_table": cond_table, "w_mod": w_mod, "b_mod": b_mod, "w_qkv": w_qkv, "b_query": b_query, "b_value": b_value, "w_out": w_out, "b_out": b_out, "w_up": w_up, "b_up": b_up, "w_down": w_down, "b_down": b_down}


@jax.custom_vjp
def low(v):
    return lax.optimization_barrier(v.astype(jnp.bfloat16)).astype(jnp.float32)

@jax.custom_vjp
def low_back(v):
    return v

def low_keep(v):
    return (low(v), None)

def low_pass(kept, grad):
    return (grad,)

def back_keep(v):
    return (v, None)

def back_low(kept, grad):
    return (low(grad),)
low.defvjp(low_keep, low_pass)
low_back.defvjp(back_keep, back_low)
EPSILON = 1e-06
HIGHEST = lax.Precision.HIGHEST
NEGATIVE = -1e+30
GELU_COEF = 0.7978845608028654

def gelu_tanh(inputs):
    return 0.5 * inputs * (1.0 + jnp.tanh(GELU_COEF * (inputs + 0.044715 * inputs * inputs * inputs)))

def layer_norm(inputs):
    average = lax.optimization_barrier(jnp.mean(inputs, axis=-1, keepdims=True))
    centred = inputs - average
    spread = lax.optimization_barrier(jnp.mean(centred * centred, axis=-1, keepdims=True))
    return centred * lax.rsqrt(spread + EPSILON)

def dense(left, right):
    return jnp.dot(left, right, precision=HIGHEST, preferred_element_type=jnp.float32)

def attention(queries, keys_all, values_all, segments):
    length = queries.shape[0]
    block_len = min(512, length)
    factor = 1.0 / math.sqrt(HD)
    keys_head = keys_all.reshape(length, H, HD)
    values_head = values_all.reshape(length, H, HD)
    query_blocks = queries.reshape(length // block_len, block_len, H, HD)
    segment_blocks = segments.reshape(length // block_len, block_len)

    def one_block(entries):
        query_block, segment_block = entries
        scores = jnp.einsum('qhd,khd->hqk', query_block, keys_head, precision=HIGHEST) * factor
        scores = low_back(scores)
        allowed = segment_block[:, None] == segments[None, :]
        scores = jnp.where(allowed[None], scores, NEGATIVE)
        row_top = lax.optimization_barrier(jnp.max(scores, axis=-1, keepdims=True))
        exponent = jnp.exp(scores - row_top)
        attn_probs = exponent / lax.optimization_barrier(jnp.sum(exponent, axis=-1, keepdims=True))
        return jnp.einsum('hqk,khd->qhd', low(attn_probs), values_head, precision=HIGHEST)
    blocks = lax.map(jax.checkpoint(one_block), (query_blocks, segment_blocks))
    return blocks.reshape(length, H * HD)

def row_forward(row_tokens, segments, indices, params):
    cond_table, w_mod, b_mod, w_qkv, b_query, b_value, w_out, b_out, w_up, b_up, w_down, b_down = params
    model_width = row_tokens.shape[-1]
    condition = cond_table[indices]
    silu_cond = low(jax.nn.silu(condition))
    modulation = dense(silu_cond, w_mod) + b_mod
    per_token = modulation[segments]
    shift_a, scale_a, gate_a, shift_b, scale_b, gate_b = jnp.split(per_token, 6, axis=-1)
    hidden_a = low(layer_norm(row_tokens) * (1.0 + scale_a) + shift_a)
    projected = dense(hidden_a, w_qkv)
    queries = low_back(low(projected[:, :model_width] + b_query))
    keys_all = low_back(low(projected[:, model_width:2 * model_width]))
    values_all = low_back(low(projected[:, 2 * model_width:] + b_value))
    attended = low_back(low(attention(queries, keys_all, values_all, segments)))
    branch = low_back(dense(attended, w_out) + b_out)
    middle = row_tokens + gate_a * branch
    hidden_b = low(layer_norm(middle) * (1.0 + scale_b) + shift_b)
    pre_act = low_back(dense(hidden_b, w_up) + b_up)
    activated = low_back(low(gelu_tanh(pre_act)))
    mlp_out = low_back(dense(activated, w_down) + b_down)
    return middle + gate_b * mlp_out

def reference(tokens, cotangent, lengths, cond_index, cond_table, w_mod, b_mod, w_qkv, b_query, b_value, w_out, b_out, w_up, b_up, w_down, b_down):
    image_ends = jnp.cumsum(lengths, axis=-1)
    places = jnp.arange(LEN, dtype=jnp.int32)
    segments = lax.optimization_barrier(jnp.sum((image_ends[:, None, :] <= places[None, :, None]).astype(jnp.int32), axis=-1)).astype(jnp.int32)
    params = tuple((member.astype(jnp.float32) for member in (cond_table, w_mod, b_mod, w_qkv, b_query, b_value, w_out, b_out, w_up, b_up, w_down, b_down)))
    inputs = tokens.astype(jnp.float32)

    def forward(row_inputs, weights):

        def one_row(entries):
            return row_forward(entries[0], entries[1], entries[2], weights)
        return lax.map(one_row, (row_inputs, segments, cond_index))
    outputs, pullback = jax.vjp(forward, inputs, params)
    grad_inputs, grad_params = pullback(cotangent.astype(jnp.float32))
    return (outputs.astype(jnp.bfloat16), grad_inputs.astype(jnp.bfloat16), grad_params[0], grad_params[1], grad_params[3], grad_params[6], grad_params[8], grad_params[10], grad_params[2], grad_params[4], grad_params[5], grad_params[7], grad_params[9], grad_params[11])
```

```python
import functools
import math

import jax
import jax.numpy as jnp
from jax import lax
from jax.experimental import pallas as pl
from jax.experimental.pallas import tpu as pltpu
from jax.sharding import PartitionSpec as P

H = 16
HD = 72

EPSILON = 1e-06
HIGHEST = lax.Precision.HIGHEST
NEGATIVE = -1e30
GELU_COEF = 0.7978845608028654
FACTOR = 1.0 / math.sqrt(HD)
VMEM_LIMIT = 56 * 1024 * 1024
F32 = jnp.float32
BF16 = jnp.bfloat16


def dot(left, right, left_dim=1, right_dim=0):
    return lax.dot_general(
        left, right, (((left_dim,), (right_dim,)), ((), ())), preferred_element_type=F32
    )


def reverse_bits(value, count):
    result = 0
    while count > 1:
        result = result * 2 + value % 2
        value, count = value // 2, count // 2
    return result


def bits_up(count):
    return [1 << place for place in range(count.bit_length() - 1)]


def xor_perm(count, mask):
    return [(place, place ^ mask) for place in range(count)]


def pick(stack, place, axis=0):
    return lax.dynamic_index_in_dim(stack, place, axis, keepdims=False)


def xor_order(count):
    order = [0]
    for bit in reversed(bits_up(count)):
        order = order + [place ^ bit for place in order]
    return order


def gather_xor(part, axis, count):
    held = part[None]
    for bit in reversed(bits_up(count)):
        held = jnp.concatenate([held, lax.ppermute(held, axis, xor_perm(count, bit))], axis=0)
    return held


def gather_all(part, axis, count):
    held = gather_xor(part, axis, count)
    order = xor_order(count)
    me = lax.axis_index(axis)
    place_of = jnp.array([order.index(place) for place in range(count)], jnp.int32)
    return jnp.stack([pick(held, place_of[me ^ place]) for place in range(count)])


def scatter_sum_xor(parts, axis, count):
    held = parts
    for bit in bits_up(count):
        half = held.shape[0] // 2
        came = lax.ppermute(held[half:].astype(BF16), axis, xor_perm(count, bit))
        held = held[:half].astype(F32) + came.astype(F32)
    return held[0]


def exchange_columns(parts, axis, count):
    me = lax.axis_index(axis)
    got = [pick(parts, me)]
    for mask in range(1, count):
        got.append(lax.ppermute(pick(parts, me ^ mask), axis, xor_perm(count, mask)))
    return got


def attend_kernel(heads, piece, segq_ref, q_ref, k_ref, v_ref, segk_ref, out_ref, prob_ref):
    step = pl.program_id(0)
    pieces = q_ref.shape[0] // piece
    parts = []
    seg_key = segk_ref[...]
    for head in range(heads):
        lanes = slice(head * HD, (head + 1) * HD)
        scores = dot(q_ref[:, lanes], k_ref[:, lanes], 1, 1) * FACTOR
        masked = [
            jnp.where(
                seg_key == segq_ref[step * pieces + at],
                scores[at * piece : (at + 1) * piece],
                NEGATIVE,
            )
            for at in range(pieces)
        ]
        scores = jnp.concatenate(masked, axis=0)
        top = jnp.max(scores, axis=-1, keepdims=True)
        exponent = jnp.exp(scores - top)
        total = jnp.sum(exponent, axis=-1, keepdims=True)
        prob = (exponent * (1.0 / total)).astype(BF16)
        prob_ref[head] = prob
        parts.append(dot(prob, v_ref[:, lanes]))
    out_ref[...] = jnp.concatenate(parts, axis=-1).astype(BF16)


def attend(queries, keys, values, seg_query, seg_key, piece):
    count, width = queries.shape
    keys_len = keys.shape[0]
    heads = width // HD
    rows = min(256, count)
    whole = lambda step, seg: (0, 0)
    chunk = lambda step, seg: (step, 0)
    return pl.pallas_call(
        functools.partial(attend_kernel, heads, piece),
        grid_spec=pltpu.PrefetchScalarGridSpec(
            num_scalar_prefetch=1,
            grid=(count // rows,),
            in_specs=[
                pl.BlockSpec((rows, width), chunk),
                pl.BlockSpec((keys_len, width), whole),
                pl.BlockSpec((keys_len, width), whole),
                pl.BlockSpec((1, keys_len), whole),
            ],
            out_specs=[
                pl.BlockSpec((rows, width), chunk),
                pl.BlockSpec((heads, rows, keys_len), lambda step, seg: (0, step, 0)),
            ],
        ),
        out_shape=[
            jax.ShapeDtypeStruct((count, width), BF16),
            jax.ShapeDtypeStruct((heads, count, keys_len), BF16),
        ],
        compiler_params=pltpu.CompilerParams(vmem_limit_bytes=VMEM_LIMIT),
        cost_estimate=pl.CostEstimate(
            flops=8 * count * keys_len * heads * 128,
            bytes_accessed=2 * heads * count * keys_len,
            transcendentals=heads * count * keys_len,
        ),
        name="attend",
    )(seg_query, queries, keys, values, seg_key[None])


def attend_back_kernel(
    heads, q_ref, k_ref, v_ref, out_ref, grad_ref, prob_ref, dq_ref, dk_ref, dv_ref, dk_sum, dv_sum
):
    step = pl.program_id(0)

    @pl.when(step == 0)
    def _():
        dk_sum[...] = jnp.zeros_like(dk_sum)
        dv_sum[...] = jnp.zeros_like(dv_sum)

    dq_parts, dk_parts, dv_parts = [], [], []
    for head in range(heads):
        lanes = slice(head * HD, (head + 1) * HD)
        grad = grad_ref[:, lanes]
        prob = prob_ref[head]
        grad_prob = dot(grad, v_ref[:, lanes], 1, 1)
        delta = jnp.sum(grad.astype(F32) * out_ref[:, lanes].astype(F32), axis=-1, keepdims=True)
        grad_score = (prob.astype(F32) * (grad_prob - delta)).astype(BF16)
        dq_parts.append(dot(grad_score, k_ref[:, lanes]))
        dk_parts.append(dot(grad_score, q_ref[:, lanes], 0, 0))
        dv_parts.append(dot(prob, grad, 0, 0))
    dq_ref[...] = (jnp.concatenate(dq_parts, axis=-1) * FACTOR).astype(BF16)
    dk_sum[...] += jnp.concatenate(dk_parts, axis=-1)
    dv_sum[...] += jnp.concatenate(dv_parts, axis=-1)

    @pl.when(step == pl.num_programs(0) - 1)
    def _():
        dk_ref[...] = (dk_sum[...] * FACTOR).astype(BF16)
        dv_ref[...] = dv_sum[...].astype(BF16)


def attend_back(queries, keys, values, attended, grad, prob):
    count, width = queries.shape
    keys_len = keys.shape[0]
    heads = width // HD
    rows = min(256, count)
    whole = lambda step: (0, 0)
    chunk = lambda step: (step, 0)
    return pl.pallas_call(
        functools.partial(attend_back_kernel, heads),
        grid=(count // rows,),
        in_specs=[
            pl.BlockSpec((rows, width), chunk),
            pl.BlockSpec((keys_len, width), whole),
            pl.BlockSpec((keys_len, width), whole),
            pl.BlockSpec((rows, width), chunk),
            pl.BlockSpec((rows, width), chunk),
            pl.BlockSpec((heads, rows, keys_len), lambda step: (0, step, 0)),
        ],
        out_specs=[
            pl.BlockSpec((rows, width), chunk),
            pl.BlockSpec((keys_len, width), whole),
            pl.BlockSpec((keys_len, width), whole),
        ],
        out_shape=[
            jax.ShapeDtypeStruct((count, width), BF16),
            jax.ShapeDtypeStruct((keys_len, width), BF16),
            jax.ShapeDtypeStruct((keys_len, width), BF16),
        ],
        scratch_shapes=[
            pltpu.VMEM((keys_len, width), F32),
            pltpu.VMEM((keys_len, width), F32),
        ],
        compiler_params=pltpu.CompilerParams(vmem_limit_bytes=VMEM_LIMIT),
        cost_estimate=pl.CostEstimate(
            flops=16 * count * keys_len * heads * 128,
            bytes_accessed=2 * heads * count * keys_len,
            transcendentals=0,
        ),
        name="attend_back",
    )(queries, keys, values, attended, grad, prob)


def gelu_pair(inputs):
    square = inputs * inputs
    tanh = jnp.tanh(GELU_COEF * (inputs + 0.044715 * inputs * square))
    value = 0.5 * inputs * (1.0 + tanh)
    slope = 0.5 * (1.0 + tanh) + 0.5 * inputs * (1.0 - tanh * tanh) * (
        GELU_COEF * (1.0 + 3.0 * 0.044715 * square)
    )
    return value, slope


def layer_norm(inputs):
    average = jnp.mean(inputs, axis=-1, keepdims=True)
    centred = inputs - average
    spread = jnp.mean(centred * centred, axis=-1, keepdims=True)
    scale = lax.rsqrt(spread + EPSILON)
    return centred * scale, scale


def layer_norm_back(grad, norm, scale):
    first = jnp.mean(grad, axis=-1, keepdims=True)
    second = jnp.mean(grad * norm, axis=-1, keepdims=True)
    return (grad - first - norm * second) * scale


def shards(
    tokens,
    cotangent,
    lengths,
    cond_index,
    cond_table,
    w_mod,
    b_mod,
    w_qkv,
    b_query,
    b_value,
    w_out,
    b_out,
    w_up,
    b_up,
    w_down,
    b_down,
):
    rows_dev, piece, width = tokens.shape
    dp, band = lax.axis_size("dp"), lax.axis_size("band")
    me, group = lax.axis_index("dp"), lax.axis_index("band")
    images = lengths.shape[1]
    rows = rows_dev * dp
    spans = band // rows
    assert band % rows == 0 and dp & (dp - 1) == 0 and band & (band - 1) == 0
    across = band // dp
    head_width = width // dp
    mod_width = w_mod.shape[1]
    hidden_width = w_up.shape[1]

    def turned(index, count=dp):
        table = jnp.array([reverse_bits(place, count) for place in range(count)], jnp.int32)
        return table[index]

    def target(d, b, turn):
        slot = (b % rows) // dp
        local = (slot + turn) % rows_dev
        home = reverse_bits(b % dp, dp)
        to_group = (rows_dev * reverse_bits(d, dp) + local) * spans + b // rows
        return home * band + to_group

    outward = [
        [(d * band + b, target(d, b, turn)) for d in range(dp) for b in range(band)]
        for turn in range(rows_dev)
    ]
    inward = [[(there, here) for here, there in pairs] for pairs in outward]
    both = ("dp", "band")
    my_slot = (group % rows) // dp

    def to_groups(local):
        return jnp.stack(
            [
                lax.ppermute(pick(local, (my_slot + turn) % rows_dev), both, outward[turn])
                for turn in range(rows_dev)
            ]
        )

    def from_groups(held):
        came = jnp.stack(
            [lax.ppermute(held[turn], both, inward[turn]) for turn in range(rows_dev)]
        )
        return jnp.stack([pick(came, (local - my_slot) % rows_dev) for local in range(rows_dev)])

    group_row = group // spans
    my_local = group_row % rows_dev
    my_row = rows_dev * turned(group_row // rows_dev) + my_local

    def piece_of(turn, mask):
        slot = (my_local - turn) % rows_dev
        return (group % spans) * rows + slot * dp + turned(me ^ mask)

    order = xor_order(dp)

    tokens_own = to_groups(tokens)
    facts = gather_all(jnp.concatenate([lengths, cond_index], axis=1), "dp", dp)
    facts = facts.reshape(rows, 2 * images)
    lengths_all, index_all = facts[:, :images], facts[:, images:]
    image_ends = jnp.cumsum(pick(lengths_all, my_row))
    class_hot = (
        index_all.reshape(-1)[:, None] == jnp.arange(cond_table.shape[0], dtype=jnp.int32)
    ).astype(BF16)
    condition = dot(class_hot, cond_table)
    silu_all = jax.nn.silu(condition).astype(BF16)
    silu_own = pick(silu_all.reshape(rows, images, width), my_row)
    b_mod_own = lax.dynamic_slice_in_dim(b_mod, me * mod_width, mod_width)
    mod_part = dot(silu_own, w_mod) + b_mod_own
    modulation = jnp.transpose(gather_all(mod_part, "dp", dp), (1, 0, 2)).reshape(images, 6, width)

    def segment(piece_index):
        return jnp.sum((image_ends <= piece_index * piece).astype(jnp.int32))

    seg_own = [segment(piece_of(turn, 0)) for turn in range(rows_dev)]
    seg_all = jnp.stack(
        [segment(piece_of(turn, mask)) for mask in order for turn in range(rows_dev)]
    )
    mod_own = jnp.stack([pick(modulation, seg) for seg in seg_own])[:, :, None, :]
    shift_a, scale_a, gate_a, shift_b, scale_b, gate_b = [mod_own[:, at] for at in range(6)]

    blocks = 3
    kind_of = [
        [next(kind for kind in range(3) if (kind * dp + d) % 3 == slot) for slot in range(3)]
        for d in range(dp)
    ]
    w_slots = [
        lax.ppermute(
            w_qkv[:, slot * head_width : (slot + 1) * head_width],
            "dp",
            [(d, (blocks * d + slot) % dp) for d in range(dp)],
        )
        for slot in range(3)
    ]
    kinds = jnp.array(kind_of, jnp.int32)[me]
    slot_of = [(kind * dp + me) % 3 for kind in range(3)]
    bias_kinds = jnp.stack(
        [
            lax.dynamic_slice_in_dim(b_query, me * head_width, head_width),
            jnp.zeros((head_width,), F32),
            lax.dynamic_slice_in_dim(b_value, me * head_width, head_width),
        ]
    )

    def to_rows(matrix):
        depth = matrix.shape[0] // dp
        parted = matrix.reshape(dp, depth, matrix.shape[1])
        got = jnp.stack(exchange_columns(parted, "dp", dp))
        return jnp.concatenate([pick(got, me ^ place) for place in range(dp)], axis=1)

    inputs = tokens_own.astype(F32)
    norm_a, spread_a = layer_norm(inputs)
    hidden_a = (norm_a * (1.0 + scale_a) + shift_a).astype(BF16)
    hidden_a_all = gather_xor(hidden_a, "dp", dp).reshape(-1, width)
    count = hidden_a_all.shape[0]
    projected = jnp.stack(
        [
            (dot(hidden_a_all, w_slots[slot]) + pick(bias_kinds, kinds[slot])).astype(BF16)
            for slot in range(3)
        ]
    )
    queries, keys, values = [pick(projected, slot_of[kind]) for kind in range(3)]
    keys_row, values_row, seg_row = keys, values, seg_all
    if spans > 1:
        mates = [[at * spans + span for span in range(spans)] for at in range(rows)]
        keys_row, values_row, seg_row = [
            lax.all_gather(member, "band", axis=0, tiled=True, axis_index_groups=mates)
            for member in (keys, values, seg_all)
        ]
    attended, prob_low = attend(
        queries, keys_row, values_row, seg_all, jnp.repeat(seg_row, piece), piece
    )
    w_out_rows = to_rows(w_out)

    def split_own(partial):
        return partial.reshape((dp, rows_dev, piece, width))

    branch = scatter_sum_xor(split_own(dot(attended, w_out_rows)), "dp", dp) + b_out
    middle = inputs + gate_a * branch
    norm_b, spread_b = layer_norm(middle)
    hidden_b = (norm_b * (1.0 + scale_b) + shift_b).astype(BF16)
    hidden_b_all = gather_xor(hidden_b, "dp", dp).reshape(count, width)

    grad_output = to_groups(cotangent).astype(F32)
    grad_mlp = (gate_b * grad_output).astype(BF16)
    grad_mlp_all = gather_xor(grad_mlp, "dp", dp).reshape(count, width)
    w_down_rows = to_rows(w_down)
    b_up_own = lax.dynamic_slice_in_dim(b_up, me * hidden_width, hidden_width)
    pre_act = dot(hidden_b_all, w_up) + b_up_own
    value, slope = gelu_pair(pre_act)
    activated = value.astype(BF16)
    slope = slope.astype(BF16)
    grad_act = dot(grad_mlp_all, w_down_rows, 1, 1)
    grad_pre = (grad_act * slope.astype(F32)).astype(BF16)
    grad_hidden_b = scatter_sum_xor(split_own(dot(grad_pre, w_up, 1, 1)), "dp", dp)
    mlp_out = scatter_sum_xor(split_own(dot(activated, w_down_rows)), "dp", dp) + b_down
    output = from_groups((middle + gate_b * mlp_out).astype(BF16))
    grad_w_down = dot(activated, grad_mlp_all, 0, 0).astype(BF16)
    grad_w_up = dot(hidden_b_all, grad_pre, 0, 0).astype(BF16)

    grad_middle = grad_output + layer_norm_back(grad_hidden_b * (1.0 + scale_b), norm_b, spread_b)
    grad_branch = (gate_a * grad_middle).astype(BF16)
    grad_branch_all = gather_xor(grad_branch, "dp", dp).reshape(count, width)
    grad_attended = dot(grad_branch_all, w_out_rows, 1, 1).astype(BF16)
    grad_w_out = dot(attended, grad_branch_all, 0, 0).astype(BF16)
    grad_q, grad_k, grad_v = attend_back(
        queries, keys_row, values_row, attended, grad_attended, prob_low
    )
    if spans > 1:
        grad_k, grad_v = [
            lax.psum_scatter(
                member, "band", scatter_dimension=0, tiled=True, axis_index_groups=mates
            )
            for member in (grad_k, grad_v)
        ]
    grad_kinds = jnp.stack([grad_q, grad_k, grad_v])
    grad_slots = [pick(grad_kinds, kinds[slot]) for slot in range(3)]
    grad_hidden_a = sum(dot(grad_slots[slot], w_slots[slot], 1, 1) for slot in range(3))
    grad_hidden_a = scatter_sum_xor(split_own(grad_hidden_a), "dp", dp)
    grad_w_slots = [dot(hidden_a_all, grad_slots[slot], 0, 0).astype(BF16) for slot in range(3)]
    grad_tokens = grad_middle + layer_norm_back(grad_hidden_a * (1.0 + scale_a), norm_a, spread_a)
    grad_tokens = from_groups(grad_tokens.astype(BF16))

    deep, unit = width // dp, width // band

    def sum_groups(pieces):
        return lax.psum_scatter(pieces, "band", scatter_dimension=0, tiled=False)

    swap = [
        (d * band + across * to + at, to * band + across * d + at)
        for d in range(dp)
        for to in range(dp)
        for at in range(across)
    ]
    up_pieces = grad_w_up.reshape(dp, deep, across, hidden_width // across)
    up_pieces = jnp.transpose(up_pieces, (0, 2, 1, 3)).reshape(band, deep, -1)
    down_pieces = grad_w_down.reshape(across, hidden_width // across, dp, deep)
    down_pieces = jnp.transpose(down_pieces, (2, 0, 1, 3)).reshape(band, -1, deep)
    final_up = lax.ppermute(sum_groups(up_pieces), both, swap).astype(F32)
    final_down = lax.ppermute(sum_groups(down_pieces), both, swap).astype(F32)
    out_pieces = jnp.transpose(grad_w_out.reshape(deep, band, unit), (1, 0, 2))
    final_out = sum_groups(out_pieces).astype(F32)
    slot_table = {}
    for turn in range(3):
        for at in range(across):
            slots = {
                slot
                for d in range(dp)
                for slot in range(3)
                if (band * kind_of[d][slot] + across * d + at) % 3 == turn
            }
            assert len(slots) == 1
            slot_table[turn, at] = slots.pop()
    unit_slots = [
        jnp.transpose(member.reshape(dp, deep, across, unit), (0, 2, 1, 3))
        for member in grad_w_slots
    ]
    qkv_pieces = jnp.stack(
        [
            jnp.stack([unit_slots[slot_table[turn, at]][:, at] for at in range(across)], axis=1)
            for turn in range(3)
        ],
        axis=2,
    ).reshape(band, 3, deep, unit)
    qkv_sum = sum_groups(qkv_pieces)
    final_qkv = []
    for turn in range(3):
        pairs = []
        for d in range(dp):
            for at in range(across):
                kind = kind_of[d][slot_table[turn, at]]
                place = band * kind + across * d + at
                assert place % 3 == turn
                for to in range(dp):
                    pairs.append((d * band + across * to + at, to * band + place // 3))
        final_qkv.append(lax.ppermute(qkv_sum[turn], both, pairs))
    final_qkv = jnp.concatenate(final_qkv, axis=1).astype(F32)

    grad_mod_pieces = jnp.stack(
        [
            jnp.sum(member, axis=1)
            for member in (
                grad_hidden_a,
                grad_hidden_a * norm_a,
                grad_middle * branch,
                grad_hidden_b,
                grad_hidden_b * norm_b,
                grad_output * mlp_out,
            )
        ],
        axis=1,
    )
    grad_mod = sum(
        jnp.where(
            (jnp.arange(images, dtype=jnp.int32) == seg_own[turn])[:, None, None],
            grad_mod_pieces[turn][None],
            0.0,
        )
        for turn in range(rows_dev)
    )
    grad_mod = jnp.transpose(grad_mod.reshape(images, dp, mod_width), (1, 0, 2))
    grad_mod_own = sum(exchange_columns(grad_mod, "dp", dp))
    high = grad_mod_own.astype(BF16)
    low = (grad_mod_own - high.astype(F32)).astype(BF16)
    grad_silu = dot(jnp.concatenate([high, low], axis=0), w_mod, 1, 1)
    grad_silu = grad_silu[:images] + grad_silu[images:]
    bias_own = jnp.concatenate(
        [
            jnp.sum(grad_mlp.astype(F32), axis=(0, 1)),
            jnp.sum(grad_branch.astype(F32), axis=(0, 1)),
            jnp.sum(grad_pre.astype(F32), axis=0),
            jnp.sum(grad_q.astype(F32), axis=0),
            jnp.sum(grad_v.astype(F32), axis=0),
        ]
    )
    packed = jnp.concatenate([grad_mod_own.reshape(-1), grad_silu.reshape(-1), bias_own])
    packed = gather_all(packed, "band", band)
    mod_size, silu_size = images * mod_width, images * width
    grad_mod_groups = packed[:, :mod_size].reshape(band * images, mod_width)
    grad_silu_groups = packed[:, mod_size : mod_size + silu_size].reshape(rows, spans, -1).sum(1)
    bias_sum = jnp.sum(packed[:, mod_size + silu_size :], axis=0)
    final_pack = jnp.concatenate(
        [grad_silu_groups.reshape(-1), jnp.sum(grad_mod_groups, axis=0), bias_sum]
    )
    final_pack = gather_all(final_pack, "dp", dp)
    silu_end = rows * silu_size
    grad_silu_rows = jnp.sum(final_pack[:, :silu_end], axis=0).reshape(rows, images, width)
    final_b_mod = final_pack[:, silu_end : silu_end + mod_width].reshape(-1)
    rest = final_pack[:, silu_end + mod_width :]
    final_b_down = jnp.sum(rest[:, :width], axis=0)
    final_b_out = jnp.sum(rest[:, width : 2 * width], axis=0)
    at = 2 * width
    final_b_up = rest[:, at : at + hidden_width].reshape(-1)
    at = at + hidden_width
    final_b_query = rest[:, at : at + head_width].reshape(-1)
    final_b_value = rest[:, at + head_width :].reshape(-1)
    row_order = jnp.array(
        [
            rows_dev * reverse_bits(place // rows_dev, dp) + place % rows_dev
            for place in range(rows)
        ],
        jnp.int32,
    )
    sigmoid = jax.nn.sigmoid(condition)
    silu_slope = sigmoid * (1.0 + condition * (1.0 - sigmoid))
    grad_condition = grad_silu_rows * silu_slope.reshape(rows, images, width)[row_order]
    index_groups = index_all[row_order].reshape(-1)
    table_hot = (
        jnp.arange(cond_table.shape[0], dtype=jnp.int32)[:, None] == index_groups[None]
    ).astype(F32)
    final_table = jnp.dot(table_hot, grad_condition.reshape(-1, width), precision=HIGHEST)
    mod_share = lax.dynamic_slice_in_dim(
        grad_mod_groups, (group % across) * (mod_width // across), mod_width // across, axis=1
    )
    mod_share = lax.ppermute(mod_share, both, swap)
    silu_groups = jnp.repeat(silu_all.reshape(rows, images, width)[row_order], spans, axis=0)
    silu_share = lax.dynamic_slice_in_dim(
        silu_groups.reshape(band * images, width), me * deep, deep, axis=1
    )
    final_mod = lax.dot_general(
        silu_share.astype(F32),
        mod_share,
        (((0,), (0,)), ((), ())),
        precision=HIGHEST,
        preferred_element_type=F32,
    )
    return (
        output,
        grad_tokens,
        final_table,
        final_mod,
        final_qkv,
        final_out,
        final_up,
        final_down,
        final_b_mod,
        final_b_query,
        final_b_value,
        final_b_out,
        final_b_up,
        final_b_down,
    )


def solution(mesh):
    rows = P("dp", "band", None)
    split = P(None, "dp")
    spread = P("dp", "band")
    return jax.shard_map(
        shards,
        mesh=mesh,
        in_specs=(
            rows,
            rows,
            P("dp", None),
            P("dp", None),
            P(),
            split,
            P(),
            split,
            P(),
            P(),
            split,
            P(),
            split,
            P(),
            split,
            P(),
        ),
        out_specs=(
            rows,
            rows,
            P(),
            spread,
            spread,
            spread,
            spread,
            P("band", "dp"),
            P(),
            P(),
            P(),
            P(),
            P(),
            P(),
        ),
        check_vma=False,
    )
```

```python
import functools
import math

import jax
import jax.numpy as jnp
from jax import lax
from jax.experimental import pallas as pl
from jax.experimental.pallas import tpu as pltpu
from jax.sharding import PartitionSpec as P

H = 16
HD = 72

EPSILON = 1e-06
HIGHEST = lax.Precision.HIGHEST
NEGATIVE = -1e30
GELU_COEF = 0.7978845608028654
FACTOR = 1.0 / math.sqrt(HD)
LOG2E = math.log2(math.e)
VMEM_LIMIT = 56 * 1024 * 1024
F32 = jnp.float32
BF16 = jnp.bfloat16


def dot(left, right, left_dim=1, right_dim=0):
    return lax.dot_general(
        left, right, (((left_dim,), (right_dim,)), ((), ())), preferred_element_type=F32
    )


def log2(count):
    assert count & (count - 1) == 0
    return count.bit_length() - 1


def reverse_bits(value, count):
    width = log2(count)
    return sum(((value >> at) & 1) << (width - 1 - at) for at in range(width)) if width else 0


def bits_up(count):
    return [1 << place for place in range(log2(count))]


def xor_perm(count, mask):
    return [(place, place ^ mask) for place in range(count)]


def pick(stack, place, axis=0):
    return lax.dynamic_index_in_dim(
        stack, place, axis, keepdims=False, allow_negative_indices=False
    )


def cut(array, start, size, axis=0):
    return lax.dynamic_slice_in_dim(array, start, size, axis, allow_negative_indices=False)


def xor_shuffle(array, mask):
    return jnp.stack([pick(array, mask ^ place) for place in range(array.shape[0])])


def after(array, *others):
    return lax.optimization_barrier((array, *others))[0]


def gather_parts(part, axis, count, *waits):
    held = part[None]
    for bit in reversed(bits_up(count)):
        came = lax.ppermute(held, axis, xor_perm(count, bit))
        if waits and held.shape[0] == 1:
            came = after(came, *waits)
        held = jnp.concatenate([held, came])
    return held


def gather_stack(part, axis, count):
    held = part[None]
    for bit in bits_up(count):
        held = jnp.concatenate([held, lax.ppermute(held, axis, xor_perm(count, bit))], axis=0)
    return held


def gather_all(part, axis, count):
    return xor_shuffle(gather_stack(part, axis, count), lax.axis_index(axis))


def mask_order(count):
    order = [0]
    for bit in reversed(bits_up(count)):
        order = order + [place ^ bit for place in order]
    return order


def scatter_sum(near, far, axis, count, *waits):
    held = near.astype(F32) + lax.ppermute(far, axis, xor_perm(count, 1)).astype(F32)
    for bit in bits_up(count)[1:]:
        half = held.shape[0] // 2
        came = lax.ppermute(held[half:].astype(BF16), axis, xor_perm(count, bit))
        if waits and half == 1:
            came = after(came, *waits)
        held = held[:half] + came.astype(F32)
    return held[0]


def exchange(parts, axis, count):
    held = xor_shuffle(parts, lax.axis_index(axis))[None]
    for bit in reversed(bits_up(count)):
        half = held.shape[1] // 2
        came = lax.ppermute(held[:, half:], axis, xor_perm(count, bit))
        held = jnp.concatenate([held[:, :half], came])
    return held[:, 0]


def scatter_blocks(parts, axis, count):
    me = lax.axis_index(axis)
    held = parts
    for at, bit in enumerate(bits_up(count)):
        held = held.reshape((-1, 2) + parts.shape[1:])
        mine = (me >> at) & 1
        held = pick(held, mine, 1) + lax.ppermute(
            pick(held, mine ^ 1, 1), axis, xor_perm(count, bit)
        )
    return held[0]


def attend_kernel(piece, facts_ref, q_ref, k_ref, v_ref, out_ref, prob_ref):
    step = pl.program_id(1)
    keys_len, lanes = k_ref.shape[-1], q_ref.shape[-1]
    pieces_key, pieces_query = keys_len // piece, lanes // piece
    values = v_ref[0]

    def finish(scores):
        top = jnp.max(scores, axis=0, keepdims=True)
        exponent = jnp.exp2(scores * (FACTOR * LOG2E) - top * (FACTOR * LOG2E))
        total = jnp.sum(exponent, axis=0, keepdims=True)
        prob = (exponent * (1.0 / total)).astype(BF16)
        prob_ref[0] = prob
        out_ref[0] = dot(values, prob).astype(BF16)

    scores = dot(k_ref[0], q_ref[0], 0, 0)

    @pl.when(facts_ref[0] == 1)
    def _():
        finish(scores)

    @pl.when(facts_ref[0] != 1)
    def _():
        seg_key = jnp.concatenate(
            [jnp.full((piece, 1), facts_ref[1 + at], jnp.int32) for at in range(pieces_key)], axis=0
        )
        base = 1 + pieces_key + step * pieces_query
        seg_query = jnp.concatenate(
            [jnp.full((1, piece), facts_ref[base + at], jnp.int32) for at in range(pieces_query)],
            axis=1,
        )
        finish(jnp.where(seg_key == seg_query, scores, NEGATIVE))


def attend(queries, keys, values, facts, piece):
    heads, depth, count = queries.shape
    keys_len = keys.shape[2]
    lanes = min(512, count)
    chunk = lambda head, step, facts: (head, 0, step)
    whole = lambda head, step, facts: (head, 0, 0)
    return pl.pallas_call(
        functools.partial(attend_kernel, piece),
        grid_spec=pltpu.PrefetchScalarGridSpec(
            num_scalar_prefetch=1,
            grid=(heads, count // lanes),
            in_specs=[
                pl.BlockSpec((1, depth, lanes), chunk),
                pl.BlockSpec((1, depth, keys_len), whole),
                pl.BlockSpec((1, depth, keys_len), whole),
            ],
            out_specs=[
                pl.BlockSpec((1, depth, lanes), chunk),
                pl.BlockSpec((1, keys_len, lanes), chunk),
            ],
        ),
        out_shape=[
            jax.ShapeDtypeStruct((heads, depth, count), BF16),
            jax.ShapeDtypeStruct((heads, keys_len, count), BF16),
        ],
        compiler_params=pltpu.CompilerParams(vmem_limit_bytes=VMEM_LIMIT),
        cost_estimate=pl.CostEstimate(
            flops=4 * count * keys_len * heads * 128,
            bytes_accessed=2 * heads * count * keys_len,
            transcendentals=heads * count * keys_len,
        ),
        name="attend",
    )(facts, queries, keys, values)


def attend_back_kernel(
    q_ref, k_ref, v_ref, out_ref, grad_ref, prob_ref, dq_ref, dk_ref, dv_ref, dk_sum, dv_sum
):
    step = pl.program_id(1)
    grad = grad_ref[0]
    prob = prob_ref[0]
    delta = jnp.sum(grad.astype(F32) * out_ref[0].astype(F32), axis=0, keepdims=True)
    grad_prob = dot(v_ref[0], grad, 0, 0)
    grad_score = (prob.astype(F32) * (grad_prob - delta)).astype(BF16)
    dq_ref[0] = (dot(k_ref[0], grad_score) * FACTOR).astype(BF16)
    dk_part = dot(grad_score, q_ref[0], 1, 1)
    dv_part = dot(prob, grad, 1, 1)

    @pl.when(step == 0)
    def _():
        dk_sum[...] = dk_part
        dv_sum[...] = dv_part

    @pl.when(step != 0)
    def _():
        dk_sum[...] += dk_part
        dv_sum[...] += dv_part

    @pl.when(step == pl.num_programs(1) - 1)
    def _():
        dk_ref[0] = jnp.transpose(dk_sum[...] * FACTOR).astype(BF16)
        dv_ref[0] = jnp.transpose(dv_sum[...]).astype(BF16)


def attend_back(queries, keys, values, attended, grad, prob):
    heads, depth, count = queries.shape
    keys_len = keys.shape[2]
    lanes = min(512, count)
    chunk = lambda head, step: (head, 0, step)
    whole = lambda head, step: (head, 0, 0)
    return pl.pallas_call(
        attend_back_kernel,
        grid=(heads, count // lanes),
        in_specs=[
            pl.BlockSpec((1, depth, lanes), chunk),
            pl.BlockSpec((1, depth, keys_len), whole),
            pl.BlockSpec((1, depth, keys_len), whole),
            pl.BlockSpec((1, depth, lanes), chunk),
            pl.BlockSpec((1, depth, lanes), chunk),
            pl.BlockSpec((1, keys_len, lanes), chunk),
        ],
        out_specs=[
            pl.BlockSpec((1, depth, lanes), chunk),
            pl.BlockSpec((1, depth, keys_len), whole),
            pl.BlockSpec((1, depth, keys_len), whole),
        ],
        out_shape=[
            jax.ShapeDtypeStruct((heads, depth, count), BF16),
            jax.ShapeDtypeStruct((heads, depth, keys_len), BF16),
            jax.ShapeDtypeStruct((heads, depth, keys_len), BF16),
        ],
        scratch_shapes=[pltpu.VMEM((keys_len, depth), F32), pltpu.VMEM((keys_len, depth), F32)],
        compiler_params=pltpu.CompilerParams(vmem_limit_bytes=VMEM_LIMIT),
        cost_estimate=pl.CostEstimate(
            flops=4 * count * keys_len * heads * 128,
            bytes_accessed=2 * heads * count * keys_len,
            transcendentals=0,
        ),
        name="attend_back",
    )(queries, keys, values, attended, grad, prob)


def gelu_pair(inputs):
    square = inputs * inputs
    tanh = jnp.tanh(GELU_COEF * (inputs + 0.044715 * inputs * square))
    value = 0.5 * inputs * (1.0 + tanh)
    slope = 0.5 * (1.0 + tanh) + 0.5 * inputs * (1.0 - tanh * tanh) * (
        GELU_COEF * (1.0 + 3.0 * 0.044715 * square)
    )
    return value, slope


def layer_norm(inputs):
    average = jnp.mean(inputs, axis=-1, keepdims=True)
    centred = inputs - average
    spread = jnp.mean(centred * centred, axis=-1, keepdims=True)
    scale = lax.rsqrt(spread + EPSILON)
    return centred * scale, scale


def layer_norm_back(grad, norm, scale):
    first = jnp.mean(grad, axis=-1, keepdims=True)
    second = jnp.mean(grad * norm, axis=-1, keepdims=True)
    return (grad - first - norm * second) * scale


def shards(
    tokens,
    cotangent,
    lengths,
    cond_index,
    cond_table,
    w_mod,
    b_mod,
    w_qkv,
    b_query,
    b_value,
    w_out,
    b_out,
    w_up,
    b_up,
    w_down,
    b_down,
):
    rows_dev, piece, width = tokens.shape
    dp, band = lax.axis_size("dp"), lax.axis_size("band")
    me, group = lax.axis_index("dp"), lax.axis_index("band")
    images = lengths.shape[1]
    rows = rows_dev * dp
    spans = band // rows
    assert band % rows == 0
    across = band // dp
    unit = width // band
    heads = H // dp
    head_width = width // dp
    mod_width = w_mod.shape[1]
    hidden_width = w_up.shape[1]
    both = ("dp", "band")
    me_turned = reverse_bits(me, dp)

    def target(d, b, turn):
        local = ((b >> log2(dp)) & (rows_dev - 1)) ^ turn
        to_group = (rows_dev * reverse_bits(d, dp) + local) * spans + b // rows
        return reverse_bits(b % dp, dp) * band + to_group

    outward = [
        [(d * band + b, target(d, b, turn)) for d in range(dp) for b in range(band)]
        for turn in range(rows_dev)
    ]
    inward = [[(there, here) for here, there in pairs] for pairs in outward]
    my_slot = (group >> log2(dp)) & (rows_dev - 1)

    def to_groups(local):
        return jnp.stack(
            [
                lax.ppermute(pick(local, my_slot ^ turn), both, outward[turn])
                for turn in range(rows_dev)
            ]
        )

    def from_groups(held):
        came = jnp.stack(
            [lax.ppermute(held[turn], both, inward[turn]) for turn in range(rows_dev)]
        )
        return xor_shuffle(came, my_slot)

    group_row = group >> log2(spans)
    my_local = group_row & (rows_dev - 1)
    order = mask_order(dp)
    places = jnp.arange(dp, dtype=jnp.int32)[:, None]
    turns = jnp.arange(rows_dev, dtype=jnp.int32)[None]
    piece_first = piece * (
        (group & (spans - 1)) * rows + ((my_local ^ turns) * dp) + (me_turned ^ places)
    )

    facts = jnp.concatenate([lengths, cond_index], axis=1)
    facts_own = lax.ppermute(pick(facts, my_slot), both, outward[0])
    tokens_own = to_groups(tokens)
    slot_to = [[(3 * d + slot) % dp for d in range(dp)] for slot in range(3)]
    w_qkv, w_out, w_down = lax.optimization_barrier((w_qkv, w_out, w_down, facts_own))[:3]
    w_slots = [w_qkv.T[slot * head_width : (slot + 1) * head_width] for slot in range(3)]
    stay = [[d == to for d, to in enumerate(target)] for target in slot_to]
    if all(first != last for first, last in zip(stay[0], stay[2], strict=True)):
        keeps_first = functools.reduce(
            jnp.logical_or, [me == d for d in range(dp) if stay[0][d]]
        )
        came = lax.ppermute(
            jnp.where(keeps_first, w_slots[2], w_slots[0]),
            "dp",
            [(d, slot_to[2 if stay[0][d] else 0][d]) for d in range(dp)],
        )
        w_slots = [
            jnp.where(keeps_first, w_slots[0], came),
            lax.ppermute(w_slots[1], "dp", list(enumerate(slot_to[1]))),
            jnp.where(keeps_first, came, w_slots[2]),
        ]
    else:
        w_slots = [
            lax.ppermute(w_slots[slot], "dp", list(enumerate(slot_to[slot]))) for slot in range(3)
        ]
    out_blocks = jnp.stack(jnp.split(w_out.T, dp, axis=1))
    out_parts = exchange(out_blocks, "dp", dp)
    out_parts = jnp.stack([out_parts[reverse_bits(mask, dp)] for mask in range(dp)])
    down_blocks = jnp.stack(jnp.split(after(w_down, tokens_own).T, dp, axis=1))
    w_down_parts = [
        pick(down_blocks, me),
        lax.ppermute(pick(down_blocks, me ^ 1), "dp", xor_perm(dp, 1)),
    ]
    far = dp - 2
    if band % far == 0 and (head_width * far) % band == 0:
        each = band // far
        share = head_width // each
        mask = 2 + lax.div(group, each)
        first = lax.rem(group, each) * share
        sent = lax.dynamic_slice(
            w_down.T,
            (first, (me ^ mask) * hidden_width),
            (share, hidden_width),
            allow_negative_indices=False,
        )
        sent = lax.ppermute(
            sent,
            both,
            [
                (d * band + b, (d ^ (2 + b // each)) * band + b)
                for d in range(dp)
                for b in range(band)
            ],
        )
        w_down_far = lax.all_gather(sent, "band", axis=0, tiled=True)
    else:
        w_down_far = jnp.concatenate(
            [
                lax.ppermute(pick(down_blocks, me ^ mask), "dp", xor_perm(dp, mask))
                for mask in range(2, dp)
            ]
        )

    image_ends = jnp.cumsum(facts_own[:images])
    classes = jnp.arange(cond_table.shape[0], dtype=jnp.int32)

    def conditions(index):
        return dot((index[:, None] == classes[None]).astype(BF16), cond_table)

    silu_own = jax.nn.silu(conditions(facts_own[images:])).astype(BF16)
    mod_part = dot(silu_own, w_mod) + cut(b_mod, me * mod_width, mod_width)
    modulation = gather_stack(mod_part, "dp", dp)
    tokens_all = gather_parts(tokens_own, "dp", dp)
    modulation = xor_shuffle(after(modulation, tokens_all), me)
    tokens_all = tokens_all.reshape((-1,) + tokens_own.shape[1:])
    seg_all = jnp.sum(
        (image_ends[None, None] <= piece_first[..., None]).astype(jnp.int32), axis=-1
    ).reshape(-1)
    image_ids = jnp.arange(images, dtype=jnp.int32)
    hot_all = seg_all[:, None] == image_ids[None]
    mod_all = jnp.sum(jnp.where(hot_all[:, None, :, None], modulation[None], 0.0), axis=2)
    mod_all = mod_all.reshape(-1, 1, 6, width)
    shift_a_all, scale_a_all, gate_b_all = [mod_all[:, :, at] for at in (0, 1, 5)]
    scale_a, gate_a, shift_b, scale_b, gate_b = [
        mod_all[:rows_dev, :, at] for at in (1, 2, 3, 4, 5)
    ]
    own_hot = hot_all[:rows_dev]

    def gather_tokens(own, *waits):
        return gather_parts(own, "dp", dp, *waits).reshape((-1,) + own.shape[1:])

    slot_of = [lax.rem(me + kind * (dp % 3), 3) for kind in range(3)]
    w_heads = jnp.concatenate(
        [
            jnp.where(
                slot_of[kind] == 0,
                w_slots[0],
                jnp.where(slot_of[kind] == 1, w_slots[1], w_slots[2]),
            )
            for kind in range(3)
        ]
    )
    bias_heads = jnp.concatenate(
        [
            cut(b_query, me * head_width, head_width),
            jnp.zeros((head_width,), F32),
            cut(b_value, me * head_width, head_width),
        ]
    )
    norm_all = layer_norm(tokens_all.astype(F32))[0]
    hidden_a_all = (norm_all * (1.0 + scale_a_all) + shift_a_all).astype(BF16).reshape(-1, width)
    norm_low = norm_all.astype(BF16).reshape(-1, width)
    cotangent_own = to_groups(after(cotangent, tokens_own))
    count = hidden_a_all.shape[0]
    half = count // 2
    projected = (dot(w_heads, hidden_a_all, 1, 1) + bias_heads[:, None]).astype(BF16)
    projected = projected.reshape(3, heads, HD, count)
    queries, keys, values = after(projected, cotangent_own)
    cotangent_all = gather_tokens(cotangent_own)
    seg_row = seg_all
    if spans > 1:
        mates = [[at * spans + span for span in range(spans)] for at in range(rows)]
        keys, values, seg_row = [
            lax.all_gather(
                member, "band", axis=member.ndim - 1, tiled=True, axis_index_groups=mates
            )
            for member in (keys, values, seg_row)
        ]
    one_image = jnp.all(seg_row == seg_row[0]).astype(jnp.int32)
    attend_facts = jnp.concatenate([one_image[None], seg_row, seg_all])
    attended, prob_low = attend(queries, keys, values, attend_facts, piece)
    attended = after(attended, cotangent_all).reshape(head_width, count)
    w_out_rows = jnp.concatenate(list(xor_shuffle(out_parts, me)))

    def split_own(partial):
        return partial.astype(BF16).reshape(dp // 2, rows_dev, piece, width)

    def products(product, left):
        return split_own(product(left(half, count))), split_own(product(left(0, half)))

    far_half, near_half = products(
        lambda part: dot(part, w_out_rows, 0, 1), lambda low, high: attended[:, low:high]
    )
    branch = scatter_sum(near_half, far_half, "dp", dp) + b_out
    middle = tokens_own.astype(F32) + gate_a * branch
    norm_b, spread_b = layer_norm(middle)
    hidden_b = (norm_b * (1.0 + scale_b) + shift_b).astype(BF16)
    hidden_b_all = gather_tokens(hidden_b).reshape(count, width)

    grad_mlp_all = (gate_b_all * cotangent_all.astype(F32)).astype(BF16).reshape(count, width)
    grad_output = cotangent_own.astype(F32)
    w_down_rows = jnp.zeros((dp, head_width, hidden_width), BF16)
    w_down_far = after(w_down_far, hidden_b).reshape(far, head_width, hidden_width)
    for mask in range(dp):
        part = w_down_parts[mask] if mask < 2 else w_down_far[mask - 2]
        w_down_rows = lax.dynamic_update_slice(
            w_down_rows, part[None], (me ^ mask, 0, 0), allow_negative_indices=False
        )
    w_down_rows = w_down_rows.reshape(width, hidden_width)
    b_up_own = cut(b_up, me * hidden_width, hidden_width)
    pre_act = dot(hidden_b_all, w_up) + b_up_own
    value, slope = gelu_pair(pre_act)
    activated, slope = lax.optimization_barrier((value.astype(BF16), slope.astype(BF16)))
    grad_act = dot(grad_mlp_all, w_down_rows)
    grad_pre = (grad_act * slope.astype(F32)).astype(BF16)
    far_half, near_half = products(
        lambda part: dot(part, w_up, 1, 1), lambda low, high: grad_pre[low:high]
    )
    grad_hidden_b = scatter_sum(near_half, far_half, "dp", dp)
    stages = log2(band)
    near_first = list(range(stages))
    far_first = [log2(across)] + [at for at in near_first if at != log2(across)]

    def halves(held, axis):
        size = held.shape[axis] // 2
        return [lax.slice_in_dim(held, at * size, (at + 1) * size, axis=axis) for at in range(2)]

    def choose(held, axis, bit):
        upper = ((group >> bit) & 1) == 1
        first, second = halves(held, axis)
        return jnp.where(upper, second, first), jnp.where(upper, first, second)

    def send(part, bit):
        return lax.ppermute(part, "band", xor_perm(band, 1 << bit))

    def joined(mine, came):
        return (mine.astype(F32) + came.astype(F32)).astype(BF16)

    def sum_groups(term, axes, bits, *waits):
        held = term
        for at, (axis, bit) in enumerate(zip(axes, bits, strict=True)):
            mine, far = choose(held, axis, bit)
            came = send(far, bit)
            if at < len(waits):
                came = after(came, *waits[at])
            held = joined(mine, came)
        return held

    def index_of(b, bits):
        return sum(((b >> bit) & 1) << (stages - 1 - at) for at, bit in enumerate(bits))

    def owner_pairs(bits, owner):
        return [
            (d * band + b, owner(d, index_of(b, bits))) for d in range(dp) for b in range(band)
        ]

    def by_rows(d, index):
        return (index // across) * band + across * d + index % across

    rows_then_units = [0] * log2(dp) + [1] * log2(across)
    grad_w_up = dot(hidden_b_all, after(grad_pre, near_half), 0, 0).astype(BF16)
    grad_w_down = dot(grad_mlp_all, after(activated, near_half), 0, 0).astype(BF16)
    up_mine, up_far = choose(grad_w_up, 0, near_first[0])
    down_mine, down_far = choose(grad_w_down, 0, far_first[0])
    up_far, down_far = halves(up_far, 0), halves(down_far, 0)
    up_came = [send(up_far[0], near_first[0])]
    down_came = [send(down_far[0], far_first[0])]
    grad_hidden_b = after(grad_hidden_b, up_came[0], down_came[0])
    up_came.append(send(after(up_far[1], grad_hidden_b), near_first[0]))
    down_came.append(send(after(down_far[1], grad_hidden_b), far_first[0]))

    grad_middle = grad_output + layer_norm_back(grad_hidden_b * (1.0 + scale_b), norm_b, spread_b)
    grad_branch = (gate_a * grad_middle).astype(BF16)
    grad_branch_all = gather_tokens(grad_branch, up_came[1], down_came[1]).reshape(count, width)
    far_mlp, near_mlp = products(
        lambda part: dot(part, w_down_rows, 1, 1),
        lambda low, high: after(activated, grad_branch)[low:high],
    )
    up_mine, up_far = choose(joined(up_mine, jnp.concatenate(up_came)), 0, near_first[1])
    down_mine, down_far = choose(joined(down_mine, jnp.concatenate(down_came)), 0, far_first[1])
    up_came, down_came = send(up_far, near_first[1]), send(down_far, far_first[1])
    grad_attended = dot(w_out_rows, grad_branch_all, 0, 1).astype(BF16)
    final_out = lax.psum_scatter(
        dot(grad_branch_all, attended, 0, 1).astype(BF16), "band", scatter_dimension=0, tiled=True
    )
    grad_q, grad_k, grad_v = attend_back(
        queries,
        keys,
        values,
        attended.reshape(heads, HD, count),
        grad_attended.reshape(heads, HD, count),
        prob_low,
    )
    if spans > 1:
        grad_k, grad_v = [
            lax.psum_scatter(
                member, "band", scatter_dimension=2, tiled=True, axis_index_groups=mates
            )
            for member in (grad_k, grad_v)
        ]
    grad_heads = jnp.concatenate(
        [member.reshape(head_width, count) for member in (grad_q, grad_k, grad_v)]
    )
    mlp_out = scatter_sum(near_mlp, after(far_mlp, grad_branch_all), "dp", dp, grad_heads) + b_down
    grad_heads = after(grad_heads, mlp_out, up_came, down_came)
    up_half, down_half = joined(up_mine, up_came), joined(down_mine, down_came)
    far_half, near_half = products(
        lambda part: dot(part, w_heads, 0, 0), lambda low, high: grad_heads[:, low:high]
    )
    grad_hidden_a = scatter_sum(near_half, far_half, "dp", dp)
    output = from_groups((middle + gate_b * mlp_out).astype(BF16))

    hot_tokens = jnp.broadcast_to(
        hot_all.T.astype(BF16)[:, :, None], (images, hot_all.shape[0], piece)
    ).reshape(images, count)

    def image_sums(near, far):
        return dot(hot_tokens[:, :half], near) + dot(hot_tokens[:, half:], far)

    near_half, far_half = near_half.reshape(half, width), far_half.reshape(half, width)
    grad_shift_a = image_sums(near_half, far_half)
    grad_scale_a = image_sums(near_half * norm_low[:half], far_half * norm_low[half:])

    def own_sums(member):
        pieces = jnp.sum(member, axis=1)
        return jnp.sum(jnp.where(own_hot[:, :, None], pieces[:, None], 0.0), axis=0)

    grad_mod = jnp.concatenate(
        [
            grad_shift_a,
            grad_scale_a,
            own_sums(grad_middle * branch),
            own_sums(grad_hidden_b),
            own_sums(grad_hidden_b * norm_b),
            own_sums(grad_output * mlp_out),
        ],
        axis=1,
    )
    grad_mod = jnp.transpose(grad_mod.reshape(images, dp, mod_width), (1, 0, 2))
    grad_mod_own = scatter_blocks(grad_mod, "dp", dp)
    high = grad_mod_own.astype(BF16)
    low = (grad_mod_own - high.astype(F32)).astype(BF16)
    grad_silu = dot(jnp.concatenate([high, low], axis=0), w_mod, 1, 1)
    grad_silu = grad_silu[:images] + grad_silu[images:]
    ones = jnp.ones((8, count), BF16)
    bias_own = jnp.concatenate(
        [
            jnp.sum(grad_mlp_all[: rows_dev * piece].astype(F32), axis=0),
            jnp.sum(grad_branch.astype(F32), axis=(0, 1)),
            dot(ones, grad_pre)[0],
            dot(ones, grad_heads, 1, 1)[0],
        ]
    )
    inputs = tokens_own.astype(F32)
    norm_a, spread_a = layer_norm(inputs)
    grad_tokens = grad_middle + layer_norm_back(grad_hidden_a * (1.0 + scale_a), norm_a, spread_a)
    grad_tokens = after(grad_tokens.astype(BF16), output)
    packed = jnp.concatenate([grad_mod_own.reshape(-1), grad_silu.reshape(-1), bias_own])
    packed = gather_all(after(packed, grad_tokens), "band", band)
    mod_size, silu_size = images * mod_width, images * width
    grad_mod_groups = packed[:, :mod_size].reshape(band * images, mod_width)
    grad_silu_groups = packed[:, mod_size : mod_size + silu_size].reshape(rows, spans, -1).sum(1)
    bias_sum = jnp.sum(packed[:, mod_size + silu_size :], axis=0)
    final_pack = jnp.concatenate(
        [grad_silu_groups.reshape(-1), jnp.sum(grad_mod_groups, axis=0), bias_sum]
    )
    final_pack = gather_all(final_pack, "dp", dp)

    grad_tokens_sent = grad_tokens
    grad_tokens = from_groups(grad_tokens)

    final_out = after(final_out, final_pack).T.astype(F32)
    final_up = sum_groups(up_half, rows_then_units[2:], near_first[2:], (packed,))
    final_up = lax.ppermute(final_up, both, owner_pairs(near_first, by_rows)).astype(F32)
    final_down = sum_groups(down_half, rows_then_units[2:], far_first[2:], (packed,))
    final_down = lax.ppermute(final_down.T, both, owner_pairs(far_first, by_rows)).astype(F32)
    hidden_a_late = after(hidden_a_all, near_half)
    grad_w_heads = dot(grad_heads, hidden_a_late).astype(BF16).reshape(3, across, unit, width)
    qkv_sum = sum_groups(
        after(grad_w_heads, grad_hidden_a),
        [1] * log2(across) + [3] * log2(dp),
        near_first,
        (packed,),
        (final_pack,),
    )
    qkv_sum = qkv_sum.reshape(3, unit, head_width)
    kind_of = [
        [next(kind for kind in range(3) if (kind * dp + d) % 3 == slot) for slot in range(3)]
        for d in range(dp)
    ]
    kind_now = [
        sum(
            jnp.where(slot_of[kind] == slot, kind, 0).astype(jnp.int32) for kind in range(3)
        )
        for slot in range(3)
    ]
    my_index = index_of(group, near_first)
    my_unit = my_index >> log2(dp)
    final_qkv = []
    for turn in range(3):
        slots = []
        for at in range(across):
            options = {
                slot
                for d in range(dp)
                for slot in range(3)
                if (band * kind_of[d][slot] + across * d + at) % 3 == turn
            }
            assert len(options) == 1
            slots.append(options.pop())

        def owner(d, index, slots=slots, turn=turn):
            at = index // dp
            start = band * kind_of[d][slots[at]] + across * d + at
            assert start % 3 == turn
            return (index % dp) * band + start // 3

        kind = sum(
            jnp.where(my_unit == at, kind_now[slots[at]], 0).astype(jnp.int32)
            for at in range(across)
        )
        final_qkv.append(
            lax.ppermute(pick(qkv_sum, kind), both, owner_pairs(near_first, owner))
        )
    final_qkv = jnp.concatenate(final_qkv).T.astype(F32)

    facts_all = gather_stack(after(facts, hidden_a_all), "dp", dp)
    facts_all = jnp.stack([facts_all[mask] for mask in order])
    index_all = xor_shuffle(facts_all, me_turned).reshape(rows, 2 * images)[:, images:].reshape(-1)
    condition = conditions(after(index_all, grad_branch))
    silu_all = jax.nn.silu(condition).astype(BF16)
    silu_end = rows * silu_size
    grad_silu_rows = jnp.sum(final_pack[:, :silu_end], axis=0).reshape(rows * images, width)
    ends = [silu_end]
    for size in (mod_width, width, width, hidden_width, head_width, head_width, head_width):
        ends.append(ends[-1] + size)
    tail = [final_pack[:, low:high] for low, high in zip(ends[:-1], ends[1:], strict=True)]
    final_b_mod = tail[0].reshape(-1)
    final_b_down = jnp.sum(tail[1], axis=0)
    final_b_out = jnp.sum(tail[2], axis=0)
    final_b_up = tail[3].reshape(-1)
    final_b_query = tail[4].reshape(-1)
    final_b_value = tail[6].reshape(-1)
    sigmoid = jax.nn.sigmoid(condition)
    grad_condition = grad_silu_rows * (sigmoid * (1.0 + condition * (1.0 - sigmoid)))
    table_hot = (
        classes[:, None] == index_all[None]
    ).astype(F32)
    final_table = jnp.dot(table_hot, grad_condition, precision=HIGHEST)
    mod_share = mod_width // across
    grad_mod_share = lax.ppermute(
        cut(grad_mod_groups, (my_index & (across - 1)) * mod_share, mod_share, 1),
        both,
        owner_pairs(near_first, by_rows),
    )
    silu_share = cut(silu_all, me * head_width, head_width, 1).astype(F32)
    silu_share = jnp.repeat(silu_share.reshape(rows, images, -1), spans, axis=0)
    final_mod = lax.dot_general(
        silu_share.reshape(band * images, -1),
        grad_mod_share,
        (((0,), (0,)), ((), ())),
        precision=HIGHEST,
        preferred_element_type=F32,
    )
    return (
        output,
        grad_tokens,
        final_table,
        final_mod,
        final_qkv,
        final_out,
        final_up,
        final_down,
        final_b_mod,
        final_b_query,
        final_b_value,
        final_b_out,
        final_b_up,
        final_b_down,
    )


def solution(mesh):
    rows = P("dp", "band", None)
    split = P(None, "dp")
    spread = P("dp", "band")
    return jax.shard_map(
        shards,
        mesh=mesh,
        in_specs=(
            rows,
            rows,
            P("dp", None),
            P("dp", None),
            P(),
            split,
            P(),
            split,
            P(),
            P(),
            split,
            P(),
            split,
            P(),
            split,
            P(),
        ),
        out_specs=(
            rows,
            rows,
            P(),
            spread,
            spread,
            spread,
            spread,
            P("band", "dp"),
            P(),
            P(),
            P(),
            P(),
            P(),
            P(),
        ),
        check_vma=False,
    )
```

```python
import functools
import math

import jax
import jax.numpy as jnp
from jax import lax
from jax.experimental import pallas as pl
from jax.experimental.pallas import tpu as pltpu
from jax.sharding import PartitionSpec as P

H = 16
HD = 72

EPSILON = 1e-06
HIGHEST = lax.Precision.HIGHEST
NEGATIVE = -1e30
GELU_COEF = 0.7978845608028654
FACTOR = 1.0 / math.sqrt(HD)
LOG2E = math.log2(math.e)
VMEM_LIMIT = 56 * 1024 * 1024
F32 = jnp.float32
BF16 = jnp.bfloat16


def dot(left, right, left_dim=1, right_dim=0):
    return lax.dot_general(
        left, right, (((left_dim,), (right_dim,)), ((), ())), preferred_element_type=F32
    )


def log2(count):
    assert count & (count - 1) == 0
    return count.bit_length() - 1


def reverse_bits(value, count):
    width = log2(count)
    return sum(((value >> at) & 1) << (width - 1 - at) for at in range(width)) if width else 0


def bits_up(count):
    return [1 << place for place in range(log2(count))]


def xor_perm(count, mask):
    return [(place, place ^ mask) for place in range(count)]


def pick(stack, place, axis=0):
    return lax.dynamic_index_in_dim(
        stack, place, axis, keepdims=False, allow_negative_indices=False
    )


def cut(array, start, size, axis=0):
    return lax.dynamic_slice_in_dim(array, start, size, axis, allow_negative_indices=False)


def xor_shuffle(array, mask):
    return jnp.stack([pick(array, mask ^ place) for place in range(array.shape[0])])


def together(*arrays):
    return lax.optimization_barrier(arrays)


def after(array, *others):
    return lax.optimization_barrier((array, *others))[0]


def gather_parts(part, axis, count, *waits):
    held = part[None]
    for bit in reversed(bits_up(count)):
        came = lax.ppermute(held, axis, xor_perm(count, bit))
        if waits and held.shape[0] == 1:
            came = after(came, *waits)
        held = jnp.concatenate([held, came])
    return held


def gather_stack(part, axis, count, bits=None):
    held, order = part[None], [0]
    for bit in bits or reversed(bits_up(count)):
        held = jnp.concatenate([held, lax.ppermute(held, axis, xor_perm(count, bit))])
        order = order + [mask ^ bit for mask in order]
    return jnp.stack([held[order.index(mask)] for mask in range(count)])


def gather_all(part, axis, count, bits=None):
    return xor_shuffle(gather_stack(part, axis, count, bits), lax.axis_index(axis))


def mask_order(count):
    order = [0]
    for bit in reversed(bits_up(count)):
        order = order + [place ^ bit for place in order]
    return order


def scatter_first(near, far, axis, count):
    return near.astype(F32) + lax.ppermute(far, axis, xor_perm(count, 1)).astype(F32)


def scatter_rest(held, axis, count, *waits):
    for bit in bits_up(count)[1:]:
        half = held.shape[0] // 2
        came = lax.ppermute(held[half:].astype(BF16), axis, xor_perm(count, bit))
        if waits and half == 1:
            came = after(came, *waits)
        held = held[:half] + came.astype(F32)
    return held[0]


def scatter_sum(near, far, axis, count, *waits):
    return scatter_rest(scatter_first(near, far, axis, count), axis, count, *waits)


def exchange(parts, axis, count):
    held = xor_shuffle(parts, lax.axis_index(axis))[None]
    for bit in reversed(bits_up(count)):
        half = held.shape[1] // 2
        came = lax.ppermute(held[:, half:], axis, xor_perm(count, bit))
        held = jnp.concatenate([held[:, :half], came])
    return held[:, 0]


def scatter_blocks(parts, axis, count):
    me = lax.axis_index(axis)
    held = parts
    for at, bit in enumerate(bits_up(count)):
        held = held.reshape((-1, 2) + parts.shape[1:])
        mine = (me >> at) & 1
        held = pick(held, mine, 1) + lax.ppermute(
            pick(held, mine ^ 1, 1), axis, xor_perm(count, bit)
        )
    return held[0]


def attend_kernel(piece, facts_ref, q_ref, k_ref, v_ref, out_ref, prob_ref):
    step = pl.program_id(1)
    keys_len, lanes = k_ref.shape[-1], q_ref.shape[-1]
    pieces_key, pieces_query = keys_len // piece, lanes // piece
    values = v_ref[0]

    def finish(scores):
        top = jnp.max(scores, axis=0, keepdims=True)
        exponent = jnp.exp2(scores * (FACTOR * LOG2E) - top * (FACTOR * LOG2E))
        total = jnp.sum(exponent, axis=0, keepdims=True)
        prob = (exponent * (1.0 / total)).astype(BF16)
        prob_ref[0] = prob
        out_ref[0] = dot(values, prob).astype(BF16)

    scores = dot(k_ref[0], q_ref[0], 0, 0)

    @pl.when(facts_ref[0] == 1)
    def _():
        finish(scores)

    @pl.when(facts_ref[0] != 1)
    def _():
        seg_key = jnp.concatenate(
            [jnp.full((piece, 1), facts_ref[1 + at], jnp.int32) for at in range(pieces_key)], axis=0
        )
        base = 1 + pieces_key + step * pieces_query
        seg_query = jnp.concatenate(
            [jnp.full((1, piece), facts_ref[base + at], jnp.int32) for at in range(pieces_query)],
            axis=1,
        )
        finish(jnp.where(seg_key == seg_query, scores, NEGATIVE))


def attend(queries, keys, values, facts, piece):
    heads, depth, count = queries.shape
    keys_len = keys.shape[2]
    lanes = min(512, count)
    chunk = lambda head, step, facts: (head, 0, step)
    whole = lambda head, step, facts: (head, 0, 0)
    return pl.pallas_call(
        functools.partial(attend_kernel, piece),
        grid_spec=pltpu.PrefetchScalarGridSpec(
            num_scalar_prefetch=1,
            grid=(heads, count // lanes),
            in_specs=[
                pl.BlockSpec((1, depth, lanes), chunk),
                pl.BlockSpec((1, depth, keys_len), whole),
                pl.BlockSpec((1, depth, keys_len), whole),
            ],
            out_specs=[
                pl.BlockSpec((1, depth, lanes), chunk),
                pl.BlockSpec((1, keys_len, lanes), chunk),
            ],
        ),
        out_shape=[
            jax.ShapeDtypeStruct((heads, depth, count), BF16),
            jax.ShapeDtypeStruct((heads, keys_len, count), BF16),
        ],
        compiler_params=pltpu.CompilerParams(vmem_limit_bytes=VMEM_LIMIT),
        cost_estimate=pl.CostEstimate(
            flops=30 * count * keys_len * heads * 128,
            bytes_accessed=2 * heads * count * keys_len,
            transcendentals=heads * count * keys_len,
        ),
        name="attend",
    )(facts, queries, keys, values)


def attend_back_kernel(
    q_ref, k_ref, v_ref, out_ref, grad_ref, prob_ref, dq_ref, dk_ref, dv_ref, dk_sum, dv_sum
):
    step = pl.program_id(1)
    grad = grad_ref[0]
    prob = prob_ref[0]
    delta = jnp.sum(grad.astype(F32) * out_ref[0].astype(F32), axis=0, keepdims=True)
    grad_prob = dot(v_ref[0], grad, 0, 0)
    grad_score = (prob.astype(F32) * (grad_prob - delta)).astype(BF16)
    dq_ref[0] = (dot(k_ref[0], grad_score) * FACTOR).astype(BF16)
    dk_part = dot(grad_score, q_ref[0], 1, 1)
    dv_part = dot(prob, grad, 1, 1)

    @pl.when(step == 0)
    def _():
        dk_sum[...] = dk_part
        dv_sum[...] = dv_part

    @pl.when(step != 0)
    def _():
        dk_sum[...] += dk_part
        dv_sum[...] += dv_part

    @pl.when(step == pl.num_programs(1) - 1)
    def _():
        dk_ref[0] = jnp.transpose(dk_sum[...] * FACTOR).astype(BF16)
        dv_ref[0] = jnp.transpose(dv_sum[...]).astype(BF16)


def attend_back(queries, keys, values, attended, grad, prob):
    heads, depth, count = queries.shape
    keys_len = keys.shape[2]
    lanes = min(512, count)
    chunk = lambda head, step: (head, 0, step)
    whole = lambda head, step: (head, 0, 0)
    return pl.pallas_call(
        attend_back_kernel,
        grid=(heads, count // lanes),
        in_specs=[
            pl.BlockSpec((1, depth, lanes), chunk),
            pl.BlockSpec((1, depth, keys_len), whole),
            pl.BlockSpec((1, depth, keys_len), whole),
            pl.BlockSpec((1, depth, lanes), chunk),
            pl.BlockSpec((1, depth, lanes), chunk),
            pl.BlockSpec((1, keys_len, lanes), chunk),
        ],
        out_specs=[
            pl.BlockSpec((1, depth, lanes), chunk),
            pl.BlockSpec((1, depth, keys_len), whole),
            pl.BlockSpec((1, depth, keys_len), whole),
        ],
        out_shape=[
            jax.ShapeDtypeStruct((heads, depth, count), BF16),
            jax.ShapeDtypeStruct((heads, depth, keys_len), BF16),
            jax.ShapeDtypeStruct((heads, depth, keys_len), BF16),
        ],
        scratch_shapes=[pltpu.VMEM((keys_len, depth), F32), pltpu.VMEM((keys_len, depth), F32)],
        compiler_params=pltpu.CompilerParams(vmem_limit_bytes=VMEM_LIMIT),
        cost_estimate=pl.CostEstimate(
            flops=30 * count * keys_len * heads * 128,
            bytes_accessed=2 * heads * count * keys_len,
            transcendentals=0,
        ),
        name="attend_back",
    )(queries, keys, values, attended, grad, prob)


def gelu_pair(inputs):
    square = inputs * inputs
    tanh = jnp.tanh(GELU_COEF * (inputs + 0.044715 * inputs * square))
    value = 0.5 * inputs * (1.0 + tanh)
    slope = 0.5 * (1.0 + tanh) + 0.5 * inputs * (1.0 - tanh * tanh) * (
        GELU_COEF * (1.0 + 3.0 * 0.044715 * square)
    )
    return value, slope


def layer_norm(inputs):
    average = jnp.mean(inputs, axis=-1, keepdims=True)
    centred = inputs - average
    spread = jnp.mean(centred * centred, axis=-1, keepdims=True)
    scale = lax.rsqrt(spread + EPSILON)
    return centred * scale, scale


def layer_norm_back(grad, norm, scale):
    first = jnp.mean(grad, axis=-1, keepdims=True)
    second = jnp.mean(grad * norm, axis=-1, keepdims=True)
    return (grad - first - norm * second) * scale


def shards(
    tokens,
    cotangent,
    lengths,
    cond_index,
    cond_table,
    w_mod,
    b_mod,
    w_qkv,
    b_query,
    b_value,
    w_out,
    b_out,
    w_up,
    b_up,
    w_down,
    b_down,
):
    rows_dev, piece, width = tokens.shape
    dp, band = lax.axis_size("dp"), lax.axis_size("band")
    me, group = lax.axis_index("dp"), lax.axis_index("band")
    images = lengths.shape[1]
    rows = rows_dev * dp
    spans = band // rows
    assert band % rows == 0
    across = band // dp
    unit = width // band
    heads = H // dp
    head_width = width // dp
    mod_width = w_mod.shape[1]
    hidden_width = w_up.shape[1]
    both = ("dp", "band")
    me_turned = reverse_bits(me, dp)

    def target(d, b, turn):
        local = ((b >> log2(dp)) & (rows_dev - 1)) ^ turn
        to_group = (rows_dev * reverse_bits(d, dp) + local) * spans + b // rows
        return reverse_bits(b % dp, dp) * band + to_group

    outward = [
        [(d * band + b, target(d, b, turn)) for d in range(dp) for b in range(band)]
        for turn in range(rows_dev)
    ]
    inward = [[(there, here) for here, there in pairs] for pairs in outward]
    my_slot = (group >> log2(dp)) & (rows_dev - 1)

    def to_groups(local):
        return jnp.stack(
            [
                lax.ppermute(pick(local, my_slot ^ turn), both, outward[turn])
                for turn in range(rows_dev)
            ]
        )

    def from_groups(held):
        came = jnp.stack(
            [lax.ppermute(held[turn], both, inward[turn]) for turn in range(rows_dev)]
        )
        return xor_shuffle(came, my_slot)

    group_row = group >> log2(spans)
    my_local = group_row & (rows_dev - 1)
    order = mask_order(dp)
    places = jnp.arange(dp, dtype=jnp.int32)[:, None]
    turns = jnp.arange(rows_dev, dtype=jnp.int32)[None]
    piece_first = piece * (
        (group & (spans - 1)) * rows + ((my_local ^ turns) * dp) + (me_turned ^ places)
    )

    facts = jnp.concatenate([lengths, cond_index], axis=1)
    facts_own = lax.ppermute(pick(facts, my_slot), both, outward[0])
    tokens_sent = [pick(tokens, my_slot ^ turn) for turn in range(rows_dev)]
    tokens_own = jnp.stack(
        [lax.ppermute(part, both, outward[turn]) for turn, part in enumerate(tokens_sent)]
    )
    slot_to = [[(3 * d + slot) % dp for d in range(dp)] for slot in range(3)]
    w_qkv = after(w_qkv, tokens_sent)
    w_slots = [w_qkv.T[slot * head_width : (slot + 1) * head_width] for slot in range(3)]
    stay = [[d == to for d, to in enumerate(target)] for target in slot_to]
    if all(first != last for first, last in zip(stay[0], stay[2], strict=True)):
        keeps_first = functools.reduce(
            jnp.logical_or, [me == d for d in range(dp) if stay[0][d]]
        )
        slots_sent = jnp.where(keeps_first, w_slots[2], w_slots[0])
        came = lax.ppermute(
            slots_sent,
            "dp",
            [(d, slot_to[2 if stay[0][d] else 0][d]) for d in range(dp)],
        )
        w_slots = [
            jnp.where(keeps_first, w_slots[0], came),
            lax.ppermute(w_slots[1], "dp", list(enumerate(slot_to[1]))),
            jnp.where(keeps_first, came, w_slots[2]),
        ]
    else:
        slots_sent = w_slots[0]
        w_slots = [
            lax.ppermute(w_slots[slot], "dp", list(enumerate(slot_to[slot]))) for slot in range(3)
        ]
    row_blocks = jnp.concatenate(
        [jnp.stack(jnp.split(member.T, dp, axis=1)) for member in (w_down, w_out)], axis=2
    )

    image_ends = jnp.cumsum(facts_own[:images])
    classes = jnp.arange(cond_table.shape[0], dtype=jnp.int32)

    def conditions(index):
        return dot((index[:, None] == classes[None]).astype(BF16), cond_table)

    silu_own = jax.nn.silu(conditions(facts_own[images:])).astype(BF16)
    mod_part = dot(after(silu_own, slots_sent), w_mod) + cut(b_mod, me * mod_width, mod_width)
    modulation = gather_stack(mod_part, "dp", dp)
    tokens_own, w_slots, modulation = together(tokens_own, w_slots, modulation)
    modulation = xor_shuffle(modulation, me)
    seg_all = jnp.sum(
        (image_ends[None, None] <= piece_first[..., None]).astype(jnp.int32), axis=-1
    ).reshape(-1)
    image_ids = jnp.arange(images, dtype=jnp.int32)
    hot_all = seg_all[:, None] == image_ids[None]
    modulation = jnp.transpose(modulation, (1, 0, 2)).reshape(images, 6 * width)
    mod_all = jnp.dot(hot_all.astype(F32), modulation, precision=HIGHEST)
    mod_all = [part[:, None] for part in jnp.split(mod_all, 6, axis=1)]
    shift_a_all, scale_a_all, gate_b_all = [mod_all[at] for at in (0, 1, 5)]
    scale_a, gate_a, shift_b, scale_b, gate_b = [
        mod_all[at][:rows_dev] for at in (1, 2, 3, 4, 5)
    ]
    own_hot = hot_all[:rows_dev]

    def gather_tokens(own, *waits):
        return gather_parts(own, "dp", dp, *waits).reshape((-1,) + own.shape[1:])

    tokens_all = gather_tokens(tokens_own)
    cotangent, row_blocks, _ = together(cotangent, row_blocks, tokens_own)
    slot_of = [lax.rem(me + kind * (dp % 3), 3) for kind in range(3)]
    w_heads = jnp.concatenate(
        [
            jnp.where(
                slot_of[kind] == 0,
                w_slots[0],
                jnp.where(slot_of[kind] == 1, w_slots[1], w_slots[2]),
            )
            for kind in range(3)
        ]
    )
    bias_heads = jnp.concatenate(
        [
            cut(b_query, me * head_width, head_width),
            jnp.zeros((head_width,), F32),
            cut(b_value, me * head_width, head_width),
        ]
    )
    norm_all = layer_norm(tokens_all.astype(F32))[0]
    hidden_a_all = (norm_all * (1.0 + scale_a_all) + shift_a_all).astype(BF16).reshape(-1, width)
    norm_low = norm_all.astype(BF16).reshape(-1, width)
    cotangent_own = to_groups(cotangent)
    count = hidden_a_all.shape[0]
    half = count // 2
    row_parts = {
        2: lax.ppermute(after(pick(row_blocks, me ^ 2), tokens_all), "dp", xor_perm(dp, 2))
    }
    projected = (dot(w_heads, hidden_a_all, 1, 1) + bias_heads[:, None]).astype(BF16)
    projected, row_parts = together(projected, row_parts)
    projected = projected.reshape(3, heads, HD, count)
    queries, keys, values = projected[0], projected[1], projected[2]
    seg_row = seg_all
    if spans > 1:
        mates = [[at * spans + span for span in range(spans)] for at in range(rows)]
        keys, values, seg_row = [
            lax.all_gather(
                member, "band", axis=member.ndim - 1, tiled=True, axis_index_groups=mates
            )
            for member in (keys, values, seg_row)
        ]
    one_image = jnp.all(seg_row == seg_row[0]).astype(jnp.int32)
    attend_facts = jnp.concatenate([one_image[None], seg_row, seg_all])
    attended, prob_low = attend(queries, keys, values, attend_facts, piece)
    row_blocks = after(row_blocks, projected)
    row_parts[0] = pick(row_blocks, me)
    for mask in range(1, dp):
        if mask != 2:
            row_parts[mask] = lax.ppermute(
                pick(row_blocks, me ^ mask), "dp", xor_perm(dp, mask)
            )
    attended, cotangent_own, row_parts = together(attended, cotangent_own, row_parts)
    attended = attended.reshape(head_width, count)
    row_parts = jnp.stack([row_parts[mask] for mask in range(dp)])
    w_out_rows = jnp.concatenate(list(xor_shuffle(row_parts[:, :, hidden_width:], me)))

    def split_own(partial):
        return partial.astype(BF16).reshape(dp // 2, rows_dev, piece, width)

    def products(product, left):
        return split_own(product(left(half, count))), split_own(product(left(0, half)))

    far_half, near_half = products(
        lambda part: dot(part, w_out_rows, 0, 1), lambda low, high: attended[:, low:high]
    )
    branch = scatter_sum(near_half, far_half, "dp", dp) + b_out
    middle = tokens_own.astype(F32) + gate_a * branch
    norm_b, spread_b = layer_norm(middle)
    hidden_b = (norm_b * (1.0 + scale_b) + shift_b).astype(BF16)
    row_parts, _ = together(row_parts, far_half)
    w_down_rows = jnp.concatenate(list(xor_shuffle(row_parts[:, :, :hidden_width], me)))
    hidden_b_all = gather_tokens(hidden_b).reshape(count, width)

    cotangent_all = gather_tokens(after(cotangent_own, hidden_b_all))
    grad_output = cotangent_own.astype(F32)
    b_up_own = cut(b_up, me * hidden_width, hidden_width)
    pre_act = dot(hidden_b_all, w_up) + b_up_own
    value, slope = gelu_pair(pre_act)
    activated, slope = lax.optimization_barrier((value.astype(BF16), slope.astype(BF16)))
    far_mlp, near_mlp = products(
        lambda part: dot(part, w_down_rows, 1, 1), lambda low, high: activated[low:high]
    )
    mlp_out = scatter_first(near_mlp, far_mlp, "dp", dp)
    cotangent_all, mlp_out = together(cotangent_all, mlp_out)
    grad_mlp_all = (gate_b_all * cotangent_all.astype(F32)).astype(BF16).reshape(count, width)
    mlp_out = scatter_rest(mlp_out, "dp", dp) + b_down
    grad_act = dot(grad_mlp_all, w_down_rows)
    grad_pre = (grad_act * slope.astype(F32)).astype(BF16)
    far_half, near_half = products(
        lambda part: dot(part, w_up, 1, 1), lambda low, high: grad_pre[low:high]
    )
    grad_hidden_b = scatter_first(near_half, far_half, "dp", dp)
    mlp_out, grad_hidden_b, near_half, grad_pre, activated = together(
        mlp_out, grad_hidden_b, near_half, grad_pre, activated
    )
    grad_hidden_b = scatter_rest(grad_hidden_b, "dp", dp)
    stages = log2(band)
    near_first = list(range(stages))

    def halves(held, axis):
        size = held.shape[axis] // 2
        return [lax.slice_in_dim(held, at * size, (at + 1) * size, axis=axis) for at in range(2)]

    def choose(held, axis, bit, plain=False):
        upper = (group >> bit) & 1
        if bit >= log2(across) and not plain:
            upper = upper ^ ((me >> (bit - log2(across))) & 1)
        upper = upper == 1
        first, second = halves(held, axis)
        return jnp.where(upper, second, first), jnp.where(upper, first, second)

    def send(part, bit):
        return lax.ppermute(part, "band", xor_perm(band, 1 << bit))

    def joined(mine, came):
        return (mine.astype(F32) + came.astype(F32)).astype(BF16)

    def sum_groups(term, axes, bits, plain=False):
        held = term
        for axis, bit in zip(axes, bits, strict=True):
            mine, far = choose(held, axis, bit, plain)
            held = joined(mine, send(far, bit))
        return held

    def piece_at(d, b):
        return reverse_bits((b // across) ^ d, dp), reverse_bits(b % across, across)

    def owner_pairs(owner):
        return [
            (d * band + b, owner(d, b, *piece_at(d, b))) for d in range(dp) for b in range(band)
        ]

    near_bits, far_bits = near_first[: log2(across)], near_first[log2(across) :]
    first_far = far_bits[0]
    grad_w_up = dot(hidden_b_all, grad_pre, 0, 0).astype(BF16)
    grad_w_down = dot(grad_mlp_all, activated, 0, 0).astype(BF16)
    up_mine, up_far = choose(grad_w_up, 1, near_bits[0])
    down_mine, down_far = choose(grad_w_down, 0, first_far)
    up_far, down_far = halves(up_far, 0), halves(down_far, 0)
    up_came = [send(up_far[0], near_bits[0])]
    down_came = [send(down_far[0], first_far)]
    grad_hidden_b = after(grad_hidden_b, up_came[0], down_came[0])
    up_came.append(send(after(up_far[1], grad_hidden_b), near_bits[0]))
    down_came.append(send(after(down_far[1], grad_hidden_b), first_far))

    grad_middle = grad_output + layer_norm_back(grad_hidden_b * (1.0 + scale_b), norm_b, spread_b)
    grad_branch = (gate_a * grad_middle).astype(BF16)
    grad_branch_all = gather_tokens(grad_branch, up_came[1], down_came[1]).reshape(count, width)
    middle, mlp_out, _ = together(middle, mlp_out, grad_branch)
    output = (middle + gate_b * mlp_out).astype(BF16)
    up_mine, up_far = choose(joined(up_mine, jnp.concatenate(up_came)), 0, first_far)
    down_mine, down_far = choose(joined(down_mine, jnp.concatenate(down_came)), 1, near_bits[0])
    up_came, down_came = send(up_far, first_far), send(down_far, near_bits[0])
    grad_attended = dot(w_out_rows, grad_branch_all, 0, 1).astype(BF16)
    out_mine, out_far = choose(
        dot(grad_branch_all, attended, 0, 1)
        .astype(BF16)
        .reshape((2,) * stages + (unit, head_width)),
        stages - 1,
        0,
        plain=True,
    )
    out_came = send(out_far, 0)
    grad_q, grad_k, grad_v = attend_back(
        queries,
        keys,
        values,
        attended.reshape(heads, HD, count),
        grad_attended.reshape(heads, HD, count),
        prob_low,
    )
    if spans > 1:
        grad_k, grad_v = [
            lax.psum_scatter(
                member, "band", scatter_dimension=2, tiled=True, axis_index_groups=mates
            )
            for member in (grad_k, grad_v)
        ]
    grad_heads = jnp.concatenate(
        [member.reshape(head_width, count) for member in (grad_q, grad_k, grad_v)]
    )
    output_came = [
        lax.ppermute(after(output[turn], grad_branch_all), both, inward[turn])
        for turn in range(rows_dev - 1)
    ]
    grad_heads, up_came, down_came, out_came, output_came = together(
        grad_heads, up_came, down_came, out_came, output_came
    )
    far_half, near_half = products(
        lambda part: dot(part, w_heads, 0, 0), lambda low, high: grad_heads[:, low:high]
    )
    grad_hidden_a = scatter_first(near_half, far_half, "dp", dp)
    out_came, grad_heads, near_half, far_half, _ = together(
        out_came, grad_heads, near_half, far_half, grad_hidden_a
    )
    grad_hidden_a = scatter_rest(grad_hidden_a, "dp", dp)
    up_mine, up_came, down_mine, down_came, _ = together(
        up_mine, up_came, down_mine, down_came, near_half
    )
    up_down = jnp.stack([joined(up_mine, up_came), joined(down_mine, down_came)])
    up_down_rest = [2] * (len(near_bits) - 1) + [1] * (len(far_bits) - 1), near_bits[1:] + far_bits[1:]
    up_down_mine, up_down_far = choose(up_down, up_down_rest[0][0], up_down_rest[1][0])
    up_down_came = send(up_down_far, up_down_rest[1][0])
    grad_w_heads = dot(grad_heads, hidden_a_all).astype(BF16).reshape(3, across, unit, width)
    qkv_axes = [1] * log2(across) + [3] * log2(dp)
    qkv_mine, qkv_far = choose(grad_w_heads, qkv_axes[0], near_first[0])
    qkv_came = send(qkv_far, near_first[0])
    output_came = output_came + [
        lax.ppermute(after(output[-1], grad_heads), both, inward[rows_dev - 1])
    ]
    out_half = joined(out_mine, out_came)
    near_half, far_half, _ = together(near_half, far_half, (qkv_far, up_down_far))

    hot_tokens = jnp.broadcast_to(
        hot_all.T.astype(BF16)[:, :, None], (images, hot_all.shape[0], piece)
    ).reshape(images, count)

    def image_sums(near, far):
        return dot(hot_tokens[:, :half], near) + dot(hot_tokens[:, half:], far)

    near_half, far_half = near_half.reshape(half, width), far_half.reshape(half, width)
    grad_shift_a = image_sums(near_half, far_half)
    grad_scale_a = image_sums(near_half * norm_low[:half], far_half * norm_low[half:])

    def own_sums(member):
        pieces = jnp.sum(member, axis=1)
        return jnp.sum(jnp.where(own_hot[:, :, None], pieces[:, None], 0.0), axis=0)

    grad_mod = jnp.concatenate(
        [
            grad_shift_a,
            grad_scale_a,
            own_sums(grad_middle * branch),
            own_sums(grad_hidden_b),
            own_sums(grad_hidden_b * norm_b),
            own_sums(grad_output * mlp_out),
        ],
        axis=1,
    )
    grad_mod = jnp.transpose(grad_mod.reshape(images, dp, mod_width), (1, 0, 2))
    grad_mod_own = jnp.sum(lax.all_to_all(grad_mod, "dp", 0, 0, tiled=True), axis=0)
    high = grad_mod_own.astype(BF16)
    low = (grad_mod_own - high.astype(F32)).astype(BF16)
    grad_silu = dot(jnp.concatenate([high, low], axis=0), w_mod, 1, 1)
    grad_silu = grad_silu[:images] + grad_silu[images:]
    ones = jnp.ones((8, count), BF16)
    bias_rows = [
        jnp.sum(grad_mlp_all[: rows_dev * piece].astype(F32), axis=0),
        jnp.sum(grad_branch.astype(F32), axis=(0, 1)),
        dot(ones, grad_pre)[0],
        dot(ones, grad_heads, 1, 1)[0],
    ]
    assert images >= len(bias_rows)
    bias_rows = [
        jnp.pad(member, (0, width - member.shape[0])) for member in bias_rows
    ] + [jnp.zeros((width,), F32)] * (images - len(bias_rows))
    packed = jnp.concatenate([grad_mod_own, grad_silu, jnp.stack(bias_rows)], axis=1)
    grad_hidden_a, output_came, packed = together(grad_hidden_a, output_came, packed)
    output = xor_shuffle(jnp.stack(output_came), my_slot)
    inputs = tokens_own.astype(F32)
    norm_a, spread_a = layer_norm(inputs)
    grad_tokens = grad_middle + layer_norm_back(grad_hidden_a * (1.0 + scale_a), norm_a, spread_a)
    grad_tokens = grad_tokens.astype(BF16)
    grad_tokens_came = [
        lax.ppermute(grad_tokens[turn], both, inward[turn]) for turn in range(rows_dev)
    ]
    packed, _ = together(packed, grad_tokens)
    packed = gather_all(packed, "band", band, [1 << bit for bit in far_bits + near_bits])
    packed, qkv_came, up_down_came, out_half = together(
        packed, qkv_came, up_down_came, out_half
    )
    qkv_half = joined(qkv_mine, qkv_came)
    qkv_mine, qkv_far = choose(qkv_half, qkv_axes[1], near_first[1])
    qkv_came = send(qkv_far, near_first[1])
    out_mine, out_far = choose(out_half, stages - 2, near_first[1], plain=True)
    out_came = send(out_far, near_first[1])
    up_down = sum_groups(
        joined(up_down_mine, up_down_came), up_down_rest[0][1:], up_down_rest[1][1:]
    )
    grad_tokens = xor_shuffle(jnp.stack(grad_tokens_came), my_slot)
    grad_mod_groups = packed[:, :, :mod_width].reshape(band * images, mod_width)
    grad_silu_groups = packed[:, :, mod_width : mod_width + width]
    grad_silu_groups = grad_silu_groups.reshape(rows, spans, images, width).sum(1)
    mod_sum = jnp.sum(grad_mod_groups, axis=0)
    mod_rows = -(-mod_width // width)
    mod_sum = jnp.pad(mod_sum, (0, mod_rows * width - mod_width)).reshape(mod_rows, width)
    final_pack = jnp.concatenate(
        [
            grad_silu_groups.reshape(rows * images, width),
            jnp.sum(packed[:, :, mod_width + width :], axis=0),
            mod_sum,
        ]
    )
    qkv_sum = sum_groups(joined(qkv_mine, qkv_came), qkv_axes[2:], near_first[2:])
    qkv_sum = qkv_sum.reshape(3, unit, head_width)
    out_sum = sum_groups(
        joined(out_mine, out_came), list(reversed(range(stages - 2))), near_first[2:], plain=True
    )
    final_out = out_sum.reshape(unit, head_width).T.astype(F32)
    final_pack = gather_all(final_pack, "dp", dp)
    up_down = lax.ppermute(up_down, both, owner_pairs(lambda d, b, block, unit: block * band + b))
    up_down = lax.ppermute(
        after(up_down, qkv_sum),
        both,
        [
            (d * band + b, d * band + ((b // across) ^ reverse_bits(d, dp)) * across + reverse_bits(b % across, across))
            for d in range(dp)
            for b in range(band)
        ],
    )
    final_up, final_down = up_down[0].astype(F32), up_down[1].T.astype(F32)

    kind_of = [
        [next(kind for kind in range(3) if (kind * dp + d) % 3 == slot) for slot in range(3)]
        for d in range(dp)
    ]
    kind_now = [
        sum(
            jnp.where(slot_of[kind] == slot, kind, 0).astype(jnp.int32) for kind in range(3)
        )
        for slot in range(3)
    ]
    my_unit = reverse_bits(group & (across - 1), across)
    final_qkv = []
    for turn in range(3):
        slots = []
        for at in range(across):
            options = {
                slot
                for d in range(dp)
                for slot in range(3)
                if (band * kind_of[d][slot] + across * d + at) % 3 == turn
            }
            assert len(options) == 1
            slots.append(options.pop())

        def owner(d, b, block, at, slots=slots, turn=turn):
            start = band * kind_of[d][slots[at]] + across * d + at
            assert start % 3 == turn
            return block * band + start // 3

        kind = sum(
            jnp.where(my_unit == at, kind_now[slots[at]], 0).astype(jnp.int32)
            for at in range(across)
        )
        final_qkv.append(
            lax.ppermute(pick(qkv_sum, kind), both, owner_pairs(owner))
        )
    final_qkv = jnp.concatenate(final_qkv).T.astype(F32)

    facts_all = gather_stack(after(facts, hidden_a_all), "dp", dp)
    facts_all = jnp.stack([facts_all[mask] for mask in order])
    index_all = xor_shuffle(facts_all, me_turned).reshape(rows, 2 * images)[:, images:].reshape(-1)
    condition = conditions(after(index_all, grad_branch))
    silu_all = jax.nn.silu(condition).astype(BF16)
    silu_rows = rows * images
    grad_silu_rows = jnp.sum(final_pack[:, :silu_rows], axis=0)
    bias_all = final_pack[:, silu_rows : silu_rows + images]
    final_b_down = jnp.sum(bias_all[:, 0], axis=0)
    final_b_out = jnp.sum(bias_all[:, 1], axis=0)
    final_b_up = bias_all[:, 2, :hidden_width].reshape(-1)
    final_b_query = bias_all[:, 3, :head_width].reshape(-1)
    final_b_value = bias_all[:, 3, 2 * head_width : 3 * head_width].reshape(-1)
    final_b_mod = final_pack[:, silu_rows + images :].reshape(dp, -1)[:, :mod_width].reshape(-1)
    sigmoid = jax.nn.sigmoid(condition)
    grad_condition = grad_silu_rows * (sigmoid * (1.0 + condition * (1.0 - sigmoid)))
    table_hot = (
        classes[:, None] == index_all[None]
    ).astype(F32)
    final_table = jnp.dot(table_hot, grad_condition, precision=HIGHEST)
    mod_share = mod_width // across
    grad_mod_share = lax.ppermute(
        cut(grad_mod_groups, my_unit * mod_share, mod_share, 1),
        both,
        owner_pairs(lambda d, b, block, at: block * band + across * d + at),
    )
    silu_share = cut(silu_all, me * head_width, head_width, 1).astype(F32)
    silu_share = jnp.repeat(silu_share.reshape(rows, images, -1), spans, axis=0)
    final_mod = lax.dot_general(
        silu_share.reshape(band * images, -1),
        grad_mod_share,
        (((0,), (0,)), ((), ())),
        precision=HIGHEST,
        preferred_element_type=F32,
    )
    return (
        output,
        grad_tokens,
        final_table,
        final_mod,
        final_qkv,
        final_out,
        final_up,
        final_down,
        final_b_mod,
        final_b_query,
        final_b_value,
        final_b_out,
        final_b_up,
        final_b_down,
    )


def solution(mesh):
    rows = P("dp", "band", None)
    split = P(None, "dp")
    spread = P("dp", "band")
    return jax.shard_map(
        shards,
        mesh=mesh,
        in_specs=(
            rows,
            rows,
            P("dp", None),
            P("dp", None),
            P(),
            split,
            P(),
            split,
            P(),
            P(),
            split,
            P(),
            split,
            P(),
            split,
            P(),
        ),
        out_specs=(
            rows,
            rows,
            P(),
            spread,
            spread,
            spread,
            spread,
            P("band", "dp"),
            P(),
            P(),
            P(),
            P(),
            P(),
            P(),
        ),
        check_vma=False,
    )
```

```python
import functools
import math

import jax
import jax.numpy as jnp
from jax import lax
from jax.experimental import pallas as pl
from jax.experimental.pallas import tpu as pltpu
from jax.sharding import PartitionSpec as P

H = 16
HD = 72

EPSILON = 1e-06
HIGHEST = lax.Precision.HIGHEST
NEGATIVE = -1e30
GELU_COEF = 0.7978845608028654
FACTOR = 1.0 / math.sqrt(HD)
LOG2E = math.log2(math.e)
VMEM_LIMIT = 56 * 1024 * 1024
F32 = jnp.float32
BF16 = jnp.bfloat16


def dot(left, right, left_dim=1, right_dim=0):
    return lax.dot_general(
        left, right, (((left_dim,), (right_dim,)), ((), ())), preferred_element_type=F32
    )


def log2(count):
    assert count & (count - 1) == 0
    return count.bit_length() - 1


def reverse_bits(value, count):
    width = log2(count)
    return sum(((value >> at) & 1) << (width - 1 - at) for at in range(width)) if width else 0


def bits_up(count):
    return [1 << place for place in range(log2(count))]


def xor_perm(count, mask):
    return [(place, place ^ mask) for place in range(count)]


def pick(stack, place, axis=0):
    return lax.dynamic_index_in_dim(
        stack, place, axis, keepdims=False, allow_negative_indices=False
    )


def cut(array, start, size, axis=0):
    return lax.dynamic_slice_in_dim(array, start, size, axis, allow_negative_indices=False)


def xor_shuffle(array, mask):
    return jnp.stack([pick(array, mask ^ place) for place in range(array.shape[0])])


def together(*arrays):
    return lax.optimization_barrier(arrays)


def gather_parts(part, axis, count):
    held = part[None]
    for bit in reversed(bits_up(count)):
        held = jnp.concatenate([held, lax.ppermute(held, axis, xor_perm(count, bit))])
    return held


def gather_stack(part, axis, count):
    held = gather_parts(part, axis, count)
    return jnp.stack([held[reverse_bits(mask, count)] for mask in range(count)])


def gather_all(part, axis, count):
    return xor_shuffle(gather_stack(part, axis, count), lax.axis_index(axis))


def mask_order(count):
    order = [0]
    for bit in reversed(bits_up(count)):
        order = order + [place ^ bit for place in order]
    return order


def scatter_first(near, far, axis, count):
    came = lax.ppermute(far, axis, xor_perm(count, 1))
    half = near.shape[0] // 2
    sent = (near[half:].astype(F32) + came[half:].astype(F32)).astype(BF16)
    sent, near, came = together(sent, near, came)
    return sent, near[:half].astype(F32) + came[:half].astype(F32)


def scatter_rest(sent, held, axis, count):
    for bit in bits_up(count)[1:]:
        held = held + lax.ppermute(sent, axis, xor_perm(count, bit)).astype(F32)
        half = held.shape[0] // 2
        sent, held = held[half:].astype(BF16), held[: max(half, 1)]
    return held[0]


def scatter_sum(near, far, axis, count):
    return scatter_rest(*scatter_first(near, far, axis, count), axis, count)


def attend_kernel(piece, facts_ref, q_ref, k_ref, v_ref, out_ref, prob_ref):
    step = pl.program_id(1)
    keys_len, lanes = k_ref.shape[-1], q_ref.shape[-1]
    pieces_key, pieces_query = keys_len // piece, lanes // piece
    values = v_ref[0]

    def finish(scores):
        top = jnp.max(scores, axis=0, keepdims=True)
        exponent = jnp.exp2(scores * (FACTOR * LOG2E) - top * (FACTOR * LOG2E))
        total = jnp.sum(exponent, axis=0, keepdims=True)
        prob = (exponent * (1.0 / total)).astype(BF16)
        prob_ref[0] = prob
        out_ref[0] = dot(values, prob).astype(BF16)

    scores = dot(k_ref[0], q_ref[0], 0, 0)

    @pl.when(facts_ref[0] == 1)
    def _():
        finish(scores)

    @pl.when(facts_ref[0] != 1)
    def _():
        seg_key = jnp.concatenate(
            [jnp.full((piece, 1), facts_ref[1 + at], jnp.int32) for at in range(pieces_key)], axis=0
        )
        base = 1 + pieces_key + step * pieces_query
        seg_query = jnp.concatenate(
            [jnp.full((1, piece), facts_ref[base + at], jnp.int32) for at in range(pieces_query)],
            axis=1,
        )
        finish(jnp.where(seg_key == seg_query, scores, NEGATIVE))


def attend(queries, keys, values, facts, piece):
    heads, depth, count = queries.shape
    keys_len = keys.shape[2]
    lanes = min(count, (1 << 20) // keys_len)
    chunk = lambda head, step, facts: (head, 0, step)
    whole = lambda head, step, facts: (head, 0, 0)
    return pl.pallas_call(
        functools.partial(attend_kernel, piece),
        grid_spec=pltpu.PrefetchScalarGridSpec(
            num_scalar_prefetch=1,
            grid=(heads, count // lanes),
            in_specs=[
                pl.BlockSpec((1, depth, lanes), chunk),
                pl.BlockSpec((1, depth, keys_len), whole),
                pl.BlockSpec((1, depth, keys_len), whole),
            ],
            out_specs=[
                pl.BlockSpec((1, depth, lanes), chunk),
                pl.BlockSpec((1, keys_len, lanes), chunk),
            ],
        ),
        out_shape=[
            jax.ShapeDtypeStruct((heads, depth, count), BF16),
            jax.ShapeDtypeStruct((heads, keys_len, count), BF16),
        ],
        compiler_params=pltpu.CompilerParams(vmem_limit_bytes=VMEM_LIMIT),
        cost_estimate=pl.CostEstimate(
            flops=30 * count * keys_len * heads * 128,
            bytes_accessed=2 * heads * count * keys_len,
            transcendentals=heads * count * keys_len,
        ),
        name="attend",
    )(facts, queries, keys, values)


def attend_back_kernel(
    q_ref, k_ref, v_ref, out_ref, grad_ref, prob_ref, dq_ref, dk_ref, dv_ref, dk_sum, dv_sum
):
    step = pl.program_id(1)
    grad = grad_ref[0]
    prob = prob_ref[0]
    delta = jnp.sum(grad.astype(F32) * out_ref[0].astype(F32), axis=0, keepdims=True)
    grad_prob = dot(v_ref[0], grad, 0, 0)
    grad_score = (prob.astype(F32) * (grad_prob - delta)).astype(BF16)
    dq_ref[0] = (dot(k_ref[0], grad_score) * FACTOR).astype(BF16)
    dk_part = dot(grad_score, q_ref[0], 1, 1)
    dv_part = dot(prob, grad, 1, 1)

    @pl.when(step == 0)
    def _():
        dk_sum[...] = dk_part
        dv_sum[...] = dv_part

    @pl.when(step != 0)
    def _():
        dk_sum[...] += dk_part
        dv_sum[...] += dv_part

    @pl.when(step == pl.num_programs(1) - 1)
    def _():
        dk_ref[0] = jnp.transpose(dk_sum[...] * FACTOR).astype(BF16)
        dv_ref[0] = jnp.transpose(dv_sum[...]).astype(BF16)


def attend_back(queries, keys, values, attended, grad, prob):
    heads, depth, count = queries.shape
    keys_len = keys.shape[2]
    lanes = min(count, (1 << 20) // keys_len)
    chunk = lambda head, step: (head, 0, step)
    whole = lambda head, step: (head, 0, 0)
    return pl.pallas_call(
        attend_back_kernel,
        grid=(heads, count // lanes),
        in_specs=[
            pl.BlockSpec((1, depth, lanes), chunk),
            pl.BlockSpec((1, depth, keys_len), whole),
            pl.BlockSpec((1, depth, keys_len), whole),
            pl.BlockSpec((1, depth, lanes), chunk),
            pl.BlockSpec((1, depth, lanes), chunk),
            pl.BlockSpec((1, keys_len, lanes), chunk),
        ],
        out_specs=[
            pl.BlockSpec((1, depth, lanes), chunk),
            pl.BlockSpec((1, depth, keys_len), whole),
            pl.BlockSpec((1, depth, keys_len), whole),
        ],
        out_shape=[
            jax.ShapeDtypeStruct((heads, depth, count), BF16),
            jax.ShapeDtypeStruct((heads, depth, keys_len), BF16),
            jax.ShapeDtypeStruct((heads, depth, keys_len), BF16),
        ],
        scratch_shapes=[pltpu.VMEM((keys_len, depth), F32), pltpu.VMEM((keys_len, depth), F32)],
        compiler_params=pltpu.CompilerParams(vmem_limit_bytes=VMEM_LIMIT),
        cost_estimate=pl.CostEstimate(
            flops=30 * count * keys_len * heads * 128,
            bytes_accessed=2 * heads * count * keys_len,
            transcendentals=0,
        ),
        name="attend_back",
    )(queries, keys, values, attended, grad, prob)


def gelu_pair(inputs):
    square = inputs * inputs
    tanh = jnp.tanh(GELU_COEF * (inputs + 0.044715 * inputs * square))
    value = 0.5 * inputs * (1.0 + tanh)
    slope = 0.5 * (1.0 + tanh) + 0.5 * inputs * (1.0 - tanh * tanh) * (
        GELU_COEF * (1.0 + 3.0 * 0.044715 * square)
    )
    return value, slope


def layer_norm(inputs):
    average = jnp.mean(inputs, axis=-1, keepdims=True)
    centred = inputs - average
    spread = jnp.mean(centred * centred, axis=-1, keepdims=True)
    scale = lax.rsqrt(spread + EPSILON)
    return centred * scale, scale


def layer_norm_back(grad, norm, scale):
    first = jnp.mean(grad, axis=-1, keepdims=True)
    second = jnp.mean(grad * norm, axis=-1, keepdims=True)
    return (grad - first - norm * second) * scale


def shards(
    tokens,
    cotangent,
    lengths,
    cond_index,
    cond_table,
    w_mod,
    b_mod,
    w_qkv,
    b_query,
    b_value,
    w_out,
    b_out,
    w_up,
    b_up,
    w_down,
    b_down,
):
    rows_dev, piece, width = tokens.shape
    dp, band = lax.axis_size("dp"), lax.axis_size("band")
    me, group = lax.axis_index("dp"), lax.axis_index("band")
    images = lengths.shape[1]
    rows = rows_dev * dp
    spans = band // rows
    assert band % rows == 0
    across = band // dp
    unit = width // band
    heads = H // dp
    head_width = width // dp
    mod_width = w_mod.shape[1]
    hidden_width = w_up.shape[1]
    both = ("dp", "band")
    me_turned = reverse_bits(me, dp)

    def target(d, b, turn):
        local = ((b >> log2(dp)) & (rows_dev - 1)) ^ turn
        to_group = (rows_dev * reverse_bits(d, dp) + local) * spans + b // rows
        return reverse_bits(b % dp, dp) * band + to_group

    outward = [
        [(d * band + b, target(d, b, turn)) for d in range(dp) for b in range(band)]
        for turn in range(rows_dev)
    ]
    inward = [[(there, here) for here, there in pairs] for pairs in outward]
    my_slot = (group >> log2(dp)) & (rows_dev - 1)

    def to_groups(local):
        return jnp.stack(
            [
                lax.ppermute(pick(local, my_slot ^ turn), both, outward[turn])
                for turn in range(rows_dev)
            ]
        )

    def from_groups(held):
        came = jnp.stack(
            [lax.ppermute(held[turn], both, inward[turn]) for turn in range(rows_dev)]
        )
        return xor_shuffle(came, my_slot)

    group_row = group >> log2(spans)
    my_local = group_row & (rows_dev - 1)
    order = mask_order(dp)
    places = jnp.arange(dp, dtype=jnp.int32)[:, None]
    turns = jnp.arange(rows_dev, dtype=jnp.int32)[None]
    piece_first = piece * (
        (group & (spans - 1)) * rows + ((my_local ^ turns) * dp) + (me_turned ^ places)
    )

    facts = jnp.concatenate([lengths, cond_index], axis=1)
    facts_own = lax.ppermute(pick(facts, my_slot), both, outward[0])
    tokens_sent = [pick(tokens, my_slot ^ turn) for turn in range(rows_dev)]
    slot_to = [[(3 * d + slot) % dp for d in range(dp)] for slot in range(3)]
    w_qkv, tokens_sent = together(w_qkv, tokens_sent)
    tokens_own = jnp.stack(
        [lax.ppermute(part, both, outward[turn]) for turn, part in enumerate(tokens_sent)]
    )
    w_slots = [w_qkv.T[slot * head_width : (slot + 1) * head_width] for slot in range(3)]
    stay = [[d == to for d, to in enumerate(target)] for target in slot_to]
    if all(first != last for first, last in zip(stay[0], stay[2], strict=True)):
        keeps_first = functools.reduce(
            jnp.logical_or, [me == d for d in range(dp) if stay[0][d]]
        )
        slots_sent = jnp.where(keeps_first, w_slots[2], w_slots[0])
        came = lax.ppermute(
            slots_sent,
            "dp",
            [(d, slot_to[2 if stay[0][d] else 0][d]) for d in range(dp)],
        )
        w_slots = [
            jnp.where(keeps_first, w_slots[0], came),
            lax.ppermute(w_slots[1], "dp", list(enumerate(slot_to[1]))),
            jnp.where(keeps_first, came, w_slots[2]),
        ]
    else:
        slots_sent = w_slots[0]
        w_slots = [
            lax.ppermute(w_slots[slot], "dp", list(enumerate(slot_to[slot]))) for slot in range(3)
        ]
    image_ends, index_own = jnp.cumsum(facts_own[:images]), facts_own[images:]
    classes = jnp.arange(cond_table.shape[0], dtype=jnp.int32)

    def conditions(index):
        return dot((index[:, None] == classes[None]).astype(BF16), cond_table)

    silu_own = jax.nn.silu(conditions(index_own)).astype(BF16)
    mod_part = dot(silu_own, w_mod) + cut(b_mod, me * mod_width, mod_width)
    w_out, w_down, mod_part = together(w_out, w_down, mod_part)
    modulation = gather_stack(mod_part, "dp", dp)
    row_blocks = jnp.concatenate(
        [jnp.stack(jnp.split(member.T, dp, axis=1)) for member in (w_down, w_out)], axis=2
    )
    tokens_own, w_slots, modulation, row_blocks, cotangent = together(
        tokens_own, w_slots, modulation, row_blocks, cotangent
    )
    modulation = xor_shuffle(modulation, me)
    seg_all = jnp.sum(
        (image_ends[None, None] <= piece_first[..., None]).astype(jnp.int32), axis=-1
    ).reshape(-1)
    image_ids = jnp.arange(images, dtype=jnp.int32)
    hot_all = seg_all[:, None] == image_ids[None]
    modulation = jnp.transpose(modulation, (1, 0, 2)).reshape(images, 6 * width)
    mod_all = jnp.dot(hot_all.astype(F32), modulation, precision=HIGHEST)
    mod_all = [part[:, None] for part in jnp.split(mod_all, 6, axis=1)]
    shift_a_all, scale_a_all, gate_b_all = [mod_all[at] for at in (0, 1, 5)]
    scale_a, gate_a, shift_b, scale_b, gate_b = [
        mod_all[at][:rows_dev] for at in (1, 2, 3, 4, 5)
    ]
    own_hot = hot_all[:rows_dev]

    def gather_tokens(own, *waits):
        return gather_parts(own, "dp", dp, *waits).reshape((-1,) + own.shape[1:])

    tokens_all = gather_tokens(tokens_own)
    row_parts = {
        mask: lax.ppermute(pick(row_blocks, me ^ mask), "dp", xor_perm(dp, mask))
        for mask in range(2, dp)
    }
    slot_of = [lax.rem(me + kind * (dp % 3), 3) for kind in range(3)]
    w_heads = jnp.concatenate(
        [
            jnp.where(
                slot_of[kind] == 0,
                w_slots[0],
                jnp.where(slot_of[kind] == 1, w_slots[1], w_slots[2]),
            )
            for kind in range(3)
        ]
    )
    bias_heads = jnp.concatenate(
        [
            cut(b_query, me * head_width, head_width),
            jnp.zeros((head_width,), F32),
            cut(b_value, me * head_width, head_width),
        ]
    )
    norm_all = layer_norm(tokens_all.astype(F32))[0]
    hidden_a_all = (norm_all * (1.0 + scale_a_all) + shift_a_all).astype(BF16).reshape(-1, width)
    norm_low = norm_all.astype(BF16).reshape(-1, width)
    cotangent_own = to_groups(cotangent)
    count = hidden_a_all.shape[0]
    half = count // 2
    projected = (dot(w_heads, hidden_a_all, 1, 1) + bias_heads[:, None]).astype(BF16)
    projected, row_blocks = together(projected, row_blocks)
    projected = projected.reshape(3, heads, HD, count)
    queries, keys, values = projected[0], projected[1], projected[2]
    seg_row = seg_all
    if spans > 1:
        mates = [[at * spans + span for span in range(spans)] for at in range(rows)]
        keys, values, seg_row = [
            lax.all_gather(
                member, "band", axis=member.ndim - 1, tiled=True, axis_index_groups=mates
            )
            for member in (keys, values, seg_row)
        ]
    one_image = jnp.all(seg_row == seg_row[0]).astype(jnp.int32)
    attend_facts = jnp.concatenate([one_image[None], seg_row, seg_all])
    attended, prob_low = attend(queries, keys, values, attend_facts, piece)
    row_parts[0] = pick(row_blocks, me)
    row_parts[1] = lax.ppermute(pick(row_blocks, me ^ 1), "dp", xor_perm(dp, 1))
    attended, cotangent_own, row_parts = together(attended, cotangent_own, row_parts)
    attended = attended.reshape(head_width, count)
    row_parts = jnp.stack([row_parts[mask] for mask in range(dp)])
    w_out_rows = jnp.concatenate(list(xor_shuffle(row_parts[:, :, hidden_width:], me)))

    def split_own(partial):
        return partial.astype(BF16).reshape(dp // 2, rows_dev, piece, width)

    def products(product, left):
        return split_own(product(left(half, count))), split_own(product(left(0, half)))

    far_half, near_half = products(
        lambda part: dot(part, w_out_rows, 0, 1), lambda low, high: attended[:, low:high]
    )
    far_half, row_parts = together(far_half, row_parts)
    branch = scatter_sum(near_half, far_half, "dp", dp) + b_out
    middle = tokens_own.astype(F32) + gate_a * branch
    norm_b, spread_b = layer_norm(middle)
    hidden_b = (norm_b * (1.0 + scale_b) + shift_b).astype(BF16)
    w_down_rows = jnp.concatenate(list(xor_shuffle(row_parts[:, :, :hidden_width], me)))
    hidden_b, w_down_rows = together(hidden_b, w_down_rows)
    hidden_b_all = gather_tokens(hidden_b).reshape(count, width)

    cotangent_own, hidden_b_all = together(cotangent_own, hidden_b_all)
    cotangent_all = gather_tokens(cotangent_own)
    grad_output = cotangent_own.astype(F32)
    b_up_own = cut(b_up, me * hidden_width, hidden_width)
    pre_act = dot(hidden_b_all, w_up) + b_up_own
    value, slope = gelu_pair(pre_act)
    activated, slope = lax.optimization_barrier((value.astype(BF16), slope.astype(BF16)))
    far_mlp, near_mlp = products(
        lambda part: dot(part, w_down_rows, 1, 1), lambda low, high: activated[low:high]
    )
    mlp_sent, mlp_held = scatter_first(near_mlp, far_mlp, "dp", dp)
    cotangent_all, mlp_sent = together(cotangent_all, mlp_sent)
    grad_mlp_all = (gate_b_all * cotangent_all.astype(F32)).astype(BF16).reshape(count, width)
    mlp_out = scatter_rest(mlp_sent, mlp_held, "dp", dp) + b_down
    grad_act = dot(grad_mlp_all, w_down_rows)
    grad_pre = (grad_act * slope.astype(F32)).astype(BF16)
    far_half, near_half = products(
        lambda part: dot(part, w_up, 1, 1), lambda low, high: grad_pre[low:high]
    )
    sent, grad_hidden_b = scatter_first(near_half, far_half, "dp", dp)
    mlp_out, sent, grad_pre, activated = together(mlp_out, sent, grad_pre, activated)
    grad_hidden_b = scatter_rest(sent, grad_hidden_b, "dp", dp)
    stages = log2(band)
    near_first = list(range(stages))

    def halves(held, axis):
        size = held.shape[axis] // 2
        return [lax.slice_in_dim(held, at * size, (at + 1) * size, axis=axis) for at in range(2)]

    def choose(held, axis, bit, plain=False):
        upper = (group >> bit) & 1
        if bit >= log2(across) and not plain:
            upper = upper ^ ((me >> (bit - log2(across))) & 1)
        upper = upper == 1
        first, second = halves(held, axis)
        return jnp.where(upper, second, first), jnp.where(upper, first, second)

    def send(part, bit):
        return lax.ppermute(part, "band", xor_perm(band, 1 << bit))

    def joined(mine, came):
        return (mine.astype(F32) + came.astype(F32)).astype(BF16)

    def sum_groups(term, axes, bits, plain=False):
        held = term
        for axis, bit in zip(axes, bits, strict=True):
            mine, far = choose(held, axis, bit, plain)
            held = joined(mine, send(far, bit))
        return held

    def piece_at(d, b):
        return reverse_bits((b // across) ^ d, dp), reverse_bits(b % across, across)

    def owner_pairs(owner):
        return [
            (d * band + b, owner(d, b, *piece_at(d, b))) for d in range(dp) for b in range(band)
        ]

    near_bits, far_bits = near_first[: log2(across)], near_first[log2(across) :]
    first_far = far_bits[0]
    grad_w_up = dot(hidden_b_all, grad_pre, 0, 0).astype(BF16)
    grad_w_down = dot(grad_mlp_all, activated, 0, 0).astype(BF16)
    up_mine, up_far = choose(grad_w_up, 1, near_bits[0])
    down_mine, down_far = choose(grad_w_down, 0, first_far)
    up_far, down_far = halves(up_far, 0), halves(down_far, 0)
    up_came = [send(up_far[0], near_bits[0])]
    down_came = [send(down_far[0], first_far)]
    up_came, up_far = together(up_came, up_far[1])
    down_came, down_far = together(down_came, down_far[1])
    up_came.append(send(up_far, near_bits[0]))
    down_came.append(send(down_far, first_far))

    grad_middle = grad_output + layer_norm_back(grad_hidden_b * (1.0 + scale_b), norm_b, spread_b)
    grad_branch = (gate_a * grad_middle).astype(BF16)
    middle, mlp_out, grad_branch = together(middle, mlp_out, grad_branch)
    grad_branch_all = gather_tokens(grad_branch).reshape(count, width)
    output = (middle + gate_b * mlp_out).astype(BF16)
    output, grad_branch_all = together(output, grad_branch_all)
    output_came = [
        lax.ppermute(output[turn], both, inward[turn]) for turn in range(rows_dev)
    ]
    up_mine, up_far = choose(joined(up_mine, jnp.concatenate(up_came)), 0, first_far)
    down_mine, down_far = choose(joined(down_mine, jnp.concatenate(down_came)), 1, near_bits[0])
    up_came, down_came = send(up_far, first_far), send(down_far, near_bits[0])
    grad_attended = dot(w_out_rows, grad_branch_all, 0, 1).astype(BF16)
    grad_q, grad_k, grad_v = attend_back(
        queries,
        keys,
        values,
        attended.reshape(heads, HD, count),
        grad_attended.reshape(heads, HD, count),
        prob_low,
    )
    if spans > 1:
        grad_k, grad_v = [
            lax.psum_scatter(
                member, "band", scatter_dimension=2, tiled=True, axis_index_groups=mates
            )
            for member in (grad_k, grad_v)
        ]
    grad_heads = jnp.concatenate(
        [member.reshape(head_width, count) for member in (grad_q, grad_k, grad_v)]
    )
    grad_heads, up_came, down_came = together(grad_heads, up_came, down_came)
    far_half, near_half = products(
        lambda part: dot(part, w_heads, 0, 0), lambda low, high: grad_heads[:, low:high]
    )
    sent, grad_hidden_a = scatter_first(near_half, far_half, "dp", dp)
    attended, grad_heads, near_half, far_half, sent, up_came, down_came, output_came = together(
        attended, grad_heads, near_half, far_half, sent, up_came, down_came, output_came
    )
    output = xor_shuffle(jnp.stack(output_came), my_slot)
    grad_hidden_a = scatter_rest(sent, grad_hidden_a, "dp", dp)
    up_down = jnp.stack([joined(up_mine, up_came), joined(down_mine, down_came)])
    up_down_rest = [2] * (len(near_bits) - 1) + [1] * (len(far_bits) - 1), near_bits[1:] + far_bits[1:]
    up_down_mine, up_down_far = choose(up_down, up_down_rest[0][0], up_down_rest[1][0])
    up_down_far, grad_heads, attended = together(up_down_far, grad_heads, attended)
    up_down_came = send(up_down_far, up_down_rest[1][0])
    grad_w_heads = dot(grad_heads, hidden_a_all).astype(BF16).reshape(3, across, unit, width)
    qkv_axes = [1] * log2(across) + [3] * log2(dp)
    qkv_mine, qkv_far = choose(grad_w_heads, qkv_axes[0], near_first[0])
    near_half, far_half, qkv_far, attended = together(near_half, far_half, qkv_far, attended)
    qkv_came = send(qkv_far, near_first[0])
    out_bits = [far_bits[0]] + near_bits + far_bits[1:]
    out_mine, out_far = choose(
        dot(grad_branch_all, attended, 0, 1)
        .astype(BF16)
        .reshape((2,) * stages + (unit, head_width)),
        stages - 1 - out_bits[0],
        out_bits[0],
        plain=True,
    )
    out_came = send(out_far, out_bits[0])

    hot_tokens = jnp.broadcast_to(
        hot_all.T.astype(BF16)[:, :, None], (images, hot_all.shape[0], piece)
    ).reshape(images, count)

    def image_sums(near, far):
        return dot(hot_tokens[:, :half], near) + dot(hot_tokens[:, half:], far)

    near_half, far_half = near_half.reshape(half, width), far_half.reshape(half, width)
    grad_shift_a = image_sums(near_half, far_half)
    grad_scale_a = image_sums(near_half * norm_low[:half], far_half * norm_low[half:])

    def own_sums(member):
        pieces = jnp.sum(member, axis=1)
        return jnp.sum(jnp.where(own_hot[:, :, None], pieces[:, None], 0.0), axis=0)

    grad_mod = jnp.concatenate(
        [
            grad_shift_a,
            grad_scale_a,
            own_sums(grad_middle * branch),
            own_sums(grad_hidden_b),
            own_sums(grad_hidden_b * norm_b),
            own_sums(grad_output * mlp_out),
        ],
        axis=1,
    )
    grad_mod = jnp.transpose(grad_mod.reshape(images, dp, mod_width), (1, 0, 2))
    grad_mod_came = lax.all_to_all(grad_mod, "dp", 0, 0, tiled=True)
    grad_mod_came, qkv_came = together(grad_mod_came, qkv_came)
    grad_mod_own = jnp.sum(grad_mod_came, axis=0)
    high = grad_mod_own.astype(BF16)
    low = (grad_mod_own - high.astype(F32)).astype(BF16)
    grad_silu = dot(jnp.concatenate([high, low], axis=0), w_mod, 1, 1)
    grad_silu = grad_silu[:images] + grad_silu[images:]
    ones = jnp.ones((8, count), BF16)
    bias_rows = [
        jnp.sum(grad_mlp_all[: rows_dev * piece].astype(F32), axis=0),
        jnp.sum(grad_branch.astype(F32), axis=(0, 1)),
        dot(ones, grad_pre)[0],
        dot(ones, grad_heads, 1, 1)[0],
    ]
    assert images >= len(bias_rows)
    bias_rows = [
        jnp.pad(member, (0, width + 128 - member.shape[0])) for member in bias_rows
    ] + [jnp.zeros((width + 128,), F32)] * (images - len(bias_rows))
    bias_rows = jnp.stack(bias_rows) + jnp.pad(
        index_own.astype(F32)[:, None], ((0, 0), (width, 127))
    )
    packed = jnp.concatenate([grad_mod_own, grad_silu, bias_rows], axis=1)
    grad_hidden_a, packed = together(grad_hidden_a, packed)
    qkv_mine, qkv_far = choose(joined(qkv_mine, qkv_came), qkv_axes[1], near_first[1])
    inputs = tokens_own.astype(F32)
    norm_a, spread_a = layer_norm(inputs)
    grad_tokens = grad_middle + layer_norm_back(grad_hidden_a * (1.0 + scale_a), norm_a, spread_a)
    grad_tokens = grad_tokens.astype(BF16)
    packed, grad_tokens = together(packed, grad_tokens)
    held, masks = packed[None], [0]
    for bit in far_bits + near_bits:
        if bit == near_bits[0]:
            held, grad_tokens, qkv_far, out_came = together(held, grad_tokens, qkv_far, out_came)
        held = jnp.concatenate([held, lax.ppermute(held, "band", xor_perm(band, 1 << bit))])
        masks = masks + [mask ^ (1 << bit) for mask in masks]
    packed = xor_shuffle(jnp.stack([held[masks.index(mask)] for mask in range(band)]), group)
    grad_tokens_came = [
        lax.ppermute(grad_tokens[turn], both, inward[turn]) for turn in range(rows_dev)
    ]
    qkv_came = send(qkv_far, near_first[1])
    out_mine, out_far = choose(
        joined(out_mine, out_came), stages - 1 - out_bits[1], out_bits[1], plain=True
    )
    out_came = send(out_far, out_bits[1])
    packed, qkv_came, up_down_came, out_came, grad_tokens_came = together(
        packed, qkv_came, up_down_came, out_came, grad_tokens_came
    )
    up_down = sum_groups(
        joined(up_down_mine, up_down_came), up_down_rest[0][1:], up_down_rest[1][1:]
    )
    grad_tokens = xor_shuffle(jnp.stack(grad_tokens_came), my_slot)
    grad_mod_groups = packed[:, :, :mod_width].reshape(band * images, mod_width)
    grad_silu_groups = packed[:, :, mod_width : mod_width + width]
    grad_silu_groups = grad_silu_groups.reshape(rows, spans, images, width).sum(1)
    mod_sum = jnp.sum(grad_mod_groups, axis=0)
    mod_rows = -(-mod_width // width)
    mod_sum = jnp.pad(mod_sum, (0, mod_rows * width - mod_width)).reshape(mod_rows, width)
    final_pack = jnp.concatenate(
        [
            grad_silu_groups.reshape(rows * images, width),
            jnp.sum(packed[:, :, mod_width + width : mod_width + 2 * width], axis=0),
            mod_sum,
        ]
    )
    qkv_sum = sum_groups(joined(qkv_mine, qkv_came), qkv_axes[2:], near_first[2:])
    qkv_sum = qkv_sum.reshape(3, unit, head_width)
    out_sum = sum_groups(
        joined(out_mine, out_came),
        [stages - 1 - bit for bit in out_bits[2:]],
        out_bits[2:],
        plain=True,
    )
    final_out = out_sum.reshape(unit, head_width).T.astype(F32)
    final_pack = gather_all(final_pack, "dp", dp)
    up_down = lax.ppermute(up_down, both, owner_pairs(lambda d, b, block, unit: block * band + b))
    up_down, qkv_sum = together(up_down, qkv_sum)
    up_down = lax.ppermute(
        up_down,
        both,
        [
            (d * band + b, d * band + ((b // across) ^ reverse_bits(d, dp)) * across + reverse_bits(b % across, across))
            for d in range(dp)
            for b in range(band)
        ],
    )
    final_up, final_down = up_down[0].astype(F32), up_down[1].T.astype(F32)

    kind_of = [
        [next(kind for kind in range(3) if (kind * dp + d) % 3 == slot) for slot in range(3)]
        for d in range(dp)
    ]
    kind_now = [
        sum(
            jnp.where(slot_of[kind] == slot, kind, 0).astype(jnp.int32) for kind in range(3)
        )
        for slot in range(3)
    ]
    my_unit = reverse_bits(group & (across - 1), across)
    final_qkv = []
    for turn in range(3):
        slots = []
        for at in range(across):
            options = {
                slot
                for d in range(dp)
                for slot in range(3)
                if (band * kind_of[d][slot] + across * d + at) % 3 == turn
            }
            assert len(options) == 1
            slots.append(options.pop())

        def owner(d, b, block, at, slots=slots, turn=turn):
            start = band * kind_of[d][slots[at]] + across * d + at
            assert start % 3 == turn
            return block * band + start // 3

        kind = sum(
            jnp.where(my_unit == at, kind_now[slots[at]], 0).astype(jnp.int32)
            for at in range(across)
        )
        final_qkv.append(
            lax.ppermute(pick(qkv_sum, kind), both, owner_pairs(owner))
        )
    final_qkv = jnp.concatenate(final_qkv).T.astype(F32)

    index_all = packed[::spans, :, mod_width + 2 * width].reshape(-1).astype(jnp.int32)
    condition = conditions(index_all)
    silu_all = jax.nn.silu(condition).astype(BF16)
    silu_rows = rows * images
    grad_silu_rows = jnp.sum(final_pack[:, :silu_rows], axis=0)
    bias_all = final_pack[:, silu_rows : silu_rows + images]
    final_b_down = jnp.sum(bias_all[:, 0], axis=0)
    final_b_out = jnp.sum(bias_all[:, 1], axis=0)
    final_b_up = bias_all[:, 2, :hidden_width].reshape(-1)
    final_b_query = bias_all[:, 3, :head_width].reshape(-1)
    final_b_value = bias_all[:, 3, 2 * head_width : 3 * head_width].reshape(-1)
    final_b_mod = final_pack[:, silu_rows + images :].reshape(dp, -1)[:, :mod_width].reshape(-1)
    sigmoid = jax.nn.sigmoid(condition)
    grad_condition = grad_silu_rows * (sigmoid * (1.0 + condition * (1.0 - sigmoid)))
    table_hot = (
        classes[:, None] == index_all[None]
    ).astype(F32)
    final_table = jnp.dot(table_hot, grad_condition, precision=HIGHEST)
    mod_share = mod_width // across
    grad_mod_share = lax.ppermute(
        cut(grad_mod_groups, my_unit * mod_share, mod_share, 1),
        both,
        owner_pairs(lambda d, b, block, at: block * band + across * d + at),
    )
    silu_share = cut(silu_all, me * head_width, head_width, 1).astype(F32)
    silu_share = jnp.repeat(silu_share.reshape(rows, images, -1), spans, axis=0)
    final_mod = lax.dot_general(
        silu_share.reshape(band * images, -1),
        grad_mod_share,
        (((0,), (0,)), ((), ())),
        precision=HIGHEST,
        preferred_element_type=F32,
    )
    return (
        output,
        grad_tokens,
        final_table,
        final_mod,
        final_qkv,
        final_out,
        final_up,
        final_down,
        final_b_mod,
        final_b_query,
        final_b_value,
        final_b_out,
        final_b_up,
        final_b_down,
    )


def solution(mesh):
    rows = P("dp", "band", None)
    split = P(None, "dp")
    spread = P("dp", "band")
    return jax.shard_map(
        shards,
        mesh=mesh,
        in_specs=(
            rows,
            rows,
            P("dp", None),
            P("dp", None),
            P(),
            split,
            P(),
            split,
            P(),
            P(),
            split,
            P(),
            split,
            P(),
            split,
            P(),
        ),
        out_specs=(
            rows,
            rows,
            P(),
            spread,
            spread,
            spread,
            spread,
            P("band", "dp"),
            P(),
            P(),
            P(),
            P(),
            P(),
            P(),
        ),
        check_vma=False,
    )
```

```python
import functools
import math

import jax
import jax.numpy as jnp
from jax import lax
from jax.experimental import pallas as pl
from jax.experimental.pallas import tpu as pltpu
from jax.sharding import PartitionSpec as P

H = 16
HD = 72

EPSILON = 1e-06
HIGHEST = lax.Precision.HIGHEST
NEGATIVE = -1e30
GELU_COEF = 0.7978845608028654
FACTOR = 1.0 / math.sqrt(HD)
LOG2E = math.log2(math.e)
VMEM_LIMIT = 56 * 1024 * 1024
F32 = jnp.float32
BF16 = jnp.bfloat16


def dot(left, right, left_dim=1, right_dim=0):
    return lax.dot_general(
        left, right, (((left_dim,), (right_dim,)), ((), ())), preferred_element_type=F32
    )


def log2(count):
    assert count & (count - 1) == 0
    return count.bit_length() - 1


def reverse_bits(value, count):
    width = log2(count)
    return sum(((value >> at) & 1) << (width - 1 - at) for at in range(width)) if width else 0


def bits_up(count):
    return [1 << place for place in range(log2(count))]


def xor_perm(count, mask):
    return [(place, place ^ mask) for place in range(count)]


def pick(stack, place, axis=0):
    return lax.dynamic_index_in_dim(
        stack, place, axis, keepdims=False, allow_negative_indices=False
    )


def cut(array, start, size, axis=0):
    return lax.dynamic_slice_in_dim(array, start, size, axis, allow_negative_indices=False)


def xor_shuffle(array, mask):
    return jnp.stack([pick(array, mask ^ place) for place in range(array.shape[0])])


def together(*arrays):
    return lax.optimization_barrier(arrays)


def gather_most(part, axis, count):
    held = part[None]
    for bit in reversed(bits_up(count)[1:]):
        held = jnp.concatenate([held, lax.ppermute(held, axis, xor_perm(count, bit))])
    return held


def gather_parts(part, axis, count):
    held = gather_most(part, axis, count)
    return jnp.concatenate([held, lax.ppermute(held, axis, xor_perm(count, 1))])


def gather_stack(part, axis, count):
    held = gather_parts(part, axis, count)
    return jnp.stack([held[reverse_bits(mask, count)] for mask in range(count)])


def gather_all(part, axis, count):
    return xor_shuffle(gather_stack(part, axis, count), lax.axis_index(axis))


def mask_order(count):
    order = [0]
    for bit in reversed(bits_up(count)):
        order = order + [place ^ bit for place in order]
    return order


def scatter_first(near, far, axis, count):
    came = lax.ppermute(far, axis, xor_perm(count, 1))
    half = near.shape[0] // 2
    sent = (near[half:].astype(F32) + came[half:].astype(F32)).astype(BF16)
    sent, near, came = together(sent, near, came)
    return sent, near[:half].astype(F32) + came[:half].astype(F32)


def scatter_rest(sent, held, axis, count):
    for bit in bits_up(count)[1:]:
        held = held + lax.ppermute(sent, axis, xor_perm(count, bit)).astype(F32)
        half = held.shape[0] // 2
        sent, held = held[half:].astype(BF16), held[: max(half, 1)]
    return held[0]


def scatter_sum(near, far, axis, count):
    return scatter_rest(*scatter_first(near, far, axis, count), axis, count)


def project_kernel(
    halves, piece, near_ref, far_ref, scale_ref, shift_ref, weight_ref, bias_ref, out_ref, hidden_ref, norm_ref
):
    def write(tokens):
        inputs = tokens.astype(F32)
        average = jnp.mean(inputs, axis=-1, keepdims=True)
        centred = inputs - average
        spread = jnp.mean(centred * centred, axis=-1, keepdims=True)
        norm = centred * lax.rsqrt(spread + EPSILON)
        norm_ref[...] = norm.astype(BF16)
        for at in range(tokens.shape[0] // piece):
            rows = slice(at * piece, (at + 1) * piece)
            hidden = norm[rows] * (1.0 + scale_ref[at]) + shift_ref[at]
            hidden_ref[rows] = hidden.astype(BF16)
        out_ref[...] = (
            dot(weight_ref[...], hidden_ref[...], 1, 1) + bias_ref[...]
        ).astype(BF16)

    step = pl.program_id(0)

    @pl.when(step < halves)
    def _():
        write(near_ref[...])

    @pl.when(step >= halves)
    def _():
        write(far_ref[...])


def norm_project(near, far, scale, shift, weight, bias, piece):
    half, width = near.shape
    columns = weight.shape[0]
    rows = min(2 * piece, half)
    halves = half // rows
    scales = pl.BlockSpec((rows // piece, 1, width), lambda step: (step, 0, 0))
    block = pl.BlockSpec((rows, width), lambda step: (step, 0))
    shape = jax.ShapeDtypeStruct((2 * half, width), BF16)
    return pl.pallas_call(
        functools.partial(project_kernel, halves, piece),
        grid=(2 * halves,),
        in_specs=[
            pl.BlockSpec((rows, width), lambda step: (jnp.minimum(step, halves - 1), 0)),
            pl.BlockSpec((rows, width), lambda step: (jnp.maximum(step - halves, 0), 0)),
            scales,
            scales,
            pl.BlockSpec((columns, width), lambda step: (0, 0)),
            pl.BlockSpec((columns, 1), lambda step: (0, 0)),
        ],
        out_specs=[pl.BlockSpec((columns, rows), lambda step: (0, step)), block, block],
        out_shape=[jax.ShapeDtypeStruct((columns, 2 * half), BF16), shape, shape],
        compiler_params=pltpu.CompilerParams(vmem_limit_bytes=VMEM_LIMIT),
        cost_estimate=pl.CostEstimate(
            flops=4 * columns * half * width, bytes_accessed=12 * half * width, transcendentals=0
        ),
        name="norm_project",
    )(near, far, scale, shift, weight, bias)


def attend_kernel(piece, facts_ref, q_ref, k_ref, v_ref, out_ref, prob_ref):
    step = pl.program_id(1)
    keys_len, lanes = k_ref.shape[-1], q_ref.shape[-1]
    pieces_key, pieces_query = keys_len // piece, lanes // piece
    values = v_ref[0, 0]

    def finish(scores):
        top = jnp.max(scores, axis=0, keepdims=True)
        exponent = jnp.exp2(scores * (FACTOR * LOG2E) - top * (FACTOR * LOG2E))
        total = jnp.sum(exponent, axis=0, keepdims=True)
        prob = (exponent * (1.0 / total)).astype(BF16)
        prob_ref[0] = prob
        out_ref[0] = dot(values, prob).astype(BF16)

    scores = dot(k_ref[0, 0], q_ref[0, 0], 0, 0)

    @pl.when(facts_ref[0] == 1)
    def _():
        finish(scores)

    @pl.when(facts_ref[0] != 1)
    def _():
        seg_key = jnp.concatenate(
            [jnp.full((piece, 1), facts_ref[1 + at], jnp.int32) for at in range(pieces_key)], axis=0
        )
        base = 1 + pieces_key + step * pieces_query
        seg_query = jnp.concatenate(
            [jnp.full((1, piece), facts_ref[base + at], jnp.int32) for at in range(pieces_query)],
            axis=1,
        )
        finish(jnp.where(seg_key == seg_query, scores, NEGATIVE))


def attend(queries, keys, values, facts, piece):
    _, heads, depth, count = queries[0].shape
    keys_len = keys[0].shape[3]
    lanes = min(count, (1 << 20) // keys_len)
    chunk = lambda head, step, facts: (head, 0, step)
    return pl.pallas_call(
        functools.partial(attend_kernel, piece),
        grid_spec=pltpu.PrefetchScalarGridSpec(
            num_scalar_prefetch=1,
            grid=(heads, count // lanes),
            in_specs=[
                pl.BlockSpec(
                    (1, 1, depth, lanes), lambda head, step, facts: (queries[1], head, 0, step)
                ),
                pl.BlockSpec((1, 1, depth, keys_len), lambda head, step, facts: (keys[1], head, 0, 0)),
                pl.BlockSpec(
                    (1, 1, depth, keys_len), lambda head, step, facts: (values[1], head, 0, 0)
                ),
            ],
            out_specs=[
                pl.BlockSpec((1, depth, lanes), chunk),
                pl.BlockSpec((1, keys_len, lanes), chunk),
            ],
        ),
        out_shape=[
            jax.ShapeDtypeStruct((heads, depth, count), BF16),
            jax.ShapeDtypeStruct((heads, keys_len, count), BF16),
        ],
        compiler_params=pltpu.CompilerParams(vmem_limit_bytes=VMEM_LIMIT),
        cost_estimate=pl.CostEstimate(
            flops=30 * count * keys_len * heads * 128,
            bytes_accessed=2 * heads * count * keys_len,
            transcendentals=heads * count * keys_len,
        ),
        name="attend",
    )(facts, queries[0], keys[0], values[0])


def attend_back_kernel(
    q_ref, k_ref, v_ref, out_ref, grad_ref, prob_ref, dq_ref, dk_ref, dv_ref, dk_sum, dv_sum
):
    step = pl.program_id(1)
    grad = grad_ref[0]
    prob = prob_ref[0]
    delta = jnp.sum(grad.astype(F32) * out_ref[0].astype(F32), axis=0, keepdims=True)
    grad_prob = dot(v_ref[0, 0], grad, 0, 0)
    grad_score = (prob.astype(F32) * (grad_prob - delta)).astype(BF16)
    dq_ref[0] = (dot(k_ref[0, 0], grad_score) * FACTOR).astype(BF16)
    dk_part = dot(grad_score, q_ref[0, 0], 1, 1)
    dv_part = dot(prob, grad, 1, 1)

    @pl.when(step == 0)
    def _():
        dk_sum[...] = dk_part
        dv_sum[...] = dv_part

    @pl.when(step != 0)
    def _():
        dk_sum[...] += dk_part
        dv_sum[...] += dv_part

    @pl.when(step == pl.num_programs(1) - 1)
    def _():
        dk_ref[0] = jnp.transpose(dk_sum[...] * FACTOR).astype(BF16)
        dv_ref[0] = jnp.transpose(dv_sum[...]).astype(BF16)


def attend_back(queries, keys, values, attended, grad, prob):
    _, heads, depth, count = queries[0].shape
    keys_len = keys[0].shape[3]
    lanes = min(count, (1 << 20) // keys_len)
    chunk = lambda head, step: (head, 0, step)
    whole = lambda head, step: (head, 0, 0)
    return pl.pallas_call(
        attend_back_kernel,
        grid=(heads, count // lanes),
        in_specs=[
            pl.BlockSpec((1, 1, depth, lanes), lambda head, step: (queries[1], head, 0, step)),
            pl.BlockSpec((1, 1, depth, keys_len), lambda head, step: (keys[1], head, 0, 0)),
            pl.BlockSpec((1, 1, depth, keys_len), lambda head, step: (values[1], head, 0, 0)),
            pl.BlockSpec((1, depth, lanes), chunk),
            pl.BlockSpec((1, depth, lanes), chunk),
            pl.BlockSpec((1, keys_len, lanes), chunk),
        ],
        out_specs=[
            pl.BlockSpec((1, depth, lanes), chunk),
            pl.BlockSpec((1, depth, keys_len), whole),
            pl.BlockSpec((1, depth, keys_len), whole),
        ],
        out_shape=[
            jax.ShapeDtypeStruct((heads, depth, count), BF16),
            jax.ShapeDtypeStruct((heads, depth, keys_len), BF16),
            jax.ShapeDtypeStruct((heads, depth, keys_len), BF16),
        ],
        scratch_shapes=[pltpu.VMEM((keys_len, depth), F32), pltpu.VMEM((keys_len, depth), F32)],
        compiler_params=pltpu.CompilerParams(vmem_limit_bytes=VMEM_LIMIT),
        cost_estimate=pl.CostEstimate(
            flops=30 * count * keys_len * heads * 128,
            bytes_accessed=2 * heads * count * keys_len,
            transcendentals=0,
        ),
        name="attend_back",
    )(queries[0], keys[0], values[0], attended, grad, prob)


def gelu_pair(inputs):
    square = inputs * inputs
    tanh = jnp.tanh(GELU_COEF * (inputs + 0.044715 * inputs * square))
    value = 0.5 * inputs * (1.0 + tanh)
    slope = 0.5 * (1.0 + tanh) + 0.5 * inputs * (1.0 - tanh * tanh) * (
        GELU_COEF * (1.0 + 3.0 * 0.044715 * square)
    )
    return value, slope


def layer_norm(inputs):
    average = jnp.mean(inputs, axis=-1, keepdims=True)
    centred = inputs - average
    spread = jnp.mean(centred * centred, axis=-1, keepdims=True)
    scale = lax.rsqrt(spread + EPSILON)
    return centred * scale, scale


def layer_norm_back(grad, norm, scale):
    first = jnp.mean(grad, axis=-1, keepdims=True)
    second = jnp.mean(grad * norm, axis=-1, keepdims=True)
    return (grad - first - norm * second) * scale


def shards(
    tokens,
    cotangent,
    lengths,
    cond_index,
    cond_table,
    w_mod,
    b_mod,
    w_qkv,
    b_query,
    b_value,
    w_out,
    b_out,
    w_up,
    b_up,
    w_down,
    b_down,
):
    rows_dev, piece, width = tokens.shape
    dp, band = lax.axis_size("dp"), lax.axis_size("band")
    me, group = lax.axis_index("dp"), lax.axis_index("band")
    images = lengths.shape[1]
    rows = rows_dev * dp
    spans = band // rows
    assert band % rows == 0
    across = band // dp
    unit = width // band
    heads = H // dp
    head_width = width // dp
    mod_width = w_mod.shape[1]
    hidden_width = w_up.shape[1]
    both = ("dp", "band")
    me_turned = reverse_bits(me, dp)

    def target(d, b, turn):
        local = ((b >> log2(dp)) & (rows_dev - 1)) ^ turn
        to_group = (rows_dev * reverse_bits(d, dp) + local) * spans + b // rows
        return reverse_bits(b % dp, dp) * band + to_group

    outward = [
        [(d * band + b, target(d, b, turn)) for d in range(dp) for b in range(band)]
        for turn in range(rows_dev)
    ]
    inward = [[(there, here) for here, there in pairs] for pairs in outward]
    my_slot = (group >> log2(dp)) & (rows_dev - 1)

    def to_groups(local):
        return jnp.stack(
            [
                lax.ppermute(pick(local, my_slot ^ turn), both, outward[turn])
                for turn in range(rows_dev)
            ]
        )

    def from_groups(held):
        came = jnp.stack(
            [lax.ppermute(held[turn], both, inward[turn]) for turn in range(rows_dev)]
        )
        return xor_shuffle(came, my_slot)

    group_row = group >> log2(spans)
    my_local = group_row & (rows_dev - 1)
    order = mask_order(dp)
    places = jnp.arange(dp, dtype=jnp.int32)[:, None]
    turns = jnp.arange(rows_dev, dtype=jnp.int32)[None]
    piece_first = piece * (
        (group & (spans - 1)) * rows + ((my_local ^ turns) * dp) + (me_turned ^ places)
    )

    facts = jnp.concatenate([lengths, cond_index], axis=1)
    facts_own = lax.ppermute(pick(facts, my_slot), both, outward[0])
    tokens_sent = [pick(tokens, my_slot ^ turn) for turn in range(rows_dev)]
    slot_to = [[(3 * d + slot) % dp for d in range(dp)] for slot in range(3)]
    w_qkv, tokens_sent = together(w_qkv, tokens_sent)
    tokens_own = jnp.stack(
        [lax.ppermute(part, both, outward[turn]) for turn, part in enumerate(tokens_sent)]
    )
    w_slots = [w_qkv.T[slot * head_width : (slot + 1) * head_width] for slot in range(3)]
    stay = [[d == to for d, to in enumerate(target)] for target in slot_to]
    if all(first != last for first, last in zip(stay[0], stay[2], strict=True)):
        keeps_first = functools.reduce(
            jnp.logical_or, [me == d for d in range(dp) if stay[0][d]]
        )
        slots_sent = jnp.where(keeps_first, w_slots[2], w_slots[0])
        came = lax.ppermute(
            slots_sent,
            "dp",
            [(d, slot_to[2 if stay[0][d] else 0][d]) for d in range(dp)],
        )
        w_slots = [
            jnp.where(keeps_first, w_slots[0], came),
            lax.ppermute(w_slots[1], "dp", list(enumerate(slot_to[1]))),
            jnp.where(keeps_first, came, w_slots[2]),
        ]
    else:
        slots_sent = w_slots[0]
        w_slots = [
            lax.ppermute(w_slots[slot], "dp", list(enumerate(slot_to[slot]))) for slot in range(3)
        ]
    image_ends, index_own = jnp.cumsum(facts_own[:images]), facts_own[images:]
    classes = jnp.arange(cond_table.shape[0], dtype=jnp.int32)

    def conditions(index):
        return dot((index[:, None] == classes[None]).astype(BF16), cond_table)

    silu_own = jax.nn.silu(conditions(index_own)).astype(BF16)
    mod_part = dot(silu_own, w_mod) + cut(b_mod, me * mod_width, mod_width)
    w_out, w_down, mod_part = together(w_out, w_down, mod_part)
    modulation = gather_stack(mod_part, "dp", dp)
    down_blocks, out_blocks = [
        jnp.stack(jnp.split(member.T, dp, axis=1)) for member in (w_down, w_out)
    ]

    def row_part(blocks, mask):
        return lax.ppermute(pick(blocks, me ^ mask), "dp", xor_perm(dp, mask))

    down_parts = {dp - 1: row_part(down_blocks, dp - 1)}
    tokens_own, w_slots, modulation = together(tokens_own, w_slots, modulation)
    modulation = xor_shuffle(modulation, me)
    seg_all = jnp.sum(
        (image_ends[None, None] <= piece_first[..., None]).astype(jnp.int32), axis=-1
    ).reshape(-1)
    image_ids = jnp.arange(images, dtype=jnp.int32)
    hot_all = seg_all[:, None] == image_ids[None]
    modulation = jnp.transpose(modulation, (1, 0, 2)).reshape(images, 6 * width)
    mod_all = jnp.dot(hot_all.astype(F32), modulation, precision=HIGHEST)
    mod_all = [part[:, None] for part in jnp.split(mod_all, 6, axis=1)]
    mod_all, down_blocks, out_blocks = together(mod_all, down_blocks, out_blocks)
    shift_a_all, scale_a_all, gate_b_all = [mod_all[at] for at in (0, 1, 5)]
    scale_a, gate_a, shift_b, scale_b, gate_b = [
        mod_all[at][:rows_dev] for at in (1, 2, 3, 4, 5)
    ]
    own_hot = hot_all[:rows_dev]

    def gather_tokens(own, *waits):
        return gather_parts(own, "dp", dp, *waits).reshape((-1,) + own.shape[1:])

    near_tokens = gather_most(tokens_own, "dp", dp).reshape(-1, width)
    far_tokens = lax.ppermute(near_tokens, "dp", xor_perm(dp, 1))
    near_tokens, far_tokens, cotangent = together(near_tokens, far_tokens, cotangent)
    out_parts = {mask: row_part(out_blocks, mask) for mask in range(2, dp)}
    down_parts.update({mask: row_part(down_blocks, mask) for mask in range(2, dp - 1)})
    slot_of = [lax.rem(me + kind * (dp % 3), 3) for kind in range(3)]
    w_heads = jnp.concatenate(
        [
            jnp.where(
                slot_of[kind] == 0,
                w_slots[0],
                jnp.where(slot_of[kind] == 1, w_slots[1], w_slots[2]),
            )
            for kind in range(3)
        ]
    )
    bias_heads = jnp.concatenate(
        [
            cut(b_query, me * head_width, head_width),
            jnp.zeros((head_width,), F32),
            cut(b_value, me * head_width, head_width),
        ]
    )
    projected, hidden_a_all, norm_low = norm_project(
        near_tokens, far_tokens, scale_a_all, shift_a_all, w_heads, bias_heads[:, None], piece
    )
    cotangent_own = to_groups(cotangent)
    count = hidden_a_all.shape[0]
    half = count // 2
    projected, down_blocks, out_blocks = together(projected, down_blocks, out_blocks)
    projected = projected.reshape(3, heads, HD, count)
    queries, keys, values = [(projected, kind) for kind in range(3)]
    seg_row = seg_all
    if spans > 1:
        mates = [[at * spans + span for span in range(spans)] for at in range(rows)]
        keys, values, seg_row = [
            lax.all_gather(
                member, "band", axis=member.ndim - 1, tiled=True, axis_index_groups=mates
            )
            for member in (projected[1:2], projected[2:3], seg_row)
        ]
        keys, values = (keys, 0), (values, 0)
    one_image = jnp.all(seg_row == seg_row[0]).astype(jnp.int32)
    attend_facts = jnp.concatenate([one_image[None], seg_row, seg_all])
    attended, prob_low = attend(queries, keys, values, attend_facts, piece)
    down_parts[0], out_parts[0] = pick(down_blocks, me), pick(out_blocks, me)
    down_parts[1], out_parts[1] = row_part(down_blocks, 1), row_part(out_blocks, 1)
    attended, out_parts = together(attended, out_parts)
    attended = attended.reshape(head_width, count)

    def by_device(parts):
        return jnp.concatenate(
            list(xor_shuffle(jnp.stack([parts[mask] for mask in range(dp)]), me))
        )

    w_out_rows = by_device(out_parts)

    def split_own(partial):
        return partial.astype(BF16).reshape(dp // 2, rows_dev, piece, width)

    def products(product, left):
        return split_own(product(left(half, count))), split_own(product(left(0, half)))

    far_half, near_half = products(
        lambda part: dot(part, w_out_rows, 0, 1), lambda low, high: attended[:, low:high]
    )
    far_half, down_parts = together(far_half, down_parts)
    branch = scatter_sum(near_half, far_half, "dp", dp) + b_out
    middle = tokens_own.astype(F32) + gate_a * branch
    norm_b, spread_b = layer_norm(middle)
    hidden_b = (norm_b * (1.0 + scale_b) + shift_b).astype(BF16)
    w_down_rows = by_device(down_parts)
    hidden_b, w_down_rows, cotangent_own = together(hidden_b, w_down_rows, cotangent_own)
    hidden_b_all = gather_tokens(hidden_b).reshape(count, width)

    cotangent_own, hidden_b_all = together(cotangent_own, hidden_b_all)
    cotangent_all = gather_tokens(cotangent_own)
    grad_output = cotangent_own.astype(F32)
    b_up_own = cut(b_up, me * hidden_width, hidden_width)
    pre_act = dot(hidden_b_all, w_up) + b_up_own
    value, slope = gelu_pair(pre_act)
    activated, slope = lax.optimization_barrier((value.astype(BF16), slope.astype(BF16)))
    far_mlp, near_mlp = products(
        lambda part: dot(part, w_down_rows, 1, 1), lambda low, high: activated[low:high]
    )
    mlp_sent, mlp_held = scatter_first(near_mlp, far_mlp, "dp", dp)
    cotangent_all, mlp_sent = together(cotangent_all, mlp_sent)
    grad_mlp_all = (gate_b_all * cotangent_all.astype(F32)).astype(BF16).reshape(count, width)
    mlp_out = scatter_rest(mlp_sent, mlp_held, "dp", dp) + b_down
    grad_act = dot(grad_mlp_all, w_down_rows)
    grad_pre = (grad_act * slope.astype(F32)).astype(BF16)
    far_half, near_half = products(
        lambda part: dot(part, w_up, 1, 1), lambda low, high: grad_pre[low:high]
    )
    sent, grad_hidden_b = scatter_first(near_half, far_half, "dp", dp)
    mlp_out, sent, grad_pre, activated = together(mlp_out, sent, grad_pre, activated)
    grad_hidden_b = scatter_rest(sent, grad_hidden_b, "dp", dp)
    stages = log2(band)
    near_first = list(range(stages))

    def halves(held, axis):
        size = held.shape[axis] // 2
        return [lax.slice_in_dim(held, at * size, (at + 1) * size, axis=axis) for at in range(2)]

    def choose(held, axis, bit, plain=False):
        upper = (group >> bit) & 1
        if bit >= log2(across) and not plain:
            upper = upper ^ ((me >> (bit - log2(across))) & 1)
        upper = upper == 1
        first, second = halves(held, axis)
        return jnp.where(upper, second, first), jnp.where(upper, first, second)

    def send(part, bit):
        return lax.ppermute(part, "band", xor_perm(band, 1 << bit))

    def joined(mine, came):
        return (mine.astype(F32) + came.astype(F32)).astype(BF16)

    def sum_groups(term, axes, bits, plain=False):
        held = term
        for axis, bit in zip(axes, bits, strict=True):
            mine, far = choose(held, axis, bit, plain)
            held = joined(mine, send(far, bit))
        return held

    def piece_at(d, b):
        return reverse_bits((b // across) ^ d, dp), reverse_bits(b % across, across)

    def owner_pairs(owner):
        return [
            (d * band + b, owner(d, b, *piece_at(d, b))) for d in range(dp) for b in range(band)
        ]

    near_bits, far_bits = near_first[: log2(across)], near_first[log2(across) :]
    first_far = far_bits[0]
    grad_w_up = dot(hidden_b_all, grad_pre, 0, 0).astype(BF16)
    grad_w_down = dot(grad_mlp_all, activated, 0, 0).astype(BF16)
    up_mine, up_far = choose(grad_w_up, 1, near_bits[0])
    down_mine, down_far = choose(grad_w_down, 0, first_far)
    up_far, down_far = halves(up_far, 0), halves(down_far, 0)
    up_came = [send(up_far[0], near_bits[0])]
    down_came = [send(down_far[0], first_far)]

    grad_middle = grad_output + layer_norm_back(grad_hidden_b * (1.0 + scale_b), norm_b, spread_b)
    grad_branch = (gate_a * grad_middle).astype(BF16)
    middle, mlp_out, grad_branch, up_far, down_far = together(
        middle, mlp_out, grad_branch, up_far[1], down_far[1]
    )
    up_came, up_far = together(up_came, up_far)
    down_came, down_far = together(down_came, down_far)
    up_came.append(send(up_far, near_bits[0]))
    down_came.append(send(down_far, first_far))
    grad_branch_all = gather_tokens(grad_branch).reshape(count, width)
    output = (middle + gate_b * mlp_out).astype(BF16)
    output, grad_branch_all = together(output, grad_branch_all)
    output_came = [
        lax.ppermute(output[turn], both, inward[turn]) for turn in range(rows_dev)
    ]
    up_mine, up_far = choose(joined(up_mine, jnp.concatenate(up_came)), 0, first_far)
    down_mine, down_far = choose(joined(down_mine, jnp.concatenate(down_came)), 1, near_bits[0])
    up_came, down_came = send(up_far, first_far), send(down_far, near_bits[0])
    grad_attended = dot(w_out_rows, grad_branch_all, 0, 1).astype(BF16)
    grad_q, grad_k, grad_v = attend_back(
        queries,
        keys,
        values,
        attended.reshape(heads, HD, count),
        grad_attended.reshape(heads, HD, count),
        prob_low,
    )
    if spans > 1:
        grad_k, grad_v = [
            lax.psum_scatter(
                member, "band", scatter_dimension=2, tiled=True, axis_index_groups=mates
            )
            for member in (grad_k, grad_v)
        ]
    grad_heads = jnp.concatenate(
        [member.reshape(head_width, count) for member in (grad_q, grad_k, grad_v)]
    )
    grad_heads, up_came, down_came = together(grad_heads, up_came, down_came)
    far_half, near_half = products(
        lambda part: dot(part, w_heads, 0, 0), lambda low, high: grad_heads[:, low:high]
    )
    sent, grad_hidden_a = scatter_first(near_half, far_half, "dp", dp)
    attended, grad_heads, near_half, far_half, sent, up_came, down_came, output_came = together(
        attended, grad_heads, near_half, far_half, sent, up_came, down_came, output_came
    )
    output = xor_shuffle(jnp.stack(output_came), my_slot)
    grad_hidden_a = scatter_rest(sent, grad_hidden_a, "dp", dp)
    up_down = jnp.stack([joined(up_mine, up_came), joined(down_mine, down_came)])
    up_down_rest = [2] * (len(near_bits) - 1) + [1] * (len(far_bits) - 1), near_bits[1:] + far_bits[1:]
    up_down_mine, up_down_far = choose(up_down, up_down_rest[0][0], up_down_rest[1][0])
    up_down_far, grad_heads, attended = together(up_down_far, grad_heads, attended)
    up_down_came = send(up_down_far, up_down_rest[1][0])
    grad_w_heads = dot(grad_heads, hidden_a_all).astype(BF16).reshape(3, across, unit, width)
    qkv_axes = [1] * log2(across) + [3] * log2(dp)
    qkv_mine, qkv_far = choose(grad_w_heads, qkv_axes[0], near_first[0])
    near_half, far_half, qkv_far, attended = together(near_half, far_half, qkv_far, attended)
    qkv_came = send(qkv_far, near_first[0])
    out_bits = [far_bits[0]] + near_bits + far_bits[1:]
    out_mine, out_far = choose(
        dot(grad_branch_all, attended, 0, 1)
        .astype(BF16)
        .reshape((2,) * stages + (unit, head_width)),
        stages - 1 - out_bits[0],
        out_bits[0],
        plain=True,
    )
    out_came = send(out_far, out_bits[0])

    hot_tokens = jnp.broadcast_to(
        hot_all.T.astype(BF16)[:, :, None], (images, hot_all.shape[0], piece)
    ).reshape(images, count)

    def image_sums(near, far):
        return dot(hot_tokens[:, :half], near) + dot(hot_tokens[:, half:], far)

    near_half, far_half = near_half.reshape(half, width), far_half.reshape(half, width)
    grad_shift_a = image_sums(near_half, far_half)
    grad_scale_a = image_sums(near_half * norm_low[:half], far_half * norm_low[half:])

    def own_sums(member):
        pieces = jnp.sum(member, axis=1)
        return jnp.sum(jnp.where(own_hot[:, :, None], pieces[:, None], 0.0), axis=0)

    grad_mod = jnp.concatenate(
        [
            grad_shift_a,
            grad_scale_a,
            own_sums(grad_middle * branch),
            own_sums(grad_hidden_b),
            own_sums(grad_hidden_b * norm_b),
            own_sums(grad_output * mlp_out),
        ],
        axis=1,
    )
    grad_mod = jnp.transpose(grad_mod.reshape(images, dp, mod_width), (1, 0, 2))
    grad_mod_came = lax.all_to_all(grad_mod, "dp", 0, 0, tiled=True)
    grad_mod_came, qkv_came = together(grad_mod_came, qkv_came)
    grad_mod_own = jnp.sum(grad_mod_came, axis=0)
    high = grad_mod_own.astype(BF16)
    low = (grad_mod_own - high.astype(F32)).astype(BF16)
    grad_silu = dot(jnp.concatenate([high, low], axis=0), w_mod, 1, 1)
    grad_silu = grad_silu[:images] + grad_silu[images:]
    ones = jnp.ones((8, count), BF16)
    bias_rows = [
        jnp.sum(grad_mlp_all[: rows_dev * piece].astype(F32), axis=0),
        jnp.sum(grad_branch.astype(F32), axis=(0, 1)),
        dot(ones, grad_pre)[0],
        dot(ones, grad_heads, 1, 1)[0],
    ]
    assert images >= len(bias_rows)
    bias_rows = [
        jnp.pad(member, (0, width + 128 - member.shape[0])) for member in bias_rows
    ] + [jnp.zeros((width + 128,), F32)] * (images - len(bias_rows))
    bias_rows = jnp.stack(bias_rows) + jnp.pad(
        index_own.astype(F32)[:, None], ((0, 0), (width, 127))
    )
    packed = jnp.concatenate([grad_mod_own, grad_silu, bias_rows], axis=1)
    grad_hidden_a, packed = together(grad_hidden_a, packed)
    qkv_mine, qkv_far = choose(joined(qkv_mine, qkv_came), qkv_axes[1], near_first[1])
    inputs = tokens_own.astype(F32)
    norm_a, spread_a = layer_norm(inputs)
    grad_tokens = grad_middle + layer_norm_back(grad_hidden_a * (1.0 + scale_a), norm_a, spread_a)
    grad_tokens = grad_tokens.astype(BF16)
    packed, grad_tokens = together(packed, grad_tokens)
    held, masks = packed[None], [0]
    for bit in far_bits + near_bits:
        if bit == near_bits[0]:
            held, grad_tokens, qkv_far, out_came = together(held, grad_tokens, qkv_far, out_came)
        held = jnp.concatenate([held, lax.ppermute(held, "band", xor_perm(band, 1 << bit))])
        masks = masks + [mask ^ (1 << bit) for mask in masks]
    packed = xor_shuffle(jnp.stack([held[masks.index(mask)] for mask in range(band)]), group)
    grad_tokens_came = [
        lax.ppermute(grad_tokens[turn], both, inward[turn]) for turn in range(rows_dev)
    ]
    qkv_came = send(qkv_far, near_first[1])
    out_mine, out_far = choose(
        joined(out_mine, out_came), stages - 1 - out_bits[1], out_bits[1], plain=True
    )
    out_came = send(out_far, out_bits[1])
    packed, qkv_came, up_down_came, out_came, grad_tokens_came = together(
        packed, qkv_came, up_down_came, out_came, grad_tokens_came
    )
    up_down = sum_groups(
        joined(up_down_mine, up_down_came), up_down_rest[0][1:], up_down_rest[1][1:]
    )
    grad_tokens = xor_shuffle(jnp.stack(grad_tokens_came), my_slot)
    grad_mod_groups = packed[:, :, :mod_width].reshape(band * images, mod_width)
    grad_silu_groups = packed[:, :, mod_width : mod_width + width]
    grad_silu_groups = grad_silu_groups.reshape(rows, spans, images, width).sum(1)
    mod_sum = jnp.sum(grad_mod_groups, axis=0)
    mod_rows = -(-mod_width // width)
    mod_sum = jnp.pad(mod_sum, (0, mod_rows * width - mod_width)).reshape(mod_rows, width)
    final_pack = jnp.concatenate(
        [
            grad_silu_groups.reshape(rows * images, width),
            jnp.sum(packed[:, :, mod_width + width : mod_width + 2 * width], axis=0),
            mod_sum,
        ]
    )
    qkv_sum = sum_groups(joined(qkv_mine, qkv_came), qkv_axes[2:], near_first[2:])
    qkv_sum = qkv_sum.reshape(3, unit, head_width)
    out_sum = sum_groups(
        joined(out_mine, out_came),
        [stages - 1 - bit for bit in out_bits[2:]],
        out_bits[2:],
        plain=True,
    )
    final_out = out_sum.reshape(unit, head_width).T.astype(F32)
    final_pack = gather_all(final_pack, "dp", dp)
    up_down = lax.ppermute(up_down, both, owner_pairs(lambda d, b, block, unit: block * band + b))
    up_down, qkv_sum = together(up_down, qkv_sum)
    up_down = lax.ppermute(
        up_down,
        both,
        [
            (d * band + b, d * band + ((b // across) ^ reverse_bits(d, dp)) * across + reverse_bits(b % across, across))
            for d in range(dp)
            for b in range(band)
        ],
    )
    final_up, final_down = up_down[0].astype(F32), up_down[1].T.astype(F32)

    kind_of = [
        [next(kind for kind in range(3) if (kind * dp + d) % 3 == slot) for slot in range(3)]
        for d in range(dp)
    ]
    kind_now = [
        sum(
            jnp.where(slot_of[kind] == slot, kind, 0).astype(jnp.int32) for kind in range(3)
        )
        for slot in range(3)
    ]
    my_unit = reverse_bits(group & (across - 1), across)
    final_qkv = []
    for turn in range(3):
        slots = []
        for at in range(across):
            options = {
                slot
                for d in range(dp)
                for slot in range(3)
                if (band * kind_of[d][slot] + across * d + at) % 3 == turn
            }
            assert len(options) == 1
            slots.append(options.pop())

        def owner(d, b, block, at, slots=slots, turn=turn):
            start = band * kind_of[d][slots[at]] + across * d + at
            assert start % 3 == turn
            return block * band + start // 3

        kind = sum(
            jnp.where(my_unit == at, kind_now[slots[at]], 0).astype(jnp.int32)
            for at in range(across)
        )
        final_qkv.append(
            lax.ppermute(pick(qkv_sum, kind), both, owner_pairs(owner))
        )
    final_qkv = jnp.concatenate(final_qkv).T.astype(F32)

    index_all = packed[::spans, :, mod_width + 2 * width].reshape(-1).astype(jnp.int32)
    condition = conditions(index_all)
    silu_all = jax.nn.silu(condition).astype(BF16)
    silu_rows = rows * images
    grad_silu_rows = jnp.sum(final_pack[:, :silu_rows], axis=0)
    bias_all = final_pack[:, silu_rows : silu_rows + images]
    final_b_down = jnp.sum(bias_all[:, 0], axis=0)
    final_b_out = jnp.sum(bias_all[:, 1], axis=0)
    final_b_up = bias_all[:, 2, :hidden_width].reshape(-1)
    final_b_query = bias_all[:, 3, :head_width].reshape(-1)
    final_b_value = bias_all[:, 3, 2 * head_width : 3 * head_width].reshape(-1)
    final_b_mod = final_pack[:, silu_rows + images :].reshape(dp, -1)[:, :mod_width].reshape(-1)
    sigmoid = jax.nn.sigmoid(condition)
    grad_condition = grad_silu_rows * (sigmoid * (1.0 + condition * (1.0 - sigmoid)))
    table_hot = (
        classes[:, None] == index_all[None]
    ).astype(F32)
    final_table = jnp.dot(table_hot, grad_condition, precision=HIGHEST)
    mod_share = mod_width // across
    grad_mod_share = lax.ppermute(
        cut(grad_mod_groups, my_unit * mod_share, mod_share, 1),
        both,
        owner_pairs(lambda d, b, block, at: block * band + across * d + at),
    )
    silu_share = cut(silu_all, me * head_width, head_width, 1).astype(F32)
    silu_share = jnp.repeat(silu_share.reshape(rows, images, -1), spans, axis=0)
    final_mod = lax.dot_general(
        silu_share.reshape(band * images, -1),
        grad_mod_share,
        (((0,), (0,)), ((), ())),
        precision=HIGHEST,
        preferred_element_type=F32,
    )
    return (
        output,
        grad_tokens,
        final_table,
        final_mod,
        final_qkv,
        final_out,
        final_up,
        final_down,
        final_b_mod,
        final_b_query,
        final_b_value,
        final_b_out,
        final_b_up,
        final_b_down,
    )


def solution(mesh):
    rows = P("dp", "band", None)
    split = P(None, "dp")
    spread = P("dp", "band")
    return jax.shard_map(
        shards,
        mesh=mesh,
        in_specs=(
            rows,
            rows,
            P("dp", None),
            P("dp", None),
            P(),
            split,
            P(),
            split,
            P(),
            P(),
            split,
            P(),
            split,
            P(),
            split,
            P(),
        ),
        out_specs=(
            rows,
            rows,
            P(),
            spread,
            spread,
            spread,
            spread,
            P("band", "dp"),
            P(),
            P(),
            P(),
            P(),
            P(),
            P(),
        ),
        check_vma=False,
    )
```

```python
import functools
import math

import jax
import jax.numpy as jnp
from jax import lax
from jax.experimental import pallas as pl
from jax.experimental.pallas import tpu as pltpu
from jax.sharding import PartitionSpec as P

H = 16
HD = 72

EPSILON = 1e-06
HIGHEST = lax.Precision.HIGHEST
NEGATIVE = -1e30
GELU_COEF = 0.7978845608028654
FACTOR = 1.0 / math.sqrt(HD)
LOG2E = math.log2(math.e)
VMEM_LIMIT = 56 * 1024 * 1024
F32 = jnp.float32
BF16 = jnp.bfloat16


def dot(left, right, left_dim=1, right_dim=0):
    return lax.dot_general(
        left, right, (((left_dim,), (right_dim,)), ((), ())), preferred_element_type=F32
    )


def log2(count):
    assert count & (count - 1) == 0
    return count.bit_length() - 1


def reverse_bits(value, count):
    width = log2(count)
    return sum(((value >> at) & 1) << (width - 1 - at) for at in range(width)) if width else 0


def bits_up(count):
    return [1 << place for place in range(log2(count))]


def xor_perm(count, mask):
    return [(place, place ^ mask) for place in range(count)]


def pick(stack, place, axis=0):
    return lax.dynamic_index_in_dim(
        stack, place, axis, keepdims=False, allow_negative_indices=False
    )


def cut(array, start, size, axis=0):
    return lax.dynamic_slice_in_dim(array, start, size, axis, allow_negative_indices=False)


def xor_shuffle(array, mask):
    return jnp.stack([pick(array, mask ^ place) for place in range(array.shape[0])])


def together(*arrays):
    return lax.optimization_barrier(arrays)


def gather_most(part, axis, count):
    held = part[None]
    for bit in reversed(bits_up(count)[1:]):
        held = jnp.concatenate([held, lax.ppermute(held, axis, xor_perm(count, bit))])
    return held


def gather_parts(part, axis, count):
    held = gather_most(part, axis, count)
    return jnp.concatenate([held, lax.ppermute(held, axis, xor_perm(count, 1))])


def gather_stack(part, axis, count):
    held = gather_parts(part, axis, count)
    return jnp.stack([held[reverse_bits(mask, count)] for mask in range(count)])


def gather_all(part, axis, count):
    return xor_shuffle(gather_stack(part, axis, count), lax.axis_index(axis))


def mask_order(count):
    order = [0]
    for bit in reversed(bits_up(count)):
        order = order + [place ^ bit for place in order]
    return order


def scatter_first(near, far, axis, count):
    came = lax.ppermute(far, axis, xor_perm(count, 1))
    half = near.shape[0] // 2
    sent = (near[half:].astype(F32) + came[half:].astype(F32)).astype(BF16)
    sent, near, came = together(sent, near, came)
    return sent, near[:half].astype(F32) + came[:half].astype(F32)


def scatter_rest(sent, held, axis, count):
    for bit in bits_up(count)[1:]:
        held = held + lax.ppermute(sent, axis, xor_perm(count, bit)).astype(F32)
        half = held.shape[0] // 2
        sent, held = held[half:].astype(BF16), held[: max(half, 1)]
    return held[0]


def scatter_sum(near, far, axis, count):
    return scatter_rest(*scatter_first(near, far, axis, count), axis, count)


def project_kernel(
    halves, piece, near_ref, far_ref, scale_ref, shift_ref, weight_ref, bias_ref, out_ref, hidden_ref, norm_ref
):
    def write(tokens):
        inputs = tokens.astype(F32)
        average = jnp.mean(inputs, axis=-1, keepdims=True)
        centred = inputs - average
        spread = jnp.mean(centred * centred, axis=-1, keepdims=True)
        norm = centred * lax.rsqrt(spread + EPSILON)
        norm_ref[...] = norm.astype(BF16)
        for at in range(tokens.shape[0] // piece):
            rows = slice(at * piece, (at + 1) * piece)
            hidden = norm[rows] * (1.0 + scale_ref[at]) + shift_ref[at]
            hidden_ref[rows] = hidden.astype(BF16)
        out_ref[...] = (
            dot(weight_ref[...], hidden_ref[...], 1, 1) + bias_ref[...]
        ).astype(BF16)

    step = pl.program_id(0)

    @pl.when(step < halves)
    def _():
        write(near_ref[...])

    @pl.when(step >= halves)
    def _():
        write(far_ref[...])


def norm_project(near, far, scale, shift, weight, bias, piece):
    half, width = near.shape
    columns = weight.shape[0]
    rows = min(2 * piece, half)
    halves = half // rows
    scales = pl.BlockSpec((rows // piece, 1, width), lambda step: (step, 0, 0))
    block = pl.BlockSpec((rows, width), lambda step: (step, 0))
    shape = jax.ShapeDtypeStruct((2 * half, width), BF16)
    return pl.pallas_call(
        functools.partial(project_kernel, halves, piece),
        grid=(2 * halves,),
        in_specs=[
            pl.BlockSpec((rows, width), lambda step: (jnp.minimum(step, halves - 1), 0)),
            pl.BlockSpec((rows, width), lambda step: (jnp.maximum(step - halves, 0), 0)),
            scales,
            scales,
            pl.BlockSpec((columns, width), lambda step: (0, 0)),
            pl.BlockSpec((columns, 1), lambda step: (0, 0)),
        ],
        out_specs=[pl.BlockSpec((columns, rows), lambda step: (0, step)), block, block],
        out_shape=[jax.ShapeDtypeStruct((columns, 2 * half), BF16), shape, shape],
        compiler_params=pltpu.CompilerParams(vmem_limit_bytes=VMEM_LIMIT),
        cost_estimate=pl.CostEstimate(
            flops=4 * columns * half * width, bytes_accessed=12 * half * width, transcendentals=0
        ),
        name="norm_project",
    )(near, far, scale, shift, weight, bias)


def attend_kernel(piece, facts_ref, q_ref, k_ref, v_ref, out_ref, prob_ref):
    step = pl.program_id(1)
    keys_len, lanes = k_ref.shape[-1], q_ref.shape[-1]
    pieces_key, pieces_query = keys_len // piece, lanes // piece
    values = v_ref[0, 0]

    def finish(scores):
        top = jnp.max(scores, axis=0, keepdims=True)
        exponent = jnp.exp2(scores * (FACTOR * LOG2E) - top * (FACTOR * LOG2E))
        total = jnp.sum(exponent, axis=0, keepdims=True)
        prob = (exponent * (1.0 / total)).astype(BF16)
        prob_ref[0] = prob
        out_ref[0] = dot(values, prob).astype(BF16)

    scores = dot(k_ref[0, 0], q_ref[0, 0], 0, 0)

    @pl.when(facts_ref[0] == 1)
    def _():
        finish(scores)

    @pl.when(facts_ref[0] != 1)
    def _():
        seg_key = jnp.concatenate(
            [jnp.full((piece, 1), facts_ref[1 + at], jnp.int32) for at in range(pieces_key)], axis=0
        )
        base = 1 + pieces_key + step * pieces_query
        seg_query = jnp.concatenate(
            [jnp.full((1, piece), facts_ref[base + at], jnp.int32) for at in range(pieces_query)],
            axis=1,
        )
        finish(jnp.where(seg_key == seg_query, scores, NEGATIVE))


def attend(queries, keys, values, facts, piece):
    _, heads, depth, count = queries[0].shape
    keys_len = keys[0].shape[3]
    lanes = min(count, (1 << 20) // keys_len)
    chunk = lambda head, step, facts: (head, 0, step)
    return pl.pallas_call(
        functools.partial(attend_kernel, piece),
        grid_spec=pltpu.PrefetchScalarGridSpec(
            num_scalar_prefetch=1,
            grid=(heads, count // lanes),
            in_specs=[
                pl.BlockSpec(
                    (1, 1, depth, lanes), lambda head, step, facts: (queries[1], head, 0, step)
                ),
                pl.BlockSpec((1, 1, depth, keys_len), lambda head, step, facts: (keys[1], head, 0, 0)),
                pl.BlockSpec(
                    (1, 1, depth, keys_len), lambda head, step, facts: (values[1], head, 0, 0)
                ),
            ],
            out_specs=[
                pl.BlockSpec((1, depth, lanes), chunk),
                pl.BlockSpec((1, keys_len, lanes), chunk),
            ],
        ),
        out_shape=[
            jax.ShapeDtypeStruct((heads, depth, count), BF16),
            jax.ShapeDtypeStruct((heads, keys_len, count), BF16),
        ],
        compiler_params=pltpu.CompilerParams(vmem_limit_bytes=VMEM_LIMIT),
        cost_estimate=pl.CostEstimate(
            flops=30 * count * keys_len * heads * 128,
            bytes_accessed=2 * heads * count * keys_len,
            transcendentals=heads * count * keys_len,
        ),
        name="attend",
    )(facts, queries[0], keys[0], values[0])


def attend_back_kernel(
    q_ref, k_ref, v_ref, out_ref, grad_ref, prob_ref, dq_ref, dk_ref, dv_ref, dk_sum, dv_sum
):
    step = pl.program_id(1)
    grad = grad_ref[0]
    prob = prob_ref[0]
    delta = jnp.sum(grad.astype(F32) * out_ref[0].astype(F32), axis=0, keepdims=True)
    grad_prob = dot(v_ref[0, 0], grad, 0, 0)
    grad_score = (prob.astype(F32) * (grad_prob - delta)).astype(BF16)
    dq_ref[0] = (dot(k_ref[0, 0], grad_score) * FACTOR).astype(BF16)
    dk_part = dot(grad_score, q_ref[0, 0], 1, 1)
    dv_part = dot(prob, grad, 1, 1)

    @pl.when(step == 0)
    def _():
        dk_sum[...] = dk_part
        dv_sum[...] = dv_part

    @pl.when(step != 0)
    def _():
        dk_sum[...] += dk_part
        dv_sum[...] += dv_part

    @pl.when(step == pl.num_programs(1) - 1)
    def _():
        dk_ref[0] = jnp.transpose(dk_sum[...] * FACTOR).astype(BF16)
        dv_ref[0] = jnp.transpose(dv_sum[...]).astype(BF16)


def attend_back(queries, keys, values, attended, grad, prob):
    _, heads, depth, count = queries[0].shape
    keys_len = keys[0].shape[3]
    lanes = min(count, (1 << 20) // keys_len)
    chunk = lambda head, step: (head, 0, step)
    whole = lambda head, step: (head, 0, 0)
    return pl.pallas_call(
        attend_back_kernel,
        grid=(heads, count // lanes),
        in_specs=[
            pl.BlockSpec((1, 1, depth, lanes), lambda head, step: (queries[1], head, 0, step)),
            pl.BlockSpec((1, 1, depth, keys_len), lambda head, step: (keys[1], head, 0, 0)),
            pl.BlockSpec((1, 1, depth, keys_len), lambda head, step: (values[1], head, 0, 0)),
            pl.BlockSpec((1, depth, lanes), chunk),
            pl.BlockSpec((1, depth, lanes), chunk),
            pl.BlockSpec((1, keys_len, lanes), chunk),
        ],
        out_specs=[
            pl.BlockSpec((1, depth, lanes), chunk),
            pl.BlockSpec((1, depth, keys_len), whole),
            pl.BlockSpec((1, depth, keys_len), whole),
        ],
        out_shape=[
            jax.ShapeDtypeStruct((heads, depth, count), BF16),
            jax.ShapeDtypeStruct((heads, depth, keys_len), BF16),
            jax.ShapeDtypeStruct((heads, depth, keys_len), BF16),
        ],
        scratch_shapes=[pltpu.VMEM((keys_len, depth), F32), pltpu.VMEM((keys_len, depth), F32)],
        compiler_params=pltpu.CompilerParams(vmem_limit_bytes=VMEM_LIMIT),
        cost_estimate=pl.CostEstimate(
            flops=30 * count * keys_len * heads * 128,
            bytes_accessed=2 * heads * count * keys_len,
            transcendentals=0,
        ),
        name="attend_back",
    )(queries[0], keys[0], values[0], attended, grad, prob)


def gelu_pair(inputs):
    square = inputs * inputs
    tanh = jnp.tanh(GELU_COEF * (inputs + 0.044715 * inputs * square))
    value = 0.5 * inputs * (1.0 + tanh)
    slope = 0.5 * (1.0 + tanh) + 0.5 * inputs * (1.0 - tanh * tanh) * (
        GELU_COEF * (1.0 + 3.0 * 0.044715 * square)
    )
    return value, slope


def layer_norm(inputs):
    average = jnp.mean(inputs, axis=-1, keepdims=True)
    centred = inputs - average
    spread = jnp.mean(centred * centred, axis=-1, keepdims=True)
    scale = lax.rsqrt(spread + EPSILON)
    return centred * scale, scale


def layer_norm_back(grad, norm, scale):
    first = jnp.mean(grad, axis=-1, keepdims=True)
    second = jnp.mean(grad * norm, axis=-1, keepdims=True)
    return (grad - first - norm * second) * scale


def shards(
    tokens,
    cotangent,
    lengths,
    cond_index,
    cond_table,
    w_mod,
    b_mod,
    w_qkv,
    b_query,
    b_value,
    w_out,
    b_out,
    w_up,
    b_up,
    w_down,
    b_down,
):
    rows_dev, piece, width = tokens.shape
    dp, band = lax.axis_size("dp"), lax.axis_size("band")
    me, group = lax.axis_index("dp"), lax.axis_index("band")
    images = lengths.shape[1]
    rows = rows_dev * dp
    spans = band // rows
    assert band % rows == 0
    across = band // dp
    unit = width // band
    heads = H // dp
    head_width = width // dp
    mod_width = w_mod.shape[1]
    hidden_width = w_up.shape[1]
    both = ("dp", "band")
    me_turned = reverse_bits(me, dp)

    def target(d, b, turn):
        local = ((b >> log2(dp)) & (rows_dev - 1)) ^ turn
        to_group = (rows_dev * reverse_bits(d, dp) + local) * spans + b // rows
        return reverse_bits(b % dp, dp) * band + to_group

    outward = [
        [(d * band + b, target(d, b, turn)) for d in range(dp) for b in range(band)]
        for turn in range(rows_dev)
    ]
    inward = [[(there, here) for here, there in pairs] for pairs in outward]
    my_slot = (group >> log2(dp)) & (rows_dev - 1)

    def to_groups(local):
        return jnp.stack(
            [
                lax.ppermute(pick(local, my_slot ^ turn), both, outward[turn])
                for turn in range(rows_dev)
            ]
        )

    def from_groups(held):
        came = jnp.stack(
            [lax.ppermute(held[turn], both, inward[turn]) for turn in range(rows_dev)]
        )
        return xor_shuffle(came, my_slot)

    group_row = group >> log2(spans)
    my_local = group_row & (rows_dev - 1)
    order = mask_order(dp)
    places = jnp.arange(dp, dtype=jnp.int32)[:, None]
    turns = jnp.arange(rows_dev, dtype=jnp.int32)[None]
    piece_first = piece * (
        (group & (spans - 1)) * rows + ((my_local ^ turns) * dp) + (me_turned ^ places)
    )

    facts = jnp.concatenate([lengths, cond_index], axis=1)
    facts_own = lax.ppermute(pick(facts, my_slot), both, outward[0])
    tokens_sent = [pick(tokens, my_slot ^ turn) for turn in range(rows_dev)]
    slot_to = [[(3 * d + slot) % dp for d in range(dp)] for slot in range(3)]
    w_qkv, tokens_sent = together(w_qkv, tokens_sent)
    tokens_own = jnp.stack(
        [lax.ppermute(part, both, outward[turn]) for turn, part in enumerate(tokens_sent)]
    )
    w_slots = [w_qkv.T[slot * head_width : (slot + 1) * head_width] for slot in range(3)]
    stay = [[d == to for d, to in enumerate(target)] for target in slot_to]
    if all(first != last for first, last in zip(stay[0], stay[2], strict=True)):
        keeps_first = functools.reduce(
            jnp.logical_or, [me == d for d in range(dp) if stay[0][d]]
        )
        slots_sent = jnp.where(keeps_first, w_slots[2], w_slots[0])
        came = lax.ppermute(
            slots_sent,
            "dp",
            [(d, slot_to[2 if stay[0][d] else 0][d]) for d in range(dp)],
        )
        w_slots = [
            jnp.where(keeps_first, w_slots[0], came),
            lax.ppermute(w_slots[1], "dp", list(enumerate(slot_to[1]))),
            jnp.where(keeps_first, came, w_slots[2]),
        ]
    else:
        slots_sent = w_slots[0]
        w_slots = [
            lax.ppermute(w_slots[slot], "dp", list(enumerate(slot_to[slot]))) for slot in range(3)
        ]
    image_ends, index_own = jnp.cumsum(facts_own[:images]), facts_own[images:]
    classes = jnp.arange(cond_table.shape[0], dtype=jnp.int32)

    def conditions(index):
        return dot((index[:, None] == classes[None]).astype(BF16), cond_table)

    silu_own = jax.nn.silu(conditions(index_own)).astype(BF16)
    mod_part = dot(silu_own, w_mod) + cut(b_mod, me * mod_width, mod_width)
    w_out, w_down, mod_part = together(w_out, w_down, mod_part)
    modulation = gather_stack(mod_part, "dp", dp)
    down_blocks, out_blocks = [
        jnp.stack(jnp.split(member.T, dp, axis=1)) for member in (w_down, w_out)
    ]

    def row_part(blocks, mask):
        return lax.ppermute(pick(blocks, me ^ mask), "dp", xor_perm(dp, mask))

    down_parts = {dp - 1: row_part(down_blocks, dp - 1)}
    tokens_own, w_slots, modulation = together(tokens_own, w_slots, modulation)
    modulation = xor_shuffle(modulation, me)
    seg_all = jnp.sum(
        (image_ends[None, None] <= piece_first[..., None]).astype(jnp.int32), axis=-1
    ).reshape(-1)
    image_ids = jnp.arange(images, dtype=jnp.int32)
    hot_all = seg_all[:, None] == image_ids[None]
    modulation = jnp.transpose(modulation, (1, 0, 2)).reshape(images, 6 * width)
    mod_all = jnp.dot(hot_all.astype(F32), modulation, precision=HIGHEST)
    mod_all = [part[:, None] for part in jnp.split(mod_all, 6, axis=1)]
    mod_all, down_blocks, out_blocks = together(mod_all, down_blocks, out_blocks)
    shift_a_all, scale_a_all, gate_b_all = [mod_all[at] for at in (0, 1, 5)]
    scale_a, gate_a, shift_b, scale_b, gate_b = [
        mod_all[at][:rows_dev] for at in (1, 2, 3, 4, 5)
    ]
    own_hot = hot_all[:rows_dev]

    def gather_tokens(own, *waits):
        return gather_parts(own, "dp", dp, *waits).reshape((-1,) + own.shape[1:])

    near_tokens = gather_most(tokens_own, "dp", dp).reshape(-1, width)
    far_tokens = lax.ppermute(near_tokens, "dp", xor_perm(dp, 1))
    near_tokens, far_tokens, cotangent = together(near_tokens, far_tokens, cotangent)
    out_parts = {mask: row_part(out_blocks, mask) for mask in range(2, dp)}
    down_parts.update({mask: row_part(down_blocks, mask) for mask in range(2, dp - 1)})
    slot_of = [lax.rem(me + kind * (dp % 3), 3) for kind in range(3)]
    w_heads = jnp.concatenate(
        [
            jnp.where(
                slot_of[kind] == 0,
                w_slots[0],
                jnp.where(slot_of[kind] == 1, w_slots[1], w_slots[2]),
            )
            for kind in range(3)
        ]
    )
    bias_heads = jnp.concatenate(
        [
            cut(b_query, me * head_width, head_width),
            jnp.zeros((head_width,), F32),
            cut(b_value, me * head_width, head_width),
        ]
    )
    projected, hidden_a_all, norm_low = norm_project(
        near_tokens, far_tokens, scale_a_all, shift_a_all, w_heads, bias_heads[:, None], piece
    )
    cotangent_own = to_groups(cotangent)
    count = hidden_a_all.shape[0]
    half = count // 2
    projected, down_blocks, out_blocks = together(projected, down_blocks, out_blocks)
    projected = projected.reshape(3, heads, HD, count)
    queries, keys, values = [(projected, kind) for kind in range(3)]
    seg_row = seg_all
    if spans > 1:
        mates = [[at * spans + span for span in range(spans)] for at in range(rows)]
        keys, values, seg_row = [
            lax.all_gather(
                member, "band", axis=member.ndim - 1, tiled=True, axis_index_groups=mates
            )
            for member in (projected[1:2], projected[2:3], seg_row)
        ]
        keys, values = (keys, 0), (values, 0)
    one_image = jnp.all(seg_row == seg_row[0]).astype(jnp.int32)
    attend_facts = jnp.concatenate([one_image[None], seg_row, seg_all])
    attended, prob_low = attend(queries, keys, values, attend_facts, piece)
    down_parts[0], out_parts[0] = pick(down_blocks, me), pick(out_blocks, me)
    down_parts[1], out_parts[1] = row_part(down_blocks, 1), row_part(out_blocks, 1)
    attended, out_parts = together(attended, out_parts)
    attended = attended.reshape(head_width, count)

    def by_device(parts):
        return jnp.concatenate(
            list(xor_shuffle(jnp.stack([parts[mask] for mask in range(dp)]), me))
        )

    w_out_rows = by_device(out_parts)

    def split_own(partial):
        return partial.astype(BF16).reshape(dp // 2, rows_dev, piece, width)

    def products(product, left):
        return split_own(product(left(half, count))), split_own(product(left(0, half)))

    far_half, near_half = products(
        lambda part: dot(part, w_out_rows, 0, 1), lambda low, high: attended[:, low:high]
    )
    far_half, down_parts = together(far_half, down_parts)
    branch = scatter_sum(near_half, far_half, "dp", dp) + b_out
    middle = tokens_own.astype(F32) + gate_a * branch
    norm_b, spread_b = layer_norm(middle)
    hidden_b = (norm_b * (1.0 + scale_b) + shift_b).astype(BF16)
    w_down_rows = by_device(down_parts)
    hidden_b, w_down_rows, cotangent_own = together(hidden_b, w_down_rows, cotangent_own)
    hidden_b_all = gather_tokens(hidden_b).reshape(count, width)

    cotangent_own, hidden_b_all = together(cotangent_own, hidden_b_all)
    cotangent_all = gather_tokens(cotangent_own)
    grad_output = cotangent_own.astype(F32)
    b_up_own = cut(b_up, me * hidden_width, hidden_width)
    pre_act = dot(hidden_b_all, w_up) + b_up_own
    value, slope = gelu_pair(pre_act)
    activated, slope = lax.optimization_barrier((value.astype(BF16), slope.astype(BF16)))
    far_mlp, near_mlp = products(
        lambda part: dot(part, w_down_rows, 1, 1), lambda low, high: activated[low:high]
    )
    mlp_sent, mlp_held = scatter_first(near_mlp, far_mlp, "dp", dp)
    cotangent_all, mlp_sent = together(cotangent_all, mlp_sent)
    grad_mlp_all = (gate_b_all * cotangent_all.astype(F32)).astype(BF16).reshape(count, width)
    mlp_out = scatter_rest(mlp_sent, mlp_held, "dp", dp) + b_down
    grad_act = dot(grad_mlp_all, w_down_rows)
    grad_pre = (grad_act * slope.astype(F32)).astype(BF16)
    far_half, near_half = products(
        lambda part: dot(part, w_up, 1, 1), lambda low, high: grad_pre[low:high]
    )
    sent, grad_hidden_b = scatter_first(near_half, far_half, "dp", dp)
    mlp_out, sent, grad_pre, activated = together(mlp_out, sent, grad_pre, activated)
    grad_hidden_b = scatter_rest(sent, grad_hidden_b, "dp", dp)
    stages = log2(band)
    near_first = list(range(stages))

    def halves(held, axis):
        size = held.shape[axis] // 2
        return [lax.slice_in_dim(held, at * size, (at + 1) * size, axis=axis) for at in range(2)]

    def choose(held, axis, bit, plain=False):
        upper = (group >> bit) & 1
        if bit >= log2(across) and not plain:
            upper = upper ^ ((me >> (bit - log2(across))) & 1)
        upper = upper == 1
        first, second = halves(held, axis)
        return jnp.where(upper, second, first), jnp.where(upper, first, second)

    def send(part, bit):
        return lax.ppermute(part, "band", xor_perm(band, 1 << bit))

    def joined(mine, came):
        return (mine.astype(F32) + came.astype(F32)).astype(BF16)

    def sum_groups(term, axes, bits, plain=False):
        held = term
        for axis, bit in zip(axes, bits, strict=True):
            mine, far = choose(held, axis, bit, plain)
            held = joined(mine, send(far, bit))
        return held

    def piece_at(d, b):
        return reverse_bits((b // across) ^ d, dp), reverse_bits(b % across, across)

    def owner_pairs(owner):
        return [
            (d * band + b, owner(d, b, *piece_at(d, b))) for d in range(dp) for b in range(band)
        ]

    near_bits, far_bits = near_first[: log2(across)], near_first[log2(across) :]
    first_far = far_bits[0]
    grad_w_up = dot(hidden_b_all, grad_pre, 0, 0).astype(BF16)
    grad_w_down = dot(grad_mlp_all, activated, 0, 0).astype(BF16)
    up_mine, up_far = choose(grad_w_up, 1, near_bits[0])
    down_mine, down_far = choose(grad_w_down, 0, first_far)
    up_far, down_far = halves(up_far, 0), halves(down_far, 0)
    up_came = [send(up_far[0], near_bits[0])]
    down_came = [send(down_far[0], first_far)]

    grad_middle = grad_output + layer_norm_back(grad_hidden_b * (1.0 + scale_b), norm_b, spread_b)
    grad_branch = (gate_a * grad_middle).astype(BF16)
    middle, mlp_out, grad_branch, up_far, down_far = together(
        middle, mlp_out, grad_branch, up_far[1], down_far[1]
    )
    up_came, up_far = together(up_came, up_far)
    down_came, down_far = together(down_came, down_far)
    up_came.append(send(up_far, near_bits[0]))
    down_came.append(send(down_far, first_far))
    grad_branch_all = gather_tokens(grad_branch).reshape(count, width)
    output = (middle + gate_b * mlp_out).astype(BF16)
    output, grad_branch_all = together(output, grad_branch_all)
    output_came = [
        lax.ppermute(output[turn], both, inward[turn]) for turn in range(rows_dev)
    ]
    up_mine, up_far = choose(joined(up_mine, jnp.concatenate(up_came)), 0, first_far)
    down_mine, down_far = choose(joined(down_mine, jnp.concatenate(down_came)), 1, near_bits[0])
    up_came, down_came = send(up_far, first_far), send(down_far, near_bits[0])
    grad_attended = dot(w_out_rows, grad_branch_all, 0, 1).astype(BF16)
    grad_q, grad_k, grad_v = attend_back(
        queries,
        keys,
        values,
        attended.reshape(heads, HD, count),
        grad_attended.reshape(heads, HD, count),
        prob_low,
    )
    if spans > 1:
        grad_k, grad_v = [
            lax.psum_scatter(
                member, "band", scatter_dimension=2, tiled=True, axis_index_groups=mates
            )
            for member in (grad_k, grad_v)
        ]
    grad_heads = jnp.concatenate(
        [member.reshape(head_width, count) for member in (grad_q, grad_k, grad_v)]
    )
    grad_heads, up_came, down_came = together(grad_heads, up_came, down_came)
    far_half, near_half = products(
        lambda part: dot(part, w_heads, 0, 0), lambda low, high: grad_heads[:, low:high]
    )
    sent, grad_hidden_a = scatter_first(near_half, far_half, "dp", dp)
    attended, grad_heads, near_half, far_half, sent, up_came, down_came, output_came = together(
        attended, grad_heads, near_half, far_half, sent, up_came, down_came, output_came
    )
    output = xor_shuffle(jnp.stack(output_came), my_slot)
    grad_hidden_a = scatter_rest(sent, grad_hidden_a, "dp", dp)
    up_down = jnp.stack([joined(up_mine, up_came), joined(down_mine, down_came)])
    up_down_rest = [2] * (len(near_bits) - 1) + [1] * (len(far_bits) - 1), near_bits[1:] + far_bits[1:]
    up_down_mine, up_down_far = choose(up_down, up_down_rest[0][0], up_down_rest[1][0])
    up_down_far, grad_heads, attended = together(up_down_far, grad_heads, attended)
    up_down_came = send(up_down_far, up_down_rest[1][0])
    grad_w_heads = dot(grad_heads, hidden_a_all).astype(BF16).reshape(3, across, unit, width)
    qkv_axes = [1] * log2(across) + [3] * log2(dp)
    qkv_mine, qkv_far = choose(grad_w_heads, qkv_axes[0], near_first[0])
    near_half, far_half, qkv_far, attended = together(near_half, far_half, qkv_far, attended)
    qkv_came = send(qkv_far, near_first[0])
    out_bits = [far_bits[0]] + near_bits + far_bits[1:]
    out_mine, out_far = choose(
        dot(grad_branch_all, attended, 0, 1)
        .astype(BF16)
        .reshape((2,) * stages + (unit, head_width)),
        stages - 1 - out_bits[0],
        out_bits[0],
        plain=True,
    )
    out_came = send(out_far, out_bits[0])

    hot_tokens = jnp.broadcast_to(
        hot_all.T.astype(BF16)[:, :, None], (images, hot_all.shape[0], piece)
    ).reshape(images, count)

    def image_sums(near, far):
        return dot(hot_tokens[:, :half], near) + dot(hot_tokens[:, half:], far)

    near_half, far_half = near_half.reshape(half, width), far_half.reshape(half, width)
    grad_shift_a = image_sums(near_half, far_half)
    grad_scale_a = image_sums(near_half * norm_low[:half], far_half * norm_low[half:])

    def own_sums(member):
        pieces = jnp.sum(member, axis=1)
        return jnp.sum(jnp.where(own_hot[:, :, None], pieces[:, None], 0.0), axis=0)

    grad_mod = jnp.concatenate(
        [
            grad_shift_a,
            grad_scale_a,
            own_sums(grad_middle * branch),
            own_sums(grad_hidden_b),
            own_sums(grad_hidden_b * norm_b),
            own_sums(grad_output * mlp_out),
        ],
        axis=1,
    )
    grad_mod = jnp.transpose(grad_mod.reshape(images, dp, mod_width), (1, 0, 2))
    grad_mod_came = lax.all_to_all(grad_mod, "dp", 0, 0, tiled=True)
    grad_mod_came, qkv_came = together(grad_mod_came, qkv_came)
    grad_mod_own = jnp.sum(grad_mod_came, axis=0)
    high = grad_mod_own.astype(BF16)
    low = (grad_mod_own - high.astype(F32)).astype(BF16)
    grad_silu = dot(jnp.concatenate([high, low], axis=0), w_mod, 1, 1)
    grad_silu = grad_silu[:images] + grad_silu[images:]
    ones = jnp.ones((8, count), BF16)
    bias_rows = [
        jnp.sum(grad_mlp_all[: rows_dev * piece].astype(F32), axis=0),
        jnp.sum(grad_branch.astype(F32), axis=(0, 1)),
        dot(ones, grad_pre)[0],
        dot(ones, grad_heads, 1, 1)[0],
    ]
    assert images >= len(bias_rows)
    bias_rows = [
        jnp.pad(member, (0, width + 128 - member.shape[0])) for member in bias_rows
    ] + [jnp.zeros((width + 128,), F32)] * (images - len(bias_rows))
    bias_rows = jnp.stack(bias_rows) + jnp.pad(
        index_own.astype(F32)[:, None], ((0, 0), (width, 127))
    )
    packed = jnp.concatenate([grad_mod_own, grad_silu, bias_rows], axis=1)
    grad_hidden_a, packed = together(grad_hidden_a, packed)
    qkv_mine, qkv_far = choose(joined(qkv_mine, qkv_came), qkv_axes[1], near_first[1])
    inputs = tokens_own.astype(F32)
    norm_a, spread_a = layer_norm(inputs)
    grad_tokens = grad_middle + layer_norm_back(grad_hidden_a * (1.0 + scale_a), norm_a, spread_a)
    grad_tokens = grad_tokens.astype(BF16)
    packed, grad_tokens = together(packed, grad_tokens)
    held, masks = packed[None], [0]
    for bit in far_bits + near_bits:
        if bit == near_bits[0]:
            held, grad_tokens, qkv_far, up_down_came = together(
                held, grad_tokens, qkv_far, up_down_came
            )
        held = jnp.concatenate([held, lax.ppermute(held, "band", xor_perm(band, 1 << bit))])
        masks = masks + [mask ^ (1 << bit) for mask in masks]
    packed = xor_shuffle(jnp.stack([held[masks.index(mask)] for mask in range(band)]), group)
    grad_tokens_came = [
        lax.ppermute(grad_tokens[turn], both, inward[turn]) for turn in range(rows_dev)
    ]
    qkv_came = send(qkv_far, near_first[1])
    up_down = sum_groups(
        joined(up_down_mine, up_down_came), up_down_rest[0][1:], up_down_rest[1][1:]
    )
    up_down = lax.ppermute(up_down, both, owner_pairs(lambda d, b, block, unit: block * band + b))
    packed, qkv_came, up_down, out_came, grad_tokens_came = together(
        packed, qkv_came, up_down, out_came, grad_tokens_came
    )
    grad_tokens = xor_shuffle(jnp.stack(grad_tokens_came), my_slot)
    grad_mod_groups = packed[:, :, :mod_width].reshape(band * images, mod_width)
    grad_silu_groups = packed[:, :, mod_width : mod_width + width]
    grad_silu_groups = grad_silu_groups.reshape(rows, spans, images, width).sum(1)
    mod_sum = jnp.sum(grad_mod_groups, axis=0)
    mod_rows = -(-mod_width // width)
    mod_sum = jnp.pad(mod_sum, (0, mod_rows * width - mod_width)).reshape(mod_rows, width)
    final_pack = jnp.concatenate(
        [
            grad_silu_groups.reshape(rows * images, width),
            jnp.sum(packed[:, :, mod_width + width : mod_width + 2 * width], axis=0),
            mod_sum,
        ]
    )
    qkv_sum = sum_groups(joined(qkv_mine, qkv_came), qkv_axes[2:], near_first[2:])
    qkv_sum = qkv_sum.reshape(3, unit, head_width)
    out_sum = sum_groups(
        joined(out_mine, out_came),
        [stages - 1 - bit for bit in out_bits[1:]],
        out_bits[1:],
        plain=True,
    )
    final_out = out_sum.reshape(unit, head_width).T.astype(F32)
    final_pack = gather_all(final_pack, "dp", dp)
    up_down, qkv_sum = together(up_down, qkv_sum)
    up_down = lax.ppermute(
        up_down,
        both,
        [
            (d * band + b, d * band + ((b // across) ^ reverse_bits(d, dp)) * across + reverse_bits(b % across, across))
            for d in range(dp)
            for b in range(band)
        ],
    )
    final_up, final_down = up_down[0].astype(F32), up_down[1].T.astype(F32)

    kind_of = [
        [next(kind for kind in range(3) if (kind * dp + d) % 3 == slot) for slot in range(3)]
        for d in range(dp)
    ]
    kind_now = [
        sum(
            jnp.where(slot_of[kind] == slot, kind, 0).astype(jnp.int32) for kind in range(3)
        )
        for slot in range(3)
    ]
    my_unit = reverse_bits(group & (across - 1), across)
    final_qkv = []
    for turn in range(3):
        slots = []
        for at in range(across):
            options = {
                slot
                for d in range(dp)
                for slot in range(3)
                if (band * kind_of[d][slot] + across * d + at) % 3 == turn
            }
            assert len(options) == 1
            slots.append(options.pop())

        def owner(d, b, block, at, slots=slots, turn=turn):
            start = band * kind_of[d][slots[at]] + across * d + at
            assert start % 3 == turn
            return block * band + start // 3

        kind = sum(
            jnp.where(my_unit == at, kind_now[slots[at]], 0).astype(jnp.int32)
            for at in range(across)
        )
        final_qkv.append(
            lax.ppermute(pick(qkv_sum, kind), both, owner_pairs(owner))
        )
    final_qkv = jnp.concatenate(final_qkv).T.astype(F32)

    index_all = packed[::spans, :, mod_width + 2 * width].reshape(-1).astype(jnp.int32)
    condition = conditions(index_all)
    silu_all = jax.nn.silu(condition).astype(BF16)
    silu_rows = rows * images
    grad_silu_rows = jnp.sum(final_pack[:, :silu_rows], axis=0)
    bias_all = final_pack[:, silu_rows : silu_rows + images]
    final_b_down = jnp.sum(bias_all[:, 0], axis=0)
    final_b_out = jnp.sum(bias_all[:, 1], axis=0)
    final_b_up = bias_all[:, 2, :hidden_width].reshape(-1)
    final_b_query = bias_all[:, 3, :head_width].reshape(-1)
    final_b_value = bias_all[:, 3, 2 * head_width : 3 * head_width].reshape(-1)
    final_b_mod = final_pack[:, silu_rows + images :].reshape(dp, -1)[:, :mod_width].reshape(-1)
    sigmoid = jax.nn.sigmoid(condition)
    grad_condition = grad_silu_rows * (sigmoid * (1.0 + condition * (1.0 - sigmoid)))
    table_hot = (
        classes[:, None] == index_all[None]
    ).astype(F32)
    final_table = jnp.dot(table_hot, grad_condition, precision=HIGHEST)
    mod_share = mod_width // across
    grad_mod_share = lax.ppermute(
        cut(grad_mod_groups, my_unit * mod_share, mod_share, 1),
        both,
        owner_pairs(lambda d, b, block, at: block * band + across * d + at),
    )
    silu_share = cut(silu_all, me * head_width, head_width, 1).astype(F32)
    silu_share = jnp.repeat(silu_share.reshape(rows, images, -1), spans, axis=0)
    final_mod = lax.dot_general(
        silu_share.reshape(band * images, -1),
        grad_mod_share,
        (((0,), (0,)), ((), ())),
        precision=HIGHEST,
        preferred_element_type=F32,
    )
    return (
        output,
        grad_tokens,
        final_table,
        final_mod,
        final_qkv,
        final_out,
        final_up,
        final_down,
        final_b_mod,
        final_b_query,
        final_b_value,
        final_b_out,
        final_b_up,
        final_b_down,
    )


def solution(mesh):
    rows = P("dp", "band", None)
    split = P(None, "dp")
    spread = P("dp", "band")
    return jax.shard_map(
        shards,
        mesh=mesh,
        in_specs=(
            rows,
            rows,
            P("dp", None),
            P("dp", None),
            P(),
            split,
            P(),
            split,
            P(),
            P(),
            split,
            P(),
            split,
            P(),
            split,
            P(),
        ),
        out_specs=(
            rows,
            rows,
            P(),
            spread,
            spread,
            spread,
            spread,
            P("band", "dp"),
            P(),
            P(),
            P(),
            P(),
            P(),
            P(),
        ),
        check_vma=False,
    )
```
